128 devices in a mesh: dp: 8 (over z, core), ctx: 16 (over x, y).
Axes of the slice: x: 4, y: 4, z: 4, core: 2. Of those that a mesh axis runs over, the one named last changes fastest.
Arguments:
- q_load: bfloat16 [16384, 4096], P(('dp', 'ctx')), may hold values from -6.5 to 6.5, as said below
- k_load: bfloat16 [16384, 1024], P(('dp', 'ctx')), may hold values from -6.5 to 6.5, as said below
- v_load: bfloat16 [16384, 1024], P(('dp', 'ctx')), may hold values from -6 to 6
- grad_out: bfloat16 [16384, 4096], P(('dp', 'ctx')), may hold values from -6 to 6
- pack_rows: int32 [128, 128, 2], P(('dp', 'ctx')), may hold values from -1 to 127, as said below
- unpack: int32 [128, 128], P(('dp', 'ctx')), may hold values from 0 to 255, as said below
- doc_lengths: int32 [8, 16], P('dp'), may hold values from 1 to 1024, 2048 in all within a row
Outputs:
- attended: bfloat16 [16384, 4096], P(('dp', 'ctx'))
- grad_q: bfloat16 [16384, 4096], P(('dp', 'ctx'))
- grad_k: bfloat16 [16384, 1024], P(('dp', 'ctx'))
- grad_v: bfloat16 [16384, 1024], P(('dp', 'ctx'))
The draws below stay inside these ranges and needn't reach their ends.
Inputs may be any that keep to these rules, and one draw needn't show every extreme that they name: `q_load`: custom queries: every entry lies in the stated range. `k_load`: custom keys: every entry lies in the stated range. pack_rows[s, b, j] is the row of device s's loader block sent in slot j of its message to device b, or -1 for an empty slot. Every row of a device is sent exactly once, every device receives exactly 128 rows, at most 2 rows go from one device to one device, and in every draw some pairs of devices carry exactly 2. Non-empty slots of a message come first. unpack[b, r] = s * 2 + j names a non-empty slot j of the message from device s to device b; each non-empty slot to b is named by exactly one r.
All inputs are finite; a program needn't handle non-finite values.
Results may differ from the reference program's by a relative error of at most 0.009.
The reference program's roundings to bfloat16 on the way count: a program that leaves them out, or rounds other values in their place, can miss the bound.
Values may be sent and summed in bfloat16 or wider, within the bound.
A program may use at most 128 MiB of HBM per device.

```python
import math
import jax
import jax.numpy as jnp
import numpy as np
from jax import lax

H = 32
KVH = 8
DH = 128
TOK_DEV = 128
SEQ = 2048
TOKENS = 16384
MOST = 1024
NDOCS = 16
N_DP = 8
DEVICES = 128


def routing_plan(key):
    per_pair = TOK_DEV // DEVICES
    capacity = 2 * per_pair
    device_ids = jnp.arange(DEVICES, dtype=jnp.int32)
    cycle_order = jax.random.permutation(jax.random.fold_in(key, 101), DEVICES).astype(jnp.int32)
    shift_level = jax.random.randint(jax.random.fold_in(key, 102), (), 0, per_pair + 1)
    main_pairs = (cycle_order[:, None] == device_ids[None, :]).astype(jnp.int32)
    next_pairs = (jnp.roll(cycle_order, -1)[:, None] == device_ids[None, :]).astype(jnp.int32)
    third_pairs = (jnp.roll(cycle_order, -2)[:, None] == device_ids[None, :]).astype(jnp.int32)
    counts = per_pair + shift_level * (main_pairs - next_pairs) + (per_pair - shift_level) * (main_pairs - third_pairs)
    row_ids = jnp.arange(TOK_DEV, dtype=jnp.int32)

    def per_source(row_counts, subkey):
        cumulative = jnp.cumsum(row_counts)
        targets = jnp.sum((cumulative[None, :] <= row_ids[:, None]).astype(jnp.int32), axis=1)
        targets = jax.random.permutation(subkey, targets)
        onehot = (targets[:, None] == device_ids[None, :]).astype(jnp.int32)
        slot_ids = jnp.sum((jnp.cumsum(onehot, axis=0) - onehot) * onehot, axis=1)
        return (targets, slot_ids)
    source_keys = jax.random.split(jax.random.fold_in(key, 103), DEVICES)
    targets, slot_ids = jax.vmap(per_source)(counts, source_keys)
    pack_table = jnp.full((DEVICES, DEVICES, capacity), -1, jnp.int32)
    pack_table = pack_table.at[device_ids[:, None], targets, slot_ids].set(jnp.broadcast_to(row_ids[None, :], (DEVICES, TOK_DEV)))
    occupied = jnp.transpose(pack_table >= 0, (1, 0, 2)).reshape(DEVICES, DEVICES * capacity)
    rank_keys = jax.random.split(jax.random.fold_in(key, 104), DEVICES)
    rank_draw = jax.vmap(lambda subkey: jax.random.permutation(subkey, DEVICES * capacity))(rank_keys).astype(jnp.int32)
    sort_keys = jnp.where(occupied, rank_draw, DEVICES * capacity + rank_draw)
    unpack_table = jnp.argsort(sort_keys, axis=1)[:, :TOK_DEV].astype(jnp.int32)
    return (pack_table, unpack_table)


def draw_pack_rows(key, part):
    pack_table, unpack_table = routing_plan(key)
    return pack_table


def draw_unpack(key, part):
    pack_table, unpack_table = routing_plan(key)
    return unpack_table


def draw_q_load(key, part):
    key = jax.random.fold_in(key, 5)
    values = jnp.clip(jax.random.normal(key, (TOKENS, H, DH), jnp.float32), -6.0, 6.0)
    return values.reshape(TOKENS, H * DH).astype(jnp.bfloat16)


def draw_k_load(key, part):
    key = jax.random.fold_in(key, 9)
    values = jnp.clip(jax.random.normal(key, (TOKENS, KVH, DH), jnp.float32), -6.0, 6.0)
    return values.reshape(TOKENS, KVH * DH).astype(jnp.bfloat16)


def shard_levels(own_key, extent, cuts, least, largest):
    factor_of, own = 1.0, jax.random.fold_in(own_key, 6)
    for position, shards_of in cuts:
        steps = jnp.exp(jax.random.uniform(jax.random.fold_in(own, position), (shards_of,), jnp.float32, least / len(cuts), largest / len(cuts)))
        factor_of = factor_of * jnp.repeat(steps, extent[position] // shards_of).reshape([-1 if axis == position else 1 for axis in range(len(extent))])
    return factor_of


def split_up(count, total, limit, skew):
    weights = [(1 << 20) // math.isqrt(grade ** skew) + 1 for grade in range(2, count + 1)]
    surplus, holding = total - limit - (count - 1), [1] * (count - 1)
    while surplus > 0:
        candidates = [i for i in range(count - 1) if holding[i] < limit]
        mass, remaining = sum([weights[i] for i in candidates]), surplus
        for i in candidates:
            addition = min(limit - holding[i], max(1, remaining * weights[i] // mass), surplus)
            holding[i] = holding[i] + addition
            surplus = surplus - addition
    return np.array([limit] + holding)


def ragged(stream_key, count, total, limit, lean):
    if count == 2:
        one = jax.random.randint(stream_key, (), max(1, total - limit), min(limit, total - 1) + 1)
        return jnp.stack([one, total - one])
    sizes = jnp.asarray(split_up(count, total, limit, lean), jnp.int32)
    pairs = (count - 1) // 2
    giver, sink = sizes[1:1 + 2 * pairs:2], sizes[2:2 + 2 * pairs:2]
    margin = jnp.minimum(giver - 1, limit - sink)
    shifted = jax.random.randint(jax.random.fold_in(stream_key, 1), (pairs,), 0, 1 << 20) % (margin + 1)
    sizes = sizes.at[1:1 + 2 * pairs:2].set(giver - shifted).at[2:2 + 2 * pairs:2].set(sink + shifted)
    return sizes[jax.random.permutation(jax.random.fold_in(stream_key, 2), count)]


def gaussian(stream_key, extent, scale, limit, cuts=(), kind=jnp.bfloat16):
    values = scale * jax.random.normal(stream_key, extent, jnp.float32)
    if cuts:
        values = values * shard_levels(stream_key, extent, cuts, -0.22, 0.18)
    return jnp.clip(values, -limit, limit).astype(kind)


def setup_inputs(seed: int = 0) -> dict:
    key_of = jax.random.split(jax.random.key(seed), 8)
    return {
        "q_load": draw_q_load(jax.random.fold_in(key_of[7], 71), 0),
        "k_load": draw_k_load(jax.random.fold_in(key_of[7], 71), 0),
        "v_load": gaussian(key_of[2], (TOKENS, KVH * DH), 1.0, 6.0, ((0, 128),)),
        "grad_out": gaussian(key_of[3], (TOKENS, H * DH), 1.0, 6.0, ((0, 128),)),
        "pack_rows": draw_pack_rows(jax.random.fold_in(key_of[7], 71), 0),
        "unpack": draw_unpack(jax.random.fold_in(key_of[7], 71), 0),
        "doc_lengths": jax.vmap(lambda own: ragged(own, NDOCS, SEQ, MOST, 2))(jax.random.split(key_of[6], N_DP)).reshape((N_DP, NDOCS)).astype(jnp.int32),
    }


def document_ids(positions, lengths):
    doc_ends = jnp.cumsum(lengths)
    return lax.optimization_barrier(jnp.sum((doc_ends[None, :] <= positions[:, None]).astype(jnp.int32), axis=1))

def block_attention(queries, grad_block, key_rows, value_rows, allowed):
    row_count = queries.shape[0]
    width = key_rows.shape[0]
    replicas = H // KVH
    score_scale = 1.0 / math.sqrt(DH)
    query_wide = queries.reshape(row_count, KVH, replicas, DH).astype(jnp.float32)
    key_wide = key_rows.reshape(width, KVH, DH).astype(jnp.float32)
    value_wide = value_rows.reshape(width, KVH, DH).astype(jnp.float32)
    scores = jnp.einsum('tgrd,kgd->grtk', query_wide, key_wide) * score_scale
    visible = allowed[None, None]
    row_max = lax.optimization_barrier(jnp.max(jnp.where(visible, scores, -jnp.inf), axis=-1, keepdims=True))
    weights = jnp.where(visible, jnp.exp(scores - row_max), 0.0)
    prob_full = weights / lax.optimization_barrier(jnp.sum(weights, axis=-1, keepdims=True))
    prob_low = prob_full.astype(jnp.bfloat16)
    attended = jnp.einsum('grtk,kgd->tgrd', prob_low.astype(jnp.float32), value_wide).astype(jnp.bfloat16)
    grad_wide = grad_block.reshape(row_count, KVH, replicas, DH).astype(jnp.float32)
    dprobs = jnp.einsum('tgrd,kgd->grtk', grad_wide, value_wide)
    row_delta = lax.optimization_barrier(jnp.sum(grad_wide * attended.astype(jnp.float32), axis=-1))
    row_delta = jnp.transpose(row_delta, (1, 2, 0))[..., None]
    dscores = (prob_full * (dprobs - row_delta) * score_scale).astype(jnp.bfloat16)
    grad_query = jnp.einsum('grtk,kgd->tgrd', dscores.astype(jnp.float32), key_wide).astype(jnp.bfloat16)
    grad_key = jnp.einsum('grtk,tgrd->kgd', dscores.astype(jnp.float32), query_wide)
    grad_value = jnp.einsum('grtk,tgrd->kgd', prob_low.astype(jnp.float32), grad_wide)
    return (attended.reshape(row_count, H * DH), grad_query.reshape(row_count, H * DH), grad_key.reshape(width, KVH * DH), grad_value.reshape(width, KVH * DH))

def rounded_term(term):
    low = lax.optimization_barrier(term.astype(jnp.bfloat16))
    return low.astype(jnp.float32)

def one_sequence(operands):
    queries, key_rows, value_rows, grad_rows, lengths = operands
    positions = jnp.arange(SEQ, dtype=jnp.int32)
    doc_index = document_ids(positions, lengths)
    key_pad = jnp.concatenate([jnp.zeros((MOST, KVH * DH), jnp.bfloat16), key_rows], axis=0)
    value_pad = jnp.concatenate([jnp.zeros((MOST, KVH * DH), jnp.bfloat16), value_rows], axis=0)
    index_pad = jnp.concatenate([jnp.full((MOST,), -1, jnp.int32), doc_index], axis=0)
    window = MOST + TOK_DEV

    def step_fn(totals, block_index):
        grad_keys, grad_values = totals
        row_start = (block_index * TOK_DEV).astype(jnp.int32)
        query_block = lax.dynamic_slice_in_dim(queries, row_start, TOK_DEV, 0)
        grad_block = lax.dynamic_slice_in_dim(grad_rows, row_start, TOK_DEV, 0)
        key_block = lax.dynamic_slice_in_dim(key_pad, row_start, window, 0)
        value_block = lax.dynamic_slice_in_dim(value_pad, row_start, window, 0)
        query_pos = row_start + jnp.arange(TOK_DEV, dtype=jnp.int32)
        key_pos = row_start - MOST + jnp.arange(window, dtype=jnp.int32)
        query_doc = lax.dynamic_slice_in_dim(doc_index, row_start, TOK_DEV, 0)
        key_doc = lax.dynamic_slice_in_dim(index_pad, row_start, window, 0)
        allowed = (key_doc[None, :] == query_doc[:, None]) & (key_pos[None, :] <= query_pos[:, None]) & (key_pos[None, :] >= 0)
        attended, grad_query, grad_key, grad_value = block_attention(query_block, grad_block, key_block, value_block, allowed)
        grad_key = rounded_term(grad_key)
        grad_value = rounded_term(grad_value)
        grad_keys = lax.dynamic_update_slice_in_dim(grad_keys, lax.dynamic_slice_in_dim(grad_keys, row_start, window, 0) + grad_key, row_start, 0)
        grad_values = lax.dynamic_update_slice_in_dim(grad_values, lax.dynamic_slice_in_dim(grad_values, row_start, window, 0) + grad_value, row_start, 0)
        return ((grad_keys, grad_values), (attended, grad_query))
    start_totals = (jnp.zeros((MOST + SEQ, KVH * DH), jnp.float32), jnp.zeros((MOST + SEQ, KVH * DH), jnp.float32))
    (grad_keys, grad_values), (attended, grad_query) = lax.scan(step_fn, start_totals, jnp.arange(SEQ // TOK_DEV, dtype=jnp.int32))
    return (attended.reshape(SEQ, H * DH), grad_query.reshape(SEQ, H * DH), grad_keys[MOST:].astype(jnp.bfloat16), grad_values[MOST:].astype(jnp.bfloat16))

def reference(q_load, k_load, v_load, grad_out, pack_rows, unpack, doc_lengths):
    capacity = pack_rows.shape[2]
    owners = jnp.arange(DEVICES, dtype=jnp.int32)[:, None]
    source = (unpack // capacity).astype(jnp.int32)
    slot_index = (unpack % capacity).astype(jnp.int32)
    local_row = pack_rows[source, owners, slot_index]
    anchor = (source * TOK_DEV + local_row).reshape(-1).astype(jnp.int32)
    queries = q_load[anchor].reshape(N_DP, SEQ, H * DH)
    key_rows = k_load[anchor].reshape(N_DP, SEQ, KVH * DH)
    value_rows = v_load[anchor].reshape(N_DP, SEQ, KVH * DH)
    grad_rows = grad_out.reshape(N_DP, SEQ, H * DH)
    attended, grad_query, grad_key, grad_value = lax.map(one_sequence, (queries, key_rows, value_rows, grad_rows, doc_lengths))
    attended = attended.reshape(TOKENS, H * DH)
    grad_q = jnp.zeros_like(q_load).at[anchor].set(grad_query.reshape(TOKENS, H * DH))
    grad_k = jnp.zeros_like(k_load).at[anchor].set(grad_key.reshape(TOKENS, KVH * DH))
    grad_v = jnp.zeros_like(v_load).at[anchor].set(grad_value.reshape(TOKENS, KVH * DH))
    return (attended, grad_q, grad_k, grad_v)
```

```python
import functools
import math

import jax
import jax.numpy as jnp
from jax import lax
from jax.experimental import pallas as pl
from jax.experimental.pallas import tpu as pltpu
from jax.sharding import PartitionSpec as P

H = 32
KVH = 8
DH = 128
TOK = 128
CTX = 16
DP = 8
DEV = 128
SEQ = 2048
MOST = 1024
COLS = 512
K = 32
GROWS = 144
BQ = 128
BK = 256
WMAX = MOST // BK + 1
VMEM_LIMIT = 56 * 2**20

F32 = jnp.float32
BF16 = jnp.bfloat16
MESH = pl.DeviceIdType.MESH


def dot(a, b, ca, cb):
    return lax.dot_general(a, b, (((ca,), (cb,)), ((), ())), preferred_element_type=F32)


def iota(shape, dim):
    return lax.broadcasted_iota(jnp.int32, shape, dim)


def pack_kernel(prow, pcol, unp, q, k, v, g, send, sendg, sel, sel_s):
    @pl.when(pl.program_id(0) == 0)
    def _():
        occupied = (prow[...] >= 0).astype(BF16)
        a, b = iota((256, 256), 0), iota((256, 256), 1)
        earlier = ((a < b) & (a // 32 == b // 32)).astype(BF16)
        rank = dot(jnp.broadcast_to(occupied, (16, 256)), earlier, 1, 0)[0:1]
        slot = iota((1, 256), 1) // 32 * K + rank.astype(jnp.int32)
        slot = jnp.where(prow[...] >= 0, slot, -1)
        place = (iota((8 * K, 256), 0) == slot).astype(BF16)
        holds = (pcol[...] == iota((256, TOK), 1)).astype(BF16)
        value = dot(place, holds, 1, 0).astype(BF16)
        sel_s[...] = value
        sel[...] = value

    s = sel_s[...]
    yq = dot(s, q[...], 1, 0)
    yk = dot(s, k[...], 1, 0)
    yv = dot(s, v[...], 1, 0)
    for d in range(DP):
        rows = slice(d * K, (d + 1) * K)
        for e in range(2):
            send[d, e, :, 0:256] = yq[rows, e * 256 : (e + 1) * 256].astype(BF16)
            send[d, e, :, 256:384] = yk[rows].astype(BF16)
            send[d, e, :, 384:512] = yv[rows].astype(BF16)
    ints = jnp.broadcast_to(unp[...].astype(F32), (16, TOK)).astype(BF16)
    for e in range(2):
        sendg[e, 0:TOK, :] = g[:, e * 256 : (e + 1) * 256]
        sendg[e, TOK:GROWS, 0:TOK] = ints
        sendg[e, TOK:GROWS, TOK:256] = jnp.zeros((16, 128), BF16)


def pack(prow, pcol, unp, q, k, v, g):
    whole = lambda shape: pl.BlockSpec(shape, lambda i: (0,) * len(shape))
    return pl.pallas_call(
        pack_kernel,
        grid=(KVH,),
        in_specs=[
            whole((1, 256)),
            whole((256, 1)),
            whole((1, TOK)),
            pl.BlockSpec((TOK, 512), lambda i: (0, i)),
            pl.BlockSpec((TOK, 128), lambda i: (0, i)),
            pl.BlockSpec((TOK, 128), lambda i: (0, i)),
            pl.BlockSpec((TOK, 512), lambda i: (0, i)),
        ],
        out_specs=[
            pl.BlockSpec((DP, 2, K, COLS), lambda i: (0, i, 0, 0)),
            pl.BlockSpec((2, GROWS, 256), lambda i: (i, 0, 0)),
            whole((8 * K, TOK)),
        ],
        out_shape=[
            jax.ShapeDtypeStruct((DP, CTX, K, COLS), BF16),
            jax.ShapeDtypeStruct((CTX, GROWS, 256), BF16),
            jax.ShapeDtypeStruct((8 * K, TOK), BF16),
        ],
        scratch_shapes=[pltpu.VMEM((8 * K, TOK), BF16)],
        compiler_params=pltpu.CompilerParams(vmem_limit_bytes=VMEM_LIMIT),
        name="pack_rows_to_messages",
    )(prow, pcol, unp, q, k, v, g)


def exchange_kernel(src, srcg, dst, dstg, send_sem, recv_sem, sendg_sem, recvg_sem, own_sem, owng_sem):
    d = lax.axis_index("dp")
    c = lax.axis_index("ctx")
    me = d * CTX + c
    z, core = lax.div(d, 2), lax.rem(d, 2)
    x, y = lax.div(c, 4), lax.rem(c, 4)

    own = pltpu.make_async_copy(src.at[me], dst.at[me], own_sem)
    own.start()
    owng = pltpu.make_async_copy(srcg.at[c], dstg.at[c], owng_sem)
    owng.start()

    def one(n):
        j = lax.rem(n * 37, DEV)
        dy = lax.rem(j, 2) + 2 * lax.rem(lax.div(j, 16), 2)
        dx = lax.rem(lax.div(j, 2), 2) + 2 * lax.rem(lax.div(j, 32), 2)
        dz = lax.rem(lax.div(j, 4), 2) + 2 * lax.div(j, 64)
        dcore = lax.rem(lax.div(j, 8), 2)
        td = lax.rem(z + dz, 4) * 2 + lax.rem(core + dcore, 2)
        tc = lax.rem(x + dx, 4) * 4 + lax.rem(y + dy, 4)
        pltpu.make_async_remote_copy(
            src_ref=src.at[td * CTX + tc],
            dst_ref=dst.at[me],
            send_sem=send_sem,
            recv_sem=recv_sem,
            device_id=(td, tc),
            device_id_type=MESH,
        ).start()

    def turn(n, carry):
        tc = lax.rem(c + lax.rem(n * 5, CTX), CTX)
        pltpu.make_async_remote_copy(
            src_ref=srcg.at[tc],
            dst_ref=dstg.at[c],
            send_sem=sendg_sem,
            recv_sem=recvg_sem,
            device_id=(d, tc),
            device_id_type=MESH,
        ).start()
        for i in range(8):
            one(8 * n - 8 + i + 1)
        return carry

    lax.fori_loop(1, CTX, turn, 0)
    for n in range(121, DEV):
        one(n)
    own.wait()
    owng.wait()
    pltpu.make_async_remote_copy(
        src_ref=srcg.at[pl.ds(0, CTX - 1)],
        dst_ref=dstg.at[pl.ds(0, CTX - 1)],
        send_sem=sendg_sem,
        recv_sem=recvg_sem,
        device_id=(d, c),
        device_id_type=MESH,
    ).wait()
    pltpu.make_async_remote_copy(
        src_ref=src.at[pl.ds(0, DEV - 1)],
        dst_ref=dst.at[pl.ds(0, DEV - 1)],
        send_sem=send_sem,
        recv_sem=recv_sem,
        device_id=(d, c),
        device_id_type=MESH,
    ).wait()


def exchange(src, srcg):
    return pl.pallas_call(
        exchange_kernel,
        in_specs=[pl.BlockSpec(memory_space=pl.ANY)] * 2,
        out_specs=[pl.BlockSpec(memory_space=pl.ANY)] * 2,
        out_shape=[
            jax.ShapeDtypeStruct(src.shape, src.dtype),
            jax.ShapeDtypeStruct(srcg.shape, srcg.dtype),
        ],
        scratch_shapes=[pltpu.SemaphoreType.DMA] * 6,
        compiler_params=pltpu.CompilerParams(has_side_effects=True),
        name="exchange",
    )(src, srcg)


def attention_kernel(lengths, recv, recvg, att, back, x, xo, mid, ts, dk, dv, col):
    scale = 1.0 / math.sqrt(DH)

    def slots_of(c):
        row = recvg[c, TOK : TOK + 8, 0:TOK].astype(F32)[0:1]
        return (iota((256, TOK), 0).astype(F32) == row).astype(BF16)

    occ = jnp.zeros((256, 128), F32)
    for c in range(CTX):
        occ = occ + dot(slots_of(c), (iota((TOK, 128), 1) == c).astype(BF16), 1, 0)
    pair = (iota((256, 256), 0) // 2 == iota((256, 256), 1) // 2).astype(BF16)
    count = dot(pair, occ.astype(BF16), 1, 0)
    before = (iota((128, 128), 0) < iota((128, 128), 1)).astype(BF16)
    base = dot(count.astype(BF16), before, 1, 0)
    u = iota((256, 128), 0)
    col[...] = base + (u % 2 + (u // 2) % 8 * K).astype(F32)

    lanes = iota((16, 8 * K), 1).astype(F32)

    def sort_senders(grp, carry):
        r0 = pl.multiple_of(grp * 16, 16)
        tab = col[pl.ds(r0, 16), :]
        t = jnp.concatenate(
            [(lanes == tab[:, c : c + 1]).astype(F32) for c in range(CTX)], axis=0
        ).astype(BF16)
        ts[grp] = t
        rows = dot(t, recv[grp], 1, 0).astype(BF16)
        for c in range(CTX):
            mid[c, pl.ds(r0, 16), :] = rows[c * 16 : (c + 1) * 16]
        return carry

    lax.fori_loop(0, 16, sort_senders, 0)

    def sort_rows(c, carry):
        x[pl.ds(pl.multiple_of(c * TOK, TOK), TOK), :] = dot(slots_of(c), mid[c], 0, 0).astype(BF16)
        return carry

    lax.fori_loop(0, CTX, sort_rows, 0)

    dk[...] = jnp.zeros_like(dk)
    dv[...] = jnp.zeros_like(dv)

    def doc_start(position):
        def step(n, carry):
            start, end = carry
            return (jnp.where(end <= position, end, start), end + lengths[0, n])

        return lax.fori_loop(0, 16, step, (jnp.int32(0), jnp.int32(0)))[0]

    def starts_of(positions):
        def step(n, carry):
            start, end = carry
            return (jnp.where(end <= positions, end, start), end + lengths[0, n])

        return lax.fori_loop(0, 16, step, (jnp.zeros_like(positions), jnp.int32(0)))[0]

    def tile(i, carry):
        q0 = pl.multiple_of(i * BQ, BQ)
        lo = doc_start(q0) // BK
        width = q0 // BK - lo + 1

        def attend(w):
            k0 = pl.multiple_of(lo * BK, BK)
            span = w * BK
            keys = x[pl.ds(k0, span), 256:384]
            values = x[pl.ds(k0, span), 384:512]
            queries = jnp.concatenate([x[pl.ds(q0, BQ), 0:128], x[pl.ds(q0, BQ), 128:256]], axis=0)
            grads = jnp.concatenate([recvg[i, 0:TOK, 0:128], recvg[i, 0:TOK, 128:256]], axis=0)
            qpos = q0 + iota((BQ, 1), 0)
            qstart = starts_of(qpos)
            qpos = jnp.concatenate([qpos, qpos], axis=0)
            qstart = jnp.concatenate([qstart, qstart], axis=0)
            kpos = k0 + iota((2 * BQ, span), 1)
            s = dot(queries, keys, 1, 1) * scale
            s = jnp.where((kpos >= qstart) & (kpos <= qpos), s, -1e30)
            top = jnp.max(s, axis=1, keepdims=True)
            e = jnp.exp(s - top)
            p = e * (1.0 / jnp.sum(e, axis=1, keepdims=True))
            low = p.astype(BF16)
            out = dot(low, values, 1, 0).astype(BF16)
            att[i, :, 0:128] = out[0:BQ]
            att[i, :, 128:256] = out[BQ:]
            delta = jnp.sum(grads.astype(F32) * out.astype(F32), axis=1, keepdims=True)
            dp = dot(grads, values, 1, 1)
            ds = (p * (dp - delta) * scale).astype(BF16)
            dq = dot(ds, keys, 1, 0).astype(BF16)
            xo[pl.ds(q0, BQ), 0:128] = dq[0:BQ]
            xo[pl.ds(q0, BQ), 128:256] = dq[BQ:]
            dk[pl.ds(k0, span), :] += dot(ds, queries, 0, 0)
            dv[pl.ds(k0, span), :] += dot(low, grads, 0, 0)

        for w in range(1, WMAX + 1):
            pl.when(width == w)(functools.partial(attend, w))
        return carry

    lax.fori_loop(0, SEQ // BQ, tile, 0)
    xo[:, 256:384] = dk[...].astype(BF16)
    xo[:, 384:512] = dv[...].astype(BF16)

    def unsort_rows(c, carry):
        mid[c] = dot(
            slots_of(c), xo[pl.ds(pl.multiple_of(c * TOK, TOK), TOK), :], 1, 0
        ).astype(BF16)
        return carry

    lax.fori_loop(0, CTX, unsort_rows, 0)

    def unsort_senders(grp, carry):
        r0 = pl.multiple_of(grp * 16, 16)
        rows = jnp.concatenate([mid[c, pl.ds(r0, 16), :] for c in range(CTX)], axis=0)
        back[grp] = dot(ts[grp], rows, 0, 0).astype(BF16)
        return carry

    lax.fori_loop(0, 16, unsort_senders, 0)


def attention(lengths, recv, recvg):
    vmem = pl.BlockSpec(memory_space=pltpu.VMEM)
    return pl.pallas_call(
        attention_kernel,
        in_specs=[pl.BlockSpec(memory_space=pltpu.SMEM), vmem, vmem],
        out_specs=[vmem, vmem],
        out_shape=[
            jax.ShapeDtypeStruct((CTX, TOK, 256), BF16),
            jax.ShapeDtypeStruct((16, 8 * K, COLS), BF16),
        ],
        scratch_shapes=[
            pltpu.VMEM((SEQ, COLS), BF16),
            pltpu.VMEM((SEQ, COLS), BF16),
            pltpu.VMEM((CTX, 256, COLS), BF16),
            pltpu.VMEM((16, 256, 8 * K), BF16),
            pltpu.VMEM((SEQ, DH), F32),
            pltpu.VMEM((SEQ, DH), F32),
            pltpu.VMEM((256, 128), F32),
        ],
        compiler_params=pltpu.CompilerParams(vmem_limit_bytes=VMEM_LIMIT),
        name="attention",
    )(lengths, recv, recvg)


def unpack_kernel(sel, back, att, attended, gq, gk, gv):
    s = sel[...]
    for e in range(2):
        attended[:, e * 256 : (e + 1) * 256] = att[e]
    parts = []
    for e in range(2):
        rows = jnp.concatenate([back[d, e].astype(F32) for d in range(DP)], axis=0).astype(BF16)
        parts.append(dot(s, rows, 0, 0))
        gq[:, e * 256 : (e + 1) * 256] = parts[e][:, 0:256].astype(BF16)
    both = parts[0][:, 256:] + parts[1][:, 256:]
    gk[...] = both[:, 0:128].astype(BF16)
    gv[...] = both[:, 128:256].astype(BF16)


def unpack_rows(sel, back, att):
    return pl.pallas_call(
        unpack_kernel,
        grid=(KVH,),
        in_specs=[
            pl.BlockSpec((8 * K, TOK), lambda i: (0, 0)),
            pl.BlockSpec((DP, 2, K, COLS), lambda i: (0, i, 0, 0)),
            pl.BlockSpec((2, TOK, 256), lambda i: (i, 0, 0)),
        ],
        out_specs=[
            pl.BlockSpec((TOK, 512), lambda i: (0, i)),
            pl.BlockSpec((TOK, 512), lambda i: (0, i)),
            pl.BlockSpec((TOK, 128), lambda i: (0, i)),
            pl.BlockSpec((TOK, 128), lambda i: (0, i)),
        ],
        out_shape=[
            jax.ShapeDtypeStruct((TOK, H * DH), BF16),
            jax.ShapeDtypeStruct((TOK, H * DH), BF16),
            jax.ShapeDtypeStruct((TOK, KVH * DH), BF16),
            jax.ShapeDtypeStruct((TOK, KVH * DH), BF16),
        ],
        compiler_params=pltpu.CompilerParams(vmem_limit_bytes=VMEM_LIMIT),
        name="messages_to_rows",
    )(sel, back, att)


def local(q_load, k_load, v_load, grad_out, pack_rows, unpack, doc_lengths):
    flat = pack_rows.reshape(1, 2 * DEV)
    send, sendg, sel = pack(
        flat, flat.reshape(2 * DEV, 1), unpack, q_load, k_load, v_load, grad_out
    )
    recv, recvg = exchange(send.reshape(DEV, K, COLS), sendg)
    att, back = attention(doc_lengths, recv.reshape(16, 8 * K, COLS), recvg)
    returned, turned = exchange(back.reshape(DEV, K, COLS), att)
    return unpack_rows(sel, returned.reshape(DP, CTX, K, COLS), turned)


def solution(mesh):
    rows = P(("dp", "ctx"), None)
    return jax.shard_map(
        local,
        mesh=mesh,
        in_specs=(rows, rows, rows, rows, P(("dp", "ctx"), None, None), rows, P("dp", None)),
        out_specs=(rows, rows, rows, rows),
        check_vma=False,
    )
```

```python
import functools
import math

import jax
import jax.numpy as jnp
from jax import lax
from jax.experimental import pallas as pl
from jax.experimental.pallas import tpu as pltpu
from jax.sharding import PartitionSpec as P

H = 32
KVH = 8
DH = 128
TOK = 128
CTX = 16
DP = 8
DEV = 128
SEQ = 2048
MOST = 1024
COLS = 512
FULL = 32
SHORT = 24
GROWS = 144
BQ = 128
BK = 256
WMAX = MOST // BK + 1
VMEM_LIMIT = 56 * 2**20

F32 = jnp.float32
BF16 = jnp.bfloat16
MESH = pl.DeviceIdType.MESH


def dot(a, b, ca, cb):
    return lax.dot_general(a, b, (((ca,), (cb,)), ((), ())), preferred_element_type=F32)


def iota(shape, dim):
    return lax.broadcasted_iota(jnp.int32, shape, dim)


def pack_kernel(K, prow, pcol, unp, q, k, v, g, send, sendg, sel, sel_s, over_s):
    @pl.when(pl.program_id(0) == 0)
    def _():
        occupied = (prow[...] >= 0).astype(BF16)
        a, b = iota((256, 256), 0), iota((256, 256), 1)
        earlier = ((a < b) & (a // 32 == b // 32)).astype(BF16)
        rank = dot(jnp.broadcast_to(occupied, (16, 256)), earlier, 1, 0)[0:1]
        rank = rank.astype(jnp.int32)
        slot = iota((1, 256), 1) // 32 * K + rank
        slot = jnp.where((prow[...] >= 0) & ((rank < K - 1) | (K == FULL)), slot, -1)
        over = jnp.max(jnp.where((prow[...] >= 0) & (rank >= K - 1), 1.0, 0.0), axis=1, keepdims=True)
        last = (iota((8 * K, TOK), 0) % K == K - 1) & (K < FULL)
        over_s[...] = jnp.where(last, over, 0.0)
        place = (iota((8 * K, 256), 0) == slot).astype(BF16)
        holds = (pcol[...] == iota((256, TOK), 1)).astype(BF16)
        value = dot(place, holds, 1, 0).astype(BF16)
        sel_s[...] = value
        sel[...] = value

    s = sel_s[...]
    yq = dot(s, q[...], 1, 0)
    yk = dot(s, k[...], 1, 0)
    yv = dot(s, v[...], 1, 0) + over_s[...]
    for d in range(DP):
        rows = slice(d * K, (d + 1) * K)
        for e in range(2):
            send[d, e, :, 0:256] = yq[rows, e * 256 : (e + 1) * 256].astype(BF16)
            send[d, e, :, 256:384] = yk[rows].astype(BF16)
            send[d, e, :, 384:512] = yv[rows].astype(BF16)
    ints = jnp.broadcast_to(unp[...].astype(F32), (16, TOK)).astype(BF16)
    for e in range(2):
        sendg[e, 0:TOK, :] = g[:, e * 256 : (e + 1) * 256]
        sendg[e, TOK:GROWS, 0:TOK] = ints
        sendg[e, TOK:GROWS, TOK:256] = jnp.zeros((16, 128), BF16)


def pack(K, prow, pcol, unp, q, k, v, g):
    whole = lambda shape: pl.BlockSpec(shape, lambda i: (0,) * len(shape))
    return pl.pallas_call(
        functools.partial(pack_kernel, K),
        grid=(KVH,),
        in_specs=[
            whole((1, 256)),
            whole((256, 1)),
            whole((1, TOK)),
            pl.BlockSpec((TOK, 512), lambda i: (0, i)),
            pl.BlockSpec((TOK, 128), lambda i: (0, i)),
            pl.BlockSpec((TOK, 128), lambda i: (0, i)),
            pl.BlockSpec((TOK, 512), lambda i: (0, i)),
        ],
        out_specs=[
            pl.BlockSpec((DP, 2, K, COLS), lambda i: (0, i, 0, 0)),
            pl.BlockSpec((2, GROWS, 256), lambda i: (i, 0, 0)),
            whole((8 * K, TOK)),
        ],
        out_shape=[
            jax.ShapeDtypeStruct((DP, CTX, K, COLS), BF16),
            jax.ShapeDtypeStruct((CTX, GROWS, 256), BF16),
            jax.ShapeDtypeStruct((8 * K, TOK), BF16),
        ],
        scratch_shapes=[pltpu.VMEM((8 * K, TOK), BF16), pltpu.VMEM((8 * K, TOK), F32)],
        compiler_params=pltpu.CompilerParams(vmem_limit_bytes=VMEM_LIMIT),
        name="pack_rows_to_messages",
    )(prow, pcol, unp, q, k, v, g)


def exchange_kernel(src, srcg, dst, dstg, send_sem, recv_sem, sendg_sem, recvg_sem, own_sem, owng_sem):
    d = lax.axis_index("dp")
    c = lax.axis_index("ctx")
    me = d * CTX + c
    z, core = lax.div(d, 2), lax.rem(d, 2)
    x, y = lax.div(c, 4), lax.rem(c, 4)

    own = pltpu.make_async_copy(src.at[me], dst.at[me], own_sem)
    own.start()
    owng = pltpu.make_async_copy(srcg.at[c], dstg.at[c], owng_sem)
    owng.start()

    def one(n):
        j = lax.rem(n * 37, DEV)
        dy = lax.rem(j, 2) + 2 * lax.rem(lax.div(j, 16), 2)
        dx = lax.rem(lax.div(j, 2), 2) + 2 * lax.rem(lax.div(j, 32), 2)
        dz = lax.rem(lax.div(j, 4), 2) + 2 * lax.div(j, 64)
        dcore = lax.rem(lax.div(j, 8), 2)
        td = lax.rem(z + dz, 4) * 2 + lax.rem(core + dcore, 2)
        tc = lax.rem(x + dx, 4) * 4 + lax.rem(y + dy, 4)
        pltpu.make_async_remote_copy(
            src_ref=src.at[td * CTX + tc],
            dst_ref=dst.at[me],
            send_sem=send_sem,
            recv_sem=recv_sem,
            device_id=(td, tc),
            device_id_type=MESH,
        ).start()

    def turn(n, carry):
        tc = lax.rem(c + lax.rem(n * 5, CTX), CTX)
        pltpu.make_async_remote_copy(
            src_ref=srcg.at[tc],
            dst_ref=dstg.at[c],
            send_sem=sendg_sem,
            recv_sem=recvg_sem,
            device_id=(d, tc),
            device_id_type=MESH,
        ).start()
        for i in range(8):
            one(8 * n - 8 + i + 1)
        return carry

    lax.fori_loop(1, CTX, turn, 0)
    for n in range(121, DEV):
        one(n)
    own.wait()
    owng.wait()
    pltpu.make_async_remote_copy(
        src_ref=srcg.at[pl.ds(0, CTX - 1)],
        dst_ref=dstg.at[pl.ds(0, CTX - 1)],
        send_sem=sendg_sem,
        recv_sem=recvg_sem,
        device_id=(d, c),
        device_id_type=MESH,
    ).wait()
    pltpu.make_async_remote_copy(
        src_ref=src.at[pl.ds(0, DEV - 1)],
        dst_ref=dst.at[pl.ds(0, DEV - 1)],
        send_sem=send_sem,
        recv_sem=recv_sem,
        device_id=(d, c),
        device_id_type=MESH,
    ).wait()


def exchange(src, srcg):
    return pl.pallas_call(
        exchange_kernel,
        in_specs=[pl.BlockSpec(memory_space=pl.ANY)] * 2,
        out_specs=[pl.BlockSpec(memory_space=pl.ANY)] * 2,
        out_shape=[
            jax.ShapeDtypeStruct(src.shape, src.dtype),
            jax.ShapeDtypeStruct(srcg.shape, srcg.dtype),
        ],
        scratch_shapes=[pltpu.SemaphoreType.DMA] * 6,
        compiler_params=pltpu.CompilerParams(has_side_effects=True),
        name="exchange",
    )(src, srcg)


def attention_kernel(K, lengths, recv, recvg, att, back, x, xo, mid, ts, dk, dv, col):
    scale = 1.0 / math.sqrt(DH)

    def slots_of(c):
        row = recvg[c, TOK : TOK + 8, 0:TOK].astype(F32)[0:1]
        return (iota((256, TOK), 0).astype(F32) == row).astype(BF16)

    occ = jnp.zeros((256, 128), F32)
    for c in range(CTX):
        occ = occ + dot(slots_of(c), (iota((TOK, 128), 1) == c).astype(BF16), 1, 0)
    pair = (iota((256, 256), 0) // 2 == iota((256, 256), 1) // 2).astype(BF16)
    count = dot(pair, occ.astype(BF16), 1, 0)
    before = (iota((128, 128), 0) < iota((128, 128), 1)).astype(BF16)
    base = dot(count.astype(BF16), before, 1, 0)
    u = iota((256, 128), 0)
    col[...] = base + (u % 2 + (u // 2) % 8 * K).astype(F32)

    lanes = iota((16, 8 * K), 1).astype(F32)

    def sort_senders(grp, carry):
        r0 = pl.multiple_of(grp * 16, 16)
        tab = col[pl.ds(r0, 16), :]
        t = jnp.concatenate(
            [(lanes == tab[:, c : c + 1]).astype(F32) for c in range(CTX)], axis=0
        ).astype(BF16)
        ts[grp] = t
        rows = dot(t, recv[grp], 1, 0).astype(BF16)
        for c in range(CTX):
            mid[c, pl.ds(r0, 16), :] = rows[c * 16 : (c + 1) * 16]
        return carry

    lax.fori_loop(0, 16, sort_senders, 0)

    def sort_rows(c, carry):
        x[pl.ds(pl.multiple_of(c * TOK, TOK), TOK), :] = dot(slots_of(c), mid[c], 0, 0).astype(BF16)
        return carry

    lax.fori_loop(0, CTX, sort_rows, 0)

    dk[...] = jnp.zeros_like(dk)
    dv[...] = jnp.zeros_like(dv)

    def doc_start(position):
        def step(n, carry):
            start, end = carry
            return (jnp.where(end <= position, end, start), end + lengths[0, n])

        return lax.fori_loop(0, 16, step, (jnp.int32(0), jnp.int32(0)))[0]

    def starts_of(positions):
        def step(n, carry):
            start, end = carry
            return (jnp.where(end <= positions, end, start), end + lengths[0, n])

        return lax.fori_loop(0, 16, step, (jnp.zeros_like(positions), jnp.int32(0)))[0]

    def tile(i, carry):
        q0 = pl.multiple_of(i * BQ, BQ)
        lo = doc_start(q0) // BK
        width = q0 // BK - lo + 1

        def attend(w):
            k0 = pl.multiple_of(lo * BK, BK)
            span = w * BK
            keys = x[pl.ds(k0, span), 256:384]
            values = x[pl.ds(k0, span), 384:512]
            queries = jnp.concatenate([x[pl.ds(q0, BQ), 0:128], x[pl.ds(q0, BQ), 128:256]], axis=0)
            grads = jnp.concatenate([recvg[i, 0:TOK, 0:128], recvg[i, 0:TOK, 128:256]], axis=0)
            qpos = q0 + iota((BQ, 1), 0)
            qstart = starts_of(qpos)
            qpos = jnp.concatenate([qpos, qpos], axis=0)
            qstart = jnp.concatenate([qstart, qstart], axis=0)
            kpos = k0 + iota((2 * BQ, span), 1)
            s = dot(queries, keys, 1, 1) * scale
            s = jnp.where((kpos >= qstart) & (kpos <= qpos), s, -1e30)
            top = jnp.max(s, axis=1, keepdims=True)
            e = jnp.exp(s - top)
            p = e * (1.0 / jnp.sum(e, axis=1, keepdims=True))
            low = p.astype(BF16)
            out = dot(low, values, 1, 0).astype(BF16)
            att[i, :, 0:128] = out[0:BQ]
            att[i, :, 128:256] = out[BQ:]
            delta = jnp.sum(grads.astype(F32) * out.astype(F32), axis=1, keepdims=True)
            dp = dot(grads, values, 1, 1)
            ds = (p * (dp - delta) * scale).astype(BF16)
            dq = dot(ds, keys, 1, 0).astype(BF16)
            xo[pl.ds(q0, BQ), 0:128] = dq[0:BQ]
            xo[pl.ds(q0, BQ), 128:256] = dq[BQ:]
            dk[pl.ds(k0, span), :] += dot(ds, queries, 0, 0)
            dv[pl.ds(k0, span), :] += dot(low, grads, 0, 0)

        for w in range(1, WMAX + 1):
            pl.when(width == w)(functools.partial(attend, w))
        return carry

    lax.fori_loop(0, SEQ // BQ, tile, 0)
    xo[:, 256:384] = dk[...].astype(BF16)
    xo[:, 384:512] = dv[...].astype(BF16)

    def unsort_rows(c, carry):
        mid[c] = dot(
            slots_of(c), xo[pl.ds(pl.multiple_of(c * TOK, TOK), TOK), :], 1, 0
        ).astype(BF16)
        return carry

    lax.fori_loop(0, CTX, unsort_rows, 0)

    def unsort_senders(grp, carry):
        r0 = pl.multiple_of(grp * 16, 16)
        rows = jnp.concatenate([mid[c, pl.ds(r0, 16), :] for c in range(CTX)], axis=0)
        back[grp] = dot(ts[grp], rows, 0, 0).astype(BF16)
        return carry

    lax.fori_loop(0, 16, unsort_senders, 0)


def attention(K, lengths, recv, recvg):
    vmem = pl.BlockSpec(memory_space=pltpu.VMEM)
    return pl.pallas_call(
        functools.partial(attention_kernel, K),
        in_specs=[pl.BlockSpec(memory_space=pltpu.SMEM), vmem, vmem],
        out_specs=[vmem, vmem],
        out_shape=[
            jax.ShapeDtypeStruct((CTX, TOK, 256), BF16),
            jax.ShapeDtypeStruct((16, 8 * K, COLS), BF16),
        ],
        scratch_shapes=[
            pltpu.VMEM((SEQ, COLS), BF16),
            pltpu.VMEM((SEQ, COLS), BF16),
            pltpu.VMEM((CTX, 256, COLS), BF16),
            pltpu.VMEM((16, 256, 8 * K), BF16),
            pltpu.VMEM((SEQ, DH), F32),
            pltpu.VMEM((SEQ, DH), F32),
            pltpu.VMEM((256, 128), F32),
        ],
        compiler_params=pltpu.CompilerParams(vmem_limit_bytes=VMEM_LIMIT),
        name="attention",
    )(lengths, recv, recvg)


def unpack_kernel(sel, back, att, attended, gq, gk, gv):
    s = sel[...]
    for e in range(2):
        attended[:, e * 256 : (e + 1) * 256] = att[e]
    parts = []
    for e in range(2):
        rows = jnp.concatenate([back[d, e].astype(F32) for d in range(DP)], axis=0).astype(BF16)
        parts.append(dot(s, rows, 0, 0))
        gq[:, e * 256 : (e + 1) * 256] = parts[e][:, 0:256].astype(BF16)
    both = parts[0][:, 256:] + parts[1][:, 256:]
    gk[...] = both[:, 0:128].astype(BF16)
    gv[...] = both[:, 128:256].astype(BF16)


def unpack_rows(K, sel, back, att):
    return pl.pallas_call(
        unpack_kernel,
        grid=(KVH,),
        in_specs=[
            pl.BlockSpec((8 * K, TOK), lambda i: (0, 0)),
            pl.BlockSpec((DP, 2, K, COLS), lambda i: (0, i, 0, 0)),
            pl.BlockSpec((2, TOK, 256), lambda i: (i, 0, 0)),
        ],
        out_specs=[
            pl.BlockSpec((TOK, 512), lambda i: (0, i)),
            pl.BlockSpec((TOK, 512), lambda i: (0, i)),
            pl.BlockSpec((TOK, 128), lambda i: (0, i)),
            pl.BlockSpec((TOK, 128), lambda i: (0, i)),
        ],
        out_shape=[
            jax.ShapeDtypeStruct((TOK, H * DH), BF16),
            jax.ShapeDtypeStruct((TOK, H * DH), BF16),
            jax.ShapeDtypeStruct((TOK, KVH * DH), BF16),
            jax.ShapeDtypeStruct((TOK, KVH * DH), BF16),
        ],
        compiler_params=pltpu.CompilerParams(vmem_limit_bytes=VMEM_LIMIT),
        name="messages_to_rows",
    )(sel, back, att)


def forward(K, q_load, k_load, v_load, grad_out, pack_rows, unpack):
    flat = pack_rows.reshape(1, 2 * DEV)
    send, sendg, sel = pack(
        K, flat, flat.reshape(2 * DEV, 1), unpack, q_load, k_load, v_load, grad_out
    )
    recv, recvg = exchange(send.reshape(DEV, K, COLS), sendg)
    return sel, recv, recvg


def finish(K, doc_lengths, sel, recv, recvg):
    att, back = attention(K, doc_lengths, recv.reshape(16, 8 * K, COLS), recvg)
    returned, turned = exchange(back.reshape(DEV, K, COLS), att)
    return unpack_rows(K, sel, returned.reshape(DP, CTX, K, COLS), turned)


def local(q_load, k_load, v_load, grad_out, pack_rows, unpack, doc_lengths):
    operands = (q_load, k_load, v_load, grad_out, pack_rows, unpack)
    sel, recv, recvg = forward(SHORT, *operands)
    over = jnp.max(recv[:, SHORT - 1, COLS - 1].astype(F32)) > 0.5
    return lax.cond(
        over,
        lambda: finish(FULL, doc_lengths, *forward(FULL, *operands)),
        lambda: finish(SHORT, doc_lengths, sel, recv, recvg),
    )


def solution(mesh):
    rows = P(("dp", "ctx"), None)
    return jax.shard_map(
        local,
        mesh=mesh,
        in_specs=(rows, rows, rows, rows, P(("dp", "ctx"), None, None), rows, P("dp", None)),
        out_specs=(rows, rows, rows, rows),
        check_vma=False,
    )
```

```python
import functools
import math

import jax
import jax.numpy as jnp
from jax import lax
from jax.experimental import pallas as pl
from jax.experimental.pallas import tpu as pltpu
from jax.sharding import PartitionSpec as P

H = 32
KVH = 8
DH = 128
TOK = 128
CTX = 16
DP = 8
DEV = 128
SEQ = 2048
MOST = 1024
COLS = 384
FULL = 32
SHORT = 24
GROWS = 144
BQ = 128
BK = 256
WMAX = MOST // BK + 1
VMEM_LIMIT = 56 * 2**20

F32 = jnp.float32
BF16 = jnp.bfloat16
MESH = pl.DeviceIdType.MESH


def dot(a, b, ca, cb):
    return lax.dot_general(a, b, (((ca,), (cb,)), ((), ())), preferred_element_type=F32)


def iota(shape, dim):
    return lax.broadcasted_iota(jnp.int32, shape, dim)


def pack_kernel(K, prow, pcol, unp, lengths, q, k, v, g, send, sendg, sel, sel_s, over_s):
    @pl.when(pl.program_id(0) == 0)
    def _():
        occupied = (prow[...] >= 0).astype(BF16)
        a, b = iota((256, 256), 0), iota((256, 256), 1)
        earlier = ((a < b) & (a // 32 == b // 32)).astype(BF16)
        rank = dot(jnp.broadcast_to(occupied, (16, 256)), earlier, 1, 0)[0:1]
        rank = rank.astype(jnp.int32)
        slot = iota((1, 256), 1) // 32 * K + rank
        slot = jnp.where((prow[...] >= 0) & ((rank < K - 1) | (K == FULL)), slot, -1)
        over = jnp.max(jnp.where((prow[...] >= 0) & (rank >= K - 1), 1.0, 0.0), axis=1, keepdims=True)
        last = (iota((8 * K, TOK), 0) % K == K - 1) & (K < FULL)
        over_s[...] = jnp.where(last, over, 0.0)
        place = (iota((8 * K, 256), 0) == slot).astype(BF16)
        holds = (pcol[...] == iota((256, TOK), 1)).astype(BF16)
        value = dot(place, holds, 1, 0).astype(BF16)
        sel_s[...] = value
        sel[...] = value

    s = sel_s[...]
    yq = dot(s, q[...], 1, 0)
    yk = dot(s, k[...], 1, 0)
    yv = dot(s, v[...], 1, 0)
    ykv = (yk + over_s[...], yv + over_s[...])
    for z in range(4):
        for core in range(2):
            for e in range(2):
                rows = slice((2 * z + e) * K, (2 * z + e + 1) * K)
                send[z, core, e, 0, :, 0:256] = yq[rows, core * 256 : (core + 1) * 256].astype(BF16)
                send[z, core, e, 0, :, 256:384] = ykv[core][rows].astype(BF16)
    r = iota((16, TOK), 0)
    spread = (iota((16, TOK), 0) == iota((16, TOK), 1)).astype(BF16)
    sizes = jnp.broadcast_to(lengths[...], (16, 16))
    high = dot((sizes // 8).astype(F32).astype(BF16), spread, 1, 0)
    low = dot((sizes % 8).astype(F32).astype(BF16), spread, 1, 0)
    ints = jnp.where(r < 8, unp[...].astype(F32), jnp.where(r < 12, high, low)).astype(BF16)
    for core in range(2):
        sendg[core, 0, 0:TOK, :] = g[:, core * 256 : (core + 1) * 256]
        sendg[core, 0, TOK:GROWS, 0:TOK] = ints
        sendg[core, 0, TOK:GROWS, TOK:256] = jnp.zeros((16, 128), BF16)


def pack(K, prow, pcol, unp, lengths, q, k, v, g):
    whole = lambda shape: pl.BlockSpec(shape, lambda i: (0,) * len(shape))
    return pl.pallas_call(
        functools.partial(pack_kernel, K),
        grid=(KVH,),
        in_specs=[
            whole((1, 256)),
            whole((256, 1)),
            whole((1, TOK)),
            whole((1, 16)),
            pl.BlockSpec((TOK, 512), lambda i: (0, i)),
            pl.BlockSpec((TOK, 128), lambda i: (0, i)),
            pl.BlockSpec((TOK, 128), lambda i: (0, i)),
            pl.BlockSpec((TOK, 512), lambda i: (0, i)),
        ],
        out_specs=[
            pl.BlockSpec((4, 2, 2, 1, K, COLS), lambda i: (0, 0, 0, i, 0, 0)),
            pl.BlockSpec((2, 1, GROWS, 256), lambda i: (0, i, 0, 0)),
            whole((8 * K, TOK)),
        ],
        out_shape=[
            jax.ShapeDtypeStruct((4, 2, 2, KVH, K, COLS), BF16),
            jax.ShapeDtypeStruct((2, KVH, GROWS, 256), BF16),
            jax.ShapeDtypeStruct((8 * K, TOK), BF16),
        ],
        scratch_shapes=[pltpu.VMEM((8 * K, TOK), BF16), pltpu.VMEM((8 * K, TOK), F32)],
        compiler_params=pltpu.CompilerParams(vmem_limit_bytes=VMEM_LIMIT),
        name="pack_rows_to_messages",
    )(prow, pcol, unp, lengths, q, k, v, g)


def remote(src, dst, send_sem, recv_sem, target):
    return pltpu.make_async_remote_copy(
        src_ref=src,
        dst_ref=dst,
        send_sem=send_sem,
        recv_sem=recv_sem,
        device_id=target,
        device_id_type=MESH,
    )


def place():
    d = lax.axis_index("dp")
    c = lax.axis_index("ctx")
    return d, c, lax.div(d, 2), lax.rem(d, 2)


def partner(n):
    d, c, z, core = place()
    x, y = lax.div(c, 4), lax.rem(c, 4)
    j = lax.rem(n * 37, DEV)
    dy = lax.rem(j, 2) + 2 * lax.rem(lax.div(j, 16), 2)
    dx = lax.rem(lax.div(j, 2), 2) + 2 * lax.rem(lax.div(j, 32), 2)
    dz = lax.rem(lax.div(j, 4), 2) + 2 * lax.div(j, 64)
    dcore = lax.rem(lax.div(j, 8), 2)
    return lax.rem(z + dz, 4) * 2 + lax.rem(core + dcore, 2), lax.rem(x + dx, 4) * 4 + lax.rem(y + dy, 4)


def to_all(src, dst, send_sem, recv_sem, beside=None):
    d, c, _, _ = place()
    me = d * CTX + c

    def one(n):
        td, tc = partner(n)
        remote(src.at[td * CTX + tc], dst.at[me], send_sem, recv_sem, (td, tc)).start()

    def some(n, carry):
        if beside is not None:
            beside(n)
        for i in range(8):
            one(8 * n - 7 + i)
        return carry

    lax.fori_loop(1, CTX, some, 0)
    for n in range(121, DEV):
        one(n)


def wait_all(src, dst, send_sem, recv_sem, count):
    d, c, _, _ = place()
    remote(src.at[pl.ds(0, count)], dst.at[pl.ds(0, count)], send_sem, recv_sem, (d, c)).wait()


def exchange_in_kernel(
    src, srcg, dst, other, dstg,
    send_sem, recv_sem, sendg_sem, recvg_sem, sendo_sem, recvo_sem, own_sem, owng_sem,
):
    d, c, z, core = place()
    me = d * CTX + c
    mine = core == lax.div(c, 8)
    first = core * 8 + lax.rem(c, 8)

    def grads(j):
        target = (2 * z + lax.div(j, 8), core * 8 + lax.rem(j, 8))
        remote(srcg.at[j], dstg.at[c], sendg_sem, recvg_sem, target).start()

    own = pltpu.make_async_copy(src.at[me], dst.at[me], own_sem)
    own.start()
    owng = pltpu.make_async_copy(srcg.at[first], dstg.at[c], owng_sem)

    @pl.when(mine)
    def _():
        owng.start()

    @pl.when(jnp.logical_not(mine))
    def _():
        grads(first)

    to_all(src, dst, send_sem, recv_sem, lambda n: grads(lax.rem(first + lax.rem(n * 5, CTX), CTX)))
    own.wait()
    wait_all(src, dst, send_sem, recv_sem, DEV - 1)
    swap = remote(dst.at[:, :, pl.ds(256, 128)], other, sendo_sem, recvo_sem, (2 * z + 1 - core, c))
    swap.start()

    @pl.when(mine)
    def _():
        owng.wait()
        wait_all(srcg, dstg, sendg_sem, recvg_sem, CTX - 1)

    @pl.when(jnp.logical_not(mine))
    def _():
        wait_all(srcg, dstg, sendg_sem, recvg_sem, CTX)

    swap.wait()


def exchange_in(src, srcg):
    anywhere = pl.BlockSpec(memory_space=pl.ANY)
    return pl.pallas_call(
        exchange_in_kernel,
        in_specs=[anywhere] * 2,
        out_specs=[anywhere] * 3,
        out_shape=[
            jax.ShapeDtypeStruct(src.shape, BF16),
            jax.ShapeDtypeStruct(src.shape[:2] + (128,), BF16),
            jax.ShapeDtypeStruct(srcg.shape, BF16),
        ],
        scratch_shapes=[pltpu.SemaphoreType.DMA] * 8,
        compiler_params=pltpu.CompilerParams(has_side_effects=True),
        name="exchange_in",
    )(src, srcg)


def exchange_out_kernel(
    src, keep, give, srcg, dst, dstkv, dstg,
    other, total,
    send_sem, recv_sem, sendk_sem, recvk_sem, sendg_sem, recvg_sem, sendo_sem, recvo_sem,
    own_sem, ownk_sem, owng_sem,
):
    d, c, z, core = place()
    me = d * CTX + c
    e = lax.div(c, 8)
    mine = core == e
    slot = core * 8 + lax.rem(c, 8)

    def grads(j):
        remote(srcg.at[j], dstg.at[slot], sendg_sem, recvg_sem, (2 * z + e, j)).start()

    swap = remote(give, other, sendo_sem, recvo_sem, (2 * z + 1 - core, c))
    swap.start()
    own = pltpu.make_async_copy(src.at[me], dst.at[me], own_sem)
    own.start()
    owng = pltpu.make_async_copy(srcg.at[c], dstg.at[slot], owng_sem)

    @pl.when(mine)
    def _():
        owng.start()

    @pl.when(jnp.logical_not(mine))
    def _():
        grads(c)

    to_all(src, dst, send_sem, recv_sem, lambda n: grads(lax.rem(c + lax.rem(n * 5, CTX), CTX)))
    swap.wait()
    total[...] = (keep[...].astype(F32) + other[...].astype(F32)).astype(BF16)
    ownk = pltpu.make_async_copy(total.at[me], dstkv.at[me], ownk_sem)
    ownk.start()
    to_all(total, dstkv, sendk_sem, recvk_sem)
    own.wait()
    ownk.wait()

    @pl.when(mine)
    def _():
        owng.wait()
        wait_all(srcg, dstg, sendg_sem, recvg_sem, CTX - 1)

    @pl.when(jnp.logical_not(mine))
    def _():
        wait_all(srcg, dstg, sendg_sem, recvg_sem, CTX)

    wait_all(src, dst, send_sem, recv_sem, DEV - 1)
    wait_all(total, dstkv, sendk_sem, recvk_sem, DEV - 1)


def exchange_out(src, keep, give, srcg):
    anywhere = pl.BlockSpec(memory_space=pl.ANY)
    return pl.pallas_call(
        exchange_out_kernel,
        in_specs=[anywhere, pl.BlockSpec(memory_space=pltpu.VMEM), anywhere, anywhere],
        out_specs=[anywhere] * 3,
        out_shape=[
            jax.ShapeDtypeStruct(src.shape, BF16),
            jax.ShapeDtypeStruct(keep.shape, BF16),
            jax.ShapeDtypeStruct(srcg.shape, BF16),
        ],
        scratch_shapes=[pltpu.VMEM(keep.shape, BF16)] * 2 + [pltpu.SemaphoreType.DMA] * 11,
        compiler_params=pltpu.CompilerParams(has_side_effects=True, vmem_limit_bytes=VMEM_LIMIT),
        name="exchange_out",
    )(src, keep, give, srcg)


def attention_kernel(
    K, recv, other, recvg, att, back, keep, give, x, xo, mid, ts, dk, dv, col, lengths
):
    scale = 1.0 / math.sqrt(DH)
    first_core = lax.rem(lax.axis_index("dp"), 2) == 0
    sizes = recvg[0, TOK:GROWS, 0:TOK].astype(F32)
    sizes = (sizes[8:9] * 8 + sizes[12:13]).astype(jnp.int32)
    for n in range(16):
        lengths[n] = jnp.sum(jnp.where(iota((1, TOK), 1) == n, sizes, 0))

    def slots_of(c):
        row = recvg[c, TOK : TOK + 8, 0:TOK].astype(F32)[0:1]
        return (iota((256, TOK), 0).astype(F32) == row).astype(BF16)

    occ = jnp.zeros((256, 128), F32)
    for c in range(CTX):
        occ = occ + dot(slots_of(c), (iota((TOK, 128), 1) == c).astype(BF16), 1, 0)
    pair = (iota((256, 256), 0) // 2 == iota((256, 256), 1) // 2).astype(BF16)
    count = dot(pair, occ.astype(BF16), 1, 0)
    before = (iota((128, 128), 0) < iota((128, 128), 1)).astype(BF16)
    base = dot(count.astype(BF16), before, 1, 0)
    u = iota((256, 128), 0)
    col[...] = base + (u % 2 + (u // 2) % 8 * K).astype(F32)

    lanes = iota((16, 8 * K), 1).astype(F32)

    def sort_senders(grp, carry):
        r0 = pl.multiple_of(grp * 16, 16)
        tab = col[pl.ds(r0, 16), :]
        t = jnp.concatenate(
            [(lanes == tab[:, c : c + 1]).astype(F32) for c in range(CTX)], axis=0
        ).astype(BF16)
        ts[grp] = t
        rows = dot(t, recv[grp], 1, 0).astype(BF16)
        rows2 = dot(t, other[grp], 1, 0).astype(BF16)
        for c in range(CTX):
            mid[c, pl.ds(r0, 16), 0:384] = rows[c * 16 : (c + 1) * 16]
            mid[c, pl.ds(r0, 16), 384:512] = rows2[c * 16 : (c + 1) * 16]
        return carry

    lax.fori_loop(0, 16, sort_senders, 0)

    def sort_rows(c, carry):
        y = dot(slots_of(c), mid[c], 0, 0)
        r = pl.ds(pl.multiple_of(c * TOK, TOK), TOK)
        x[r, 0:256] = y[:, 0:256].astype(BF16)
        x[r, 256:384] = jnp.where(first_core, y[:, 256:384], y[:, 384:512]).astype(BF16)
        x[r, 384:512] = jnp.where(first_core, y[:, 384:512], y[:, 256:384]).astype(BF16)
        return carry

    lax.fori_loop(0, CTX, sort_rows, 0)

    dk[...] = jnp.zeros_like(dk)
    dv[...] = jnp.zeros_like(dv)

    def doc_start(position):
        def step(n, carry):
            start, end = carry
            return (jnp.where(end <= position, end, start), end + lengths[n])

        return lax.fori_loop(0, 16, step, (jnp.int32(0), jnp.int32(0)))[0]

    def starts_of(positions):
        def step(n, carry):
            start, end = carry
            return (jnp.where(end <= positions, end, start), end + lengths[n])

        return lax.fori_loop(0, 16, step, (jnp.zeros_like(positions), jnp.int32(0)))[0]

    def tile(i, carry):
        q0 = pl.multiple_of(i * BQ, BQ)
        lo = doc_start(q0) // BK
        width = q0 // BK - lo + 1

        def attend(w):
            k0 = pl.multiple_of(lo * BK, BK)
            span = w * BK
            keys = x[pl.ds(k0, span), 256:384]
            values = x[pl.ds(k0, span), 384:512]
            queries = jnp.concatenate([x[pl.ds(q0, BQ), 0:128], x[pl.ds(q0, BQ), 128:256]], axis=0)
            grads = jnp.concatenate([recvg[i, 0:TOK, 0:128], recvg[i, 0:TOK, 128:256]], axis=0)
            qpos = q0 + iota((BQ, 1), 0)
            qstart = starts_of(qpos)
            qpos = jnp.concatenate([qpos, qpos], axis=0)
            qstart = jnp.concatenate([qstart, qstart], axis=0)
            kpos = k0 + iota((2 * BQ, span), 1)
            s = dot(queries, keys, 1, 1) * scale
            s = jnp.where((kpos >= qstart) & (kpos <= qpos), s, -1e30)
            top = jnp.max(s, axis=1, keepdims=True)
            e = jnp.exp(s - top)
            p = e * (1.0 / jnp.sum(e, axis=1, keepdims=True))
            low = p.astype(BF16)
            out = dot(low, values, 1, 0).astype(BF16)
            att[i, :, 0:128] = out[0:BQ]
            att[i, :, 128:256] = out[BQ:]
            delta = jnp.sum(grads.astype(F32) * out.astype(F32), axis=1, keepdims=True)
            dp = dot(grads, values, 1, 1)
            ds = (p * (dp - delta) * scale).astype(BF16)
            dq = dot(ds, keys, 1, 0).astype(BF16)
            xo[pl.ds(q0, BQ), 0:128] = dq[0:BQ]
            xo[pl.ds(q0, BQ), 128:256] = dq[BQ:]
            dk[pl.ds(k0, span), :] += dot(ds, queries, 0, 0)
            dv[pl.ds(k0, span), :] += dot(low, grads, 0, 0)

        for w in range(1, WMAX + 1):
            pl.when(width == w)(functools.partial(attend, w))
        return carry

    lax.fori_loop(0, SEQ // BQ, tile, 0)
    xo[:, 256:384] = jnp.where(first_core, dk[...], dv[...]).astype(BF16)
    xo[:, 384:512] = jnp.where(first_core, dv[...], dk[...]).astype(BF16)

    def unsort_rows(c, carry):
        mid[c] = dot(
            slots_of(c), xo[pl.ds(pl.multiple_of(c * TOK, TOK), TOK), :], 1, 0
        ).astype(BF16)
        return carry

    lax.fori_loop(0, CTX, unsort_rows, 0)

    def unsort_senders(grp, carry):
        r0 = pl.multiple_of(grp * 16, 16)
        rows = jnp.concatenate([mid[c, pl.ds(r0, 16), :] for c in range(CTX)], axis=0)
        out = dot(ts[grp], rows, 0, 0).astype(BF16)
        back[grp] = out[:, 0:256]
        keep[grp] = out[:, 256:384]
        give[grp] = out[:, 384:512]
        return carry

    lax.fori_loop(0, 16, unsort_senders, 0)


def attention(K, recv, other, recvg):
    vmem = pl.BlockSpec(memory_space=pltpu.VMEM)
    return pl.pallas_call(
        functools.partial(attention_kernel, K),
        in_specs=[vmem] * 3,
        out_specs=[vmem] * 4,
        out_shape=[
            jax.ShapeDtypeStruct((CTX, TOK, 256), BF16),
            jax.ShapeDtypeStruct((16, 8 * K, 256), BF16),
            jax.ShapeDtypeStruct((16, 8 * K, 128), BF16),
            jax.ShapeDtypeStruct((16, 8 * K, 128), BF16),
        ],
        scratch_shapes=[
            pltpu.VMEM((SEQ, 512), BF16),
            pltpu.VMEM((SEQ, 512), BF16),
            pltpu.VMEM((CTX, 256, 512), BF16),
            pltpu.VMEM((16, 256, 8 * K), BF16),
            pltpu.VMEM((SEQ, DH), F32),
            pltpu.VMEM((SEQ, DH), F32),
            pltpu.VMEM((256, 128), F32),
            pltpu.SMEM((16,), jnp.int32),
        ],
        compiler_params=pltpu.CompilerParams(vmem_limit_bytes=VMEM_LIMIT),
        name="attention",
    )(recv, other, recvg)


def unpack_kernel(K, sel, back, backkv, att, attended, gq, gk, gv):
    s = sel[...]
    by_sequence = [(z, e) for z in range(4) for e in range(2)]
    for core, out in ((0, gk), (1, gv)):
        cols = slice(core * 256, (core + 1) * 256)
        attended[:, cols] = att[core, 0]
        rows = [back[z, core, e, 0].astype(F32) for z, e in by_sequence]
        gq[:, cols] = dot(s, jnp.concatenate(rows, axis=0).astype(BF16), 0, 0).astype(BF16)
        rows = [backkv[z, core, e, 0].astype(F32) for z, e in by_sequence]
        out[...] = dot(s, jnp.concatenate(rows, axis=0).astype(BF16), 0, 0).astype(BF16)


def unpack_rows(K, sel, back, backkv, att):
    return pl.pallas_call(
        functools.partial(unpack_kernel, K),
        grid=(KVH,),
        in_specs=[
            pl.BlockSpec((8 * K, TOK), lambda i: (0, 0)),
            pl.BlockSpec((4, 2, 2, 1, K, 256), lambda i: (0, 0, 0, i, 0, 0)),
            pl.BlockSpec((4, 2, 2, 1, K, 128), lambda i: (0, 0, 0, i, 0, 0)),
            pl.BlockSpec((2, 1, TOK, 256), lambda i: (0, i, 0, 0)),
        ],
        out_specs=[
            pl.BlockSpec((TOK, 512), lambda i: (0, i)),
            pl.BlockSpec((TOK, 512), lambda i: (0, i)),
            pl.BlockSpec((TOK, 128), lambda i: (0, i)),
            pl.BlockSpec((TOK, 128), lambda i: (0, i)),
        ],
        out_shape=[
            jax.ShapeDtypeStruct((TOK, H * DH), BF16),
            jax.ShapeDtypeStruct((TOK, H * DH), BF16),
            jax.ShapeDtypeStruct((TOK, KVH * DH), BF16),
            jax.ShapeDtypeStruct((TOK, KVH * DH), BF16),
        ],
        compiler_params=pltpu.CompilerParams(vmem_limit_bytes=VMEM_LIMIT),
        name="messages_to_rows",
    )(sel, back, backkv, att)


def forward(K, q_load, k_load, v_load, grad_out, pack_rows, unpack, doc_lengths):
    flat = pack_rows.reshape(1, 2 * DEV)
    send, sendg, sel = pack(
        K, flat, flat.reshape(2 * DEV, 1), unpack, doc_lengths, q_load, k_load, v_load, grad_out
    )
    return sel, *exchange_in(send.reshape(DEV, K, COLS), sendg.reshape(CTX, GROWS, 256))


def finish(K, sel, recv, other, recvg):
    recv, other = (a.reshape(16, 8 * K, -1) for a in (recv, other))
    att, *parts = attention(K, recv, other, recvg)
    back, keep, give = (a.reshape(DEV, K, -1) for a in parts)
    returned, returnedkv, turned = exchange_out(back, keep, give, att)
    returned, returnedkv = (a.reshape(4, 2, 2, KVH, K, -1) for a in (returned, returnedkv))
    return unpack_rows(K, sel, returned, returnedkv, turned.reshape(2, KVH, TOK, 256))


def local(*operands):
    sel, recv, other, recvg = forward(SHORT, *operands)
    over = jnp.max(recv[:, SHORT - 1, COLS - 1].astype(F32)) > 0.5
    return lax.cond(
        over,
        lambda: finish(FULL, *forward(FULL, *operands)),
        lambda: finish(SHORT, sel, recv, other, recvg),
    )


def solution(mesh):
    rows = P(("dp", "ctx"), None)
    return jax.shard_map(
        local,
        mesh=mesh,
        in_specs=(rows, rows, rows, rows, P(("dp", "ctx"), None, None), rows, P("dp", None)),
        out_specs=(rows, rows, rows, rows),
        check_vma=False,
    )
```

```python
import functools
import math

import jax
import jax.numpy as jnp
from jax import lax
from jax.experimental import pallas as pl
from jax.experimental.pallas import tpu as pltpu
from jax.sharding import PartitionSpec as P

H = 32
KVH = 8
DH = 128
TOK = 128
CTX = 16
DP = 8
DEV = 128
SEQ = 2048
MOST = 1024
COLS = 384
FULL = 32
SHORT = 24
GROWS = 144
BQ = 256
BK = 256
WMAX = MOST // BK + 1
VMEM_LIMIT = 56 * 2**20

F32 = jnp.float32
BF16 = jnp.bfloat16
MESH = pl.DeviceIdType.MESH


def dot(a, b, ca, cb):
    return lax.dot_general(a, b, (((ca,), (cb,)), ((), ())), preferred_element_type=F32)


def iota(shape, dim):
    return lax.broadcasted_iota(jnp.int32, shape, dim)


def pack_kernel(K, prow, pcol, unp, lengths, q, k, v, g, send, sendg, sel, sel_s, over_s):
    @pl.when(pl.program_id(0) == 0)
    def _():
        occupied = (prow[...] >= 0).astype(BF16)
        a, b = iota((256, 256), 0), iota((256, 256), 1)
        earlier = ((a < b) & (a // 32 == b // 32)).astype(BF16)
        rank = dot(jnp.broadcast_to(occupied, (16, 256)), earlier, 1, 0)[0:1]
        rank = rank.astype(jnp.int32)
        slot = iota((1, 256), 1) // 32 * K + rank
        slot = jnp.where((prow[...] >= 0) & ((rank < K - 1) | (K == FULL)), slot, -1)
        over = jnp.max(jnp.where((prow[...] >= 0) & (rank >= K - 1), 1.0, 0.0), axis=1, keepdims=True)
        last = (iota((8 * K, TOK), 0) % K == K - 1) & (K < FULL)
        over_s[...] = jnp.where(last, over, 0.0)
        place = (iota((8 * K, 256), 0) == slot).astype(BF16)
        holds = (pcol[...] == iota((256, TOK), 1)).astype(BF16)
        value = dot(place, holds, 1, 0).astype(BF16)
        sel_s[...] = value
        sel[...] = value

    s = sel_s[...]
    yq = dot(s, q[...], 1, 0)
    yk = dot(s, k[...], 1, 0)
    yv = dot(s, v[...], 1, 0)
    ykv = (yk + over_s[...], yv + over_s[...])
    for z in range(4):
        for core in range(2):
            for e in range(2):
                rows = slice((2 * z + e) * K, (2 * z + e + 1) * K)
                send[z, core, e, 0, :, 0:256] = yq[rows, core * 256 : (core + 1) * 256].astype(BF16)
                send[z, core, e, 0, :, 256:384] = ykv[core][rows].astype(BF16)
    r = iota((16, TOK), 0)
    spread = (iota((16, TOK), 0) == iota((16, TOK), 1)).astype(BF16)
    sizes = jnp.broadcast_to(lengths[...], (16, 16))
    high = dot((sizes // 8).astype(F32).astype(BF16), spread, 1, 0)
    low = dot((sizes % 8).astype(F32).astype(BF16), spread, 1, 0)
    ints = jnp.where(r < 8, unp[...].astype(F32), jnp.where(r < 12, high, low)).astype(BF16)
    for core in range(2):
        sendg[core, 0, 0:TOK, :] = g[:, core * 256 : (core + 1) * 256]
        sendg[core, 0, TOK:GROWS, 0:TOK] = ints
        sendg[core, 0, TOK:GROWS, TOK:256] = jnp.zeros((16, 128), BF16)


def pack(K, prow, pcol, unp, lengths, q, k, v, g):
    whole = lambda shape: pl.BlockSpec(shape, lambda i: (0,) * len(shape))
    return pl.pallas_call(
        functools.partial(pack_kernel, K),
        grid=(KVH,),
        in_specs=[
            whole((1, 256)),
            whole((256, 1)),
            whole((1, TOK)),
            whole((1, 16)),
            pl.BlockSpec((TOK, 512), lambda i: (0, i)),
            pl.BlockSpec((TOK, 128), lambda i: (0, i)),
            pl.BlockSpec((TOK, 128), lambda i: (0, i)),
            pl.BlockSpec((TOK, 512), lambda i: (0, i)),
        ],
        out_specs=[
            pl.BlockSpec((4, 2, 2, 1, K, COLS), lambda i: (0, 0, 0, i, 0, 0)),
            pl.BlockSpec((2, 1, GROWS, 256), lambda i: (0, i, 0, 0)),
            whole((8 * K, TOK)),
        ],
        out_shape=[
            jax.ShapeDtypeStruct((4, 2, 2, KVH, K, COLS), BF16),
            jax.ShapeDtypeStruct((2, KVH, GROWS, 256), BF16),
            jax.ShapeDtypeStruct((8 * K, TOK), BF16),
        ],
        scratch_shapes=[pltpu.VMEM((8 * K, TOK), BF16), pltpu.VMEM((8 * K, TOK), F32)],
        compiler_params=pltpu.CompilerParams(vmem_limit_bytes=VMEM_LIMIT),
        name="pack_rows_to_messages",
    )(prow, pcol, unp, lengths, q, k, v, g)


def remote(src, dst, send_sem, recv_sem, target):
    return pltpu.make_async_remote_copy(
        src_ref=src,
        dst_ref=dst,
        send_sem=send_sem,
        recv_sem=recv_sem,
        device_id=target,
        device_id_type=MESH,
    )


def place():
    d = lax.axis_index("dp")
    c = lax.axis_index("ctx")
    return d, c, lax.div(d, 2), lax.rem(d, 2)


def partner(n):
    d, c, z, core = place()
    x, y = lax.div(c, 4), lax.rem(c, 4)
    j = lax.rem(n * 37, DEV)
    dy = lax.rem(j, 2) + 2 * lax.rem(lax.div(j, 16), 2)
    dx = lax.rem(lax.div(j, 2), 2) + 2 * lax.rem(lax.div(j, 32), 2)
    dz = lax.rem(lax.div(j, 4), 2) + 2 * lax.div(j, 64)
    dcore = lax.rem(lax.div(j, 8), 2)
    return lax.rem(z + dz, 4) * 2 + lax.rem(core + dcore, 2), lax.rem(x + dx, 4) * 4 + lax.rem(y + dy, 4)


def to_all(src, dst, send_sem, recv_sem, beside=None):
    d, c, _, _ = place()
    me = d * CTX + c

    def one(n):
        td, tc = partner(n)
        remote(src.at[td * CTX + tc], dst.at[me], send_sem, recv_sem, (td, tc)).start()

    def some(n, carry):
        if beside is not None:
            beside(n)
        for i in range(8):
            one(8 * n - 7 + i)
        return carry

    lax.fori_loop(1, CTX, some, 0)
    for n in range(121, DEV):
        one(n)


def wait_all(src, dst, send_sem, recv_sem, count):
    d, c, _, _ = place()
    remote(src.at[pl.ds(0, count)], dst.at[pl.ds(0, count)], send_sem, recv_sem, (d, c)).wait()


def exchange_in_kernel(
    src, srcg, dst, other, dstg,
    send_sem, recv_sem, sendg_sem, recvg_sem, sendo_sem, recvo_sem, own_sem, owng_sem,
):
    d, c, z, core = place()
    me = d * CTX + c
    mine = core == lax.div(c, 8)
    first = core * 8 + lax.rem(c, 8)

    def grads(j):
        target = (2 * z + lax.div(j, 8), core * 8 + lax.rem(j, 8))
        remote(srcg.at[j], dstg.at[c], sendg_sem, recvg_sem, target).start()

    own = pltpu.make_async_copy(src.at[me], dst.at[me], own_sem)
    own.start()
    owng = pltpu.make_async_copy(srcg.at[first], dstg.at[c], owng_sem)

    @pl.when(mine)
    def _():
        owng.start()

    @pl.when(jnp.logical_not(mine))
    def _():
        grads(first)

    to_all(src, dst, send_sem, recv_sem, lambda n: grads(lax.rem(first + lax.rem(n * 5, CTX), CTX)))
    own.wait()
    wait_all(src, dst, send_sem, recv_sem, DEV - 1)
    swap = remote(dst.at[:, :, pl.ds(256, 128)], other, sendo_sem, recvo_sem, (2 * z + 1 - core, c))
    swap.start()

    @pl.when(mine)
    def _():
        owng.wait()
        wait_all(srcg, dstg, sendg_sem, recvg_sem, CTX - 1)

    @pl.when(jnp.logical_not(mine))
    def _():
        wait_all(srcg, dstg, sendg_sem, recvg_sem, CTX)

    swap.wait()


def exchange_in(src, srcg):
    anywhere = pl.BlockSpec(memory_space=pl.ANY)
    return pl.pallas_call(
        exchange_in_kernel,
        in_specs=[anywhere] * 2,
        out_specs=[anywhere] * 3,
        out_shape=[
            jax.ShapeDtypeStruct(src.shape, BF16),
            jax.ShapeDtypeStruct(src.shape[:2] + (128,), BF16),
            jax.ShapeDtypeStruct(srcg.shape, BF16),
        ],
        scratch_shapes=[pltpu.SemaphoreType.DMA] * 8,
        compiler_params=pltpu.CompilerParams(has_side_effects=True),
        name="exchange_in",
    )(src, srcg)


def exchange_out_kernel(
    src, keep, give, srcg, dst, dstkv, dstg,
    other, total,
    send_sem, recv_sem, sendk_sem, recvk_sem, sendg_sem, recvg_sem, sendo_sem, recvo_sem,
    own_sem, ownk_sem, owng_sem,
):
    d, c, z, core = place()
    me = d * CTX + c
    e = lax.div(c, 8)
    mine = core == e
    slot = core * 8 + lax.rem(c, 8)

    def grads(j):
        remote(srcg.at[j], dstg.at[slot], sendg_sem, recvg_sem, (2 * z + e, j)).start()

    swap = remote(give, other, sendo_sem, recvo_sem, (2 * z + 1 - core, c))
    swap.start()
    own = pltpu.make_async_copy(src.at[me], dst.at[me], own_sem)
    own.start()
    owng = pltpu.make_async_copy(srcg.at[c], dstg.at[slot], owng_sem)

    @pl.when(mine)
    def _():
        owng.start()

    @pl.when(jnp.logical_not(mine))
    def _():
        grads(c)

    to_all(src, dst, send_sem, recv_sem, lambda n: grads(lax.rem(c + lax.rem(n * 5, CTX), CTX)))
    swap.wait()
    total[...] = (keep[...].astype(F32) + other[...].astype(F32)).astype(BF16)
    ownk = pltpu.make_async_copy(total.at[me], dstkv.at[me], ownk_sem)
    ownk.start()
    to_all(total, dstkv, sendk_sem, recvk_sem)
    own.wait()
    ownk.wait()

    @pl.when(mine)
    def _():
        owng.wait()
        wait_all(srcg, dstg, sendg_sem, recvg_sem, CTX - 1)

    @pl.when(jnp.logical_not(mine))
    def _():
        wait_all(srcg, dstg, sendg_sem, recvg_sem, CTX)

    wait_all(src, dst, send_sem, recv_sem, DEV - 1)
    wait_all(total, dstkv, sendk_sem, recvk_sem, DEV - 1)


def exchange_out(src, keep, give, srcg):
    anywhere = pl.BlockSpec(memory_space=pl.ANY)
    return pl.pallas_call(
        exchange_out_kernel,
        in_specs=[anywhere, pl.BlockSpec(memory_space=pltpu.VMEM), anywhere, anywhere],
        out_specs=[anywhere] * 3,
        out_shape=[
            jax.ShapeDtypeStruct(src.shape, BF16),
            jax.ShapeDtypeStruct(keep.shape, BF16),
            jax.ShapeDtypeStruct(srcg.shape, BF16),
        ],
        scratch_shapes=[pltpu.VMEM(keep.shape, BF16)] * 2 + [pltpu.SemaphoreType.DMA] * 11,
        compiler_params=pltpu.CompilerParams(has_side_effects=True, vmem_limit_bytes=VMEM_LIMIT),
        name="exchange_out",
    )(src, keep, give, srcg)


def attention_kernel(
    K, recv, other, recvg, att, back, keep, give, x, keyt, valuet, xo, mid, dk, dv, col, lengths
):
    scale = 1.0 / math.sqrt(DH)
    first_core = lax.rem(lax.axis_index("dp"), 2) == 0
    sizes = recvg[0, TOK:GROWS, 0:TOK].astype(F32)
    sizes = (sizes[8:9] * 8 + sizes[12:13]).astype(jnp.int32)
    for n in range(16):
        lengths[n] = jnp.sum(jnp.where(iota((1, TOK), 1) == n, sizes, 0))

    def slots_of(c):
        row = recvg[c, TOK : TOK + 8, 0:TOK].astype(F32)[0:1]
        return (iota((256, TOK), 0).astype(F32) == row).astype(BF16)

    occ = jnp.zeros((256, 128), F32)
    for c in range(CTX):
        occ = occ + dot(slots_of(c), (iota((TOK, 128), 1) == c).astype(BF16), 1, 0)
    pair = (iota((256, 256), 0) // 2 == iota((256, 256), 1) // 2).astype(BF16)
    count = dot(pair, occ.astype(BF16), 1, 0)
    before = (iota((128, 128), 0) < iota((128, 128), 1)).astype(BF16)
    base = dot(count.astype(BF16), before, 1, 0)
    u = iota((256, 128), 0)
    col[...] = base + (u % 2 + (u // 2) % 8 * K).astype(F32)

    own_c = iota((256, 128), 0) // 16 == iota((256, 128), 1)

    def compact_slot(grp):
        tab = col[pl.ds(pl.multiple_of(grp * 16, 16), 16), :]
        return jnp.where(own_c, jnp.concatenate([tab] * CTX, axis=0), 0.0).astype(BF16)

    def sort_senders(grp, carry):
        r0 = pl.multiple_of(grp * 16, 16)
        slot = dot(compact_slot(grp), jnp.ones((128, 8 * K), BF16), 1, 0)
        t = (slot == iota((256, 8 * K), 1).astype(F32)).astype(BF16)
        rows = dot(t, recv[grp], 1, 0).astype(BF16)
        rows2 = dot(t, other[grp], 1, 0).astype(BF16)
        for c in range(CTX):
            mid[c, pl.ds(r0, 16), 0:384] = rows[c * 16 : (c + 1) * 16]
            mid[c, pl.ds(r0, 16), 384:512] = rows2[c * 16 : (c + 1) * 16]
        return carry

    lax.fori_loop(0, 16, sort_senders, 0, unroll=4)

    def sort_rows(c, carry):
        y = dot(slots_of(c), mid[c], 0, 0)
        r = pl.ds(pl.multiple_of(c * TOK, TOK), TOK)
        keys = jnp.where(first_core, y[:, 256:384], y[:, 384:512])
        values = jnp.where(first_core, y[:, 384:512], y[:, 256:384])
        x[r, 0:256] = y[:, 0:256].astype(BF16)
        x[r, 256:384] = keys.astype(BF16)
        x[r, 384:512] = values.astype(BF16)
        keyt[:, r] = keys.T.astype(BF16)
        valuet[:, r] = values.T.astype(BF16)
        return carry

    lax.fori_loop(0, CTX, sort_rows, 0, unroll=4)

    dk[...] = jnp.zeros_like(dk)
    dv[...] = jnp.zeros_like(dv)

    def doc_start(position):
        start, end = jnp.zeros_like(position), jnp.int32(0)
        for n in range(16):
            start = jnp.where(end <= position, end, start)
            end = end + lengths[n]
        return start

    def tile(i, carry):
        q0 = pl.multiple_of(i * BQ, BQ)
        lo = doc_start(q0) // BK
        width = i - lo + 1

        def attend(w):
            k0 = pl.multiple_of(lo * BK, BK)
            span = pl.ds(k0, w * BK)
            here = pl.ds(q0, BQ)
            chunks = [pl.ds(pl.multiple_of(k0 + t * BK, BK), BK) for t in range(w)]
            qpos = q0 + iota((1, BQ), 1)
            qstart = doc_start(qpos)

            def scores(h):
                queries = x[here, h * 128 : (h + 1) * 128]
                out = []
                for t in range(w):
                    kpos = k0 + t * BK + iota((BK, BQ), 0)
                    seen = kpos >= qstart
                    if t == w - 1:
                        seen = seen & (kpos <= qpos)
                    out.append(jnp.where(seen, dot(x[chunks[t], 256:384], queries, 1, 1), -1e30))
                return out

            def grads_of(h):
                return jnp.concatenate(
                    [recvg[2 * i + n, 0:TOK, h * 128 : (h + 1) * 128] for n in range(2)], axis=0
                )

            def probs(s):
                top = functools.reduce(jnp.maximum, [jnp.max(a, axis=0, keepdims=True) for a in s])
                e = [jnp.exp2((a - top) * (scale * math.log2(math.e))) for a in s]
                total = functools.reduce(jnp.add, [jnp.sum(a, axis=0, keepdims=True) for a in e])
                inverse = 1.0 / total
                return [a * inverse for a in e]

            def attend_values(h, p, grads):
                low = jnp.concatenate([a.astype(BF16) for a in p], axis=0)
                outt = dot(valuet[:, span], low, 1, 0).astype(BF16)
                out = outt.astype(F32).T.astype(BF16)
                for n in range(2):
                    att[2 * i + n, :, h * 128 : (h + 1) * 128] = out[n * TOK : (n + 1) * TOK]
                delta = jnp.sum(grads.astype(F32).T * outt.astype(F32), axis=0, keepdims=True)
                return low, delta

            def dprobs(grads):
                return [dot(x[r, 384:512], grads, 1, 1) for r in chunks]

            def dscores(p, dp, delta):
                return jnp.concatenate(
                    [(a * (b - delta) * scale).astype(BF16) for a, b in zip(p, dp)], axis=0
                )

            def query_grads(h, ds):
                xo[here, h * 128 : (h + 1) * 128] = dot(keyt[:, span], ds, 1, 0).T.astype(BF16)

            ga, gb = grads_of(0), grads_of(1)
            sa = scores(0)
            sb = scores(1)
            pa = probs(sa)
            dpa = dprobs(ga)
            pb = probs(sb)
            lowa, deltaa = attend_values(0, pa, ga)
            dpb = dprobs(gb)
            dsa = dscores(pa, dpa, deltaa)
            lowb, deltab = attend_values(1, pb, gb)
            query_grads(0, dsa)
            dsb = dscores(pb, dpb, deltab)
            query_grads(1, dsb)
            dv[span, :] += dot(lowa, ga, 1, 0) + dot(lowb, gb, 1, 0)
            dk[span, :] += dot(dsa, x[here, 0:128], 1, 0) + dot(dsb, x[here, 128:256], 1, 0)

        for w in range(1, WMAX + 1):
            pl.when(width == w)(functools.partial(attend, w))
        return carry

    lax.fori_loop(0, SEQ // BQ, tile, 0)
    xo[:, 256:384] = jnp.where(first_core, dk[...], dv[...]).astype(BF16)
    xo[:, 384:512] = jnp.where(first_core, dv[...], dk[...]).astype(BF16)

    def unsort_rows(c, carry):
        mid[c] = dot(
            slots_of(c), xo[pl.ds(pl.multiple_of(c * TOK, TOK), TOK), :], 1, 0
        ).astype(BF16)
        return carry

    lax.fori_loop(0, CTX, unsort_rows, 0, unroll=4)

    def unsort_senders(grp, carry):
        r0 = pl.multiple_of(grp * 16, 16)
        rows = jnp.concatenate([mid[c, pl.ds(r0, 16), :] for c in range(CTX)], axis=0)
        slot = dot(jnp.ones((8 * K, 128), BF16), compact_slot(grp), 1, 1)
        t = (slot == iota((8 * K, 256), 0).astype(F32)).astype(BF16)
        out = dot(t, rows, 1, 0).astype(BF16)
        back[grp] = out[:, 0:256]
        keep[grp] = out[:, 256:384]
        give[grp] = out[:, 384:512]
        return carry

    lax.fori_loop(0, 16, unsort_senders, 0, unroll=4)


def attention(K, recv, other, recvg):
    vmem = pl.BlockSpec(memory_space=pltpu.VMEM)
    return pl.pallas_call(
        functools.partial(attention_kernel, K),
        in_specs=[vmem] * 3,
        out_specs=[vmem] * 4,
        out_shape=[
            jax.ShapeDtypeStruct((CTX, TOK, 256), BF16),
            jax.ShapeDtypeStruct((16, 8 * K, 256), BF16),
            jax.ShapeDtypeStruct((16, 8 * K, 128), BF16),
            jax.ShapeDtypeStruct((16, 8 * K, 128), BF16),
        ],
        scratch_shapes=[
            pltpu.VMEM((SEQ, 512), BF16),
            pltpu.VMEM((DH, SEQ), BF16),
            pltpu.VMEM((DH, SEQ), BF16),
            pltpu.VMEM((SEQ, 512), BF16),
            pltpu.VMEM((CTX, 256, 512), BF16),
            pltpu.VMEM((SEQ, DH), F32),
            pltpu.VMEM((SEQ, DH), F32),
            pltpu.VMEM((256, 128), F32),
            pltpu.SMEM((16,), jnp.int32),
        ],
        compiler_params=pltpu.CompilerParams(vmem_limit_bytes=VMEM_LIMIT),
        name="attention",
    )(recv, other, recvg)


def unpack_kernel(K, sel, back, backkv, att, attended, gq, gk, gv):
    s = sel[...]
    by_sequence = [(z, e) for z in range(4) for e in range(2)]
    for core, out in ((0, gk), (1, gv)):
        cols = slice(core * 256, (core + 1) * 256)
        attended[:, cols] = att[core, 0]
        rows = [back[z, core, e, 0].astype(F32) for z, e in by_sequence]
        gq[:, cols] = dot(s, jnp.concatenate(rows, axis=0).astype(BF16), 0, 0).astype(BF16)
        rows = [backkv[z, core, e, 0].astype(F32) for z, e in by_sequence]
        out[...] = dot(s, jnp.concatenate(rows, axis=0).astype(BF16), 0, 0).astype(BF16)


def unpack_rows(K, sel, back, backkv, att):
    return pl.pallas_call(
        functools.partial(unpack_kernel, K),
        grid=(KVH,),
        in_specs=[
            pl.BlockSpec((8 * K, TOK), lambda i: (0, 0)),
            pl.BlockSpec((4, 2, 2, 1, K, 256), lambda i: (0, 0, 0, i, 0, 0)),
            pl.BlockSpec((4, 2, 2, 1, K, 128), lambda i: (0, 0, 0, i, 0, 0)),
            pl.BlockSpec((2, 1, TOK, 256), lambda i: (0, i, 0, 0)),
        ],
        out_specs=[
            pl.BlockSpec((TOK, 512), lambda i: (0, i)),
            pl.BlockSpec((TOK, 512), lambda i: (0, i)),
            pl.BlockSpec((TOK, 128), lambda i: (0, i)),
            pl.BlockSpec((TOK, 128), lambda i: (0, i)),
        ],
        out_shape=[
            jax.ShapeDtypeStruct((TOK, H * DH), BF16),
            jax.ShapeDtypeStruct((TOK, H * DH), BF16),
            jax.ShapeDtypeStruct((TOK, KVH * DH), BF16),
            jax.ShapeDtypeStruct((TOK, KVH * DH), BF16),
        ],
        compiler_params=pltpu.CompilerParams(vmem_limit_bytes=VMEM_LIMIT),
        name="messages_to_rows",
    )(sel, back, backkv, att)


def forward(K, q_load, k_load, v_load, grad_out, pack_rows, unpack, doc_lengths):
    flat = pack_rows.reshape(1, 2 * DEV)
    send, sendg, sel = pack(
        K, flat, flat.reshape(2 * DEV, 1), unpack, doc_lengths, q_load, k_load, v_load, grad_out
    )
    return sel, *exchange_in(send.reshape(DEV, K, COLS), sendg.reshape(CTX, GROWS, 256))


def finish(K, sel, recv, other, recvg):
    recv, other = (a.reshape(16, 8 * K, -1) for a in (recv, other))
    att, *parts = attention(K, recv, other, recvg)
    back, keep, give = (a.reshape(DEV, K, -1) for a in parts)
    returned, returnedkv, turned = exchange_out(back, keep, give, att)
    returned, returnedkv = (a.reshape(4, 2, 2, KVH, K, -1) for a in (returned, returnedkv))
    return unpack_rows(K, sel, returned, returnedkv, turned.reshape(2, KVH, TOK, 256))


def local(*operands):
    sel, recv, other, recvg = forward(SHORT, *operands)
    over = jnp.max(recv[:, SHORT - 1, COLS - 1].astype(F32)) > 0.5
    return lax.cond(
        over,
        lambda: finish(FULL, *forward(FULL, *operands)),
        lambda: finish(SHORT, sel, recv, other, recvg),
    )


def solution(mesh):
    rows = P(("dp", "ctx"), None)
    return jax.shard_map(
        local,
        mesh=mesh,
        in_specs=(rows, rows, rows, rows, P(("dp", "ctx"), None, None), rows, P("dp", None)),
        out_specs=(rows, rows, rows, rows),
        check_vma=False,
    )
```

```python
import functools
import math

import jax
import jax.numpy as jnp
from jax import lax
from jax.experimental import pallas as pl
from jax.experimental.pallas import tpu as pltpu
from jax.sharding import PartitionSpec as P

H = 32
KVH = 8
DH = 128
TOK = 128
CTX = 16
DP = 8
DEV = 128
SEQ = 2048
MOST = 1024
COLS = 384
FULL = 32
SHORT = 24
GROWS = 144
BQ = 256
BK = 256
WMAX = MOST // BK + 1
VMEM_LIMIT = 56 * 2**20

F32 = jnp.float32
BF16 = jnp.bfloat16
MESH = pl.DeviceIdType.MESH


def dot(a, b, ca, cb):
    return lax.dot_general(a, b, (((ca,), (cb,)), ((), ())), preferred_element_type=F32)


def iota(shape, dim):
    return lax.broadcasted_iota(jnp.int32, shape, dim)


def remote(src, dst, send_sem, recv_sem, target):
    return pltpu.make_async_remote_copy(
        src_ref=src,
        dst_ref=dst,
        send_sem=send_sem,
        recv_sem=recv_sem,
        device_id=target,
        device_id_type=MESH,
    )


def place():
    d = lax.axis_index("dp")
    c = lax.axis_index("ctx")
    return d, c, lax.div(d, 2), lax.rem(d, 2)


def partner(n):
    d, c, z, core = place()
    x, y = lax.div(c, 4), lax.rem(c, 4)
    j = lax.rem(n * 37, DEV)
    dy = lax.rem(j, 2) + 2 * lax.rem(lax.div(j, 16), 2)
    dx = lax.rem(lax.div(j, 2), 2) + 2 * lax.rem(lax.div(j, 32), 2)
    dz = lax.rem(lax.div(j, 4), 2) + 2 * lax.div(j, 64)
    dcore = lax.rem(lax.div(j, 8), 2)
    return lax.rem(z + dz, 4) * 2 + lax.rem(core + dcore, 2), lax.rem(x + dx, 4) * 4 + lax.rem(y + dy, 4)


def to_all(src, dst, send_sem, recv_sem, beside=None):
    d, c, _, _ = place()
    me = d * CTX + c

    def one(n):
        td, tc = partner(n)
        remote(src.at[td * CTX + tc], dst.at[me], send_sem, recv_sem, (td, tc)).start()

    def some(n, carry):
        if beside is not None:
            beside(n)
        for i in range(8):
            one(8 * n - 7 + i)
        return carry

    lax.fori_loop(1, CTX, some, 0)
    for n in range(121, DEV):
        one(n)


def greet_all():
    barrier = pltpu.get_barrier_semaphore()

    def greet(n, carry):
        pl.semaphore_signal(barrier, inc=1, device_id=partner(n), device_id_type=MESH)
        return carry

    lax.fori_loop(1, DEV, greet, 0)
    return lambda: pl.semaphore_wait(barrier, DEV - 1)


def wait_all(src, dst, send_sem, recv_sem, count):
    d, c, _, _ = place()
    remote(src.at[pl.ds(0, count)], dst.at[pl.ds(0, count)], send_sem, recv_sem, (d, c)).wait()


def exchange_in_kernel(
    K, slots, unp, lengths, q, k, v, g, dst, other, dstg, sel,
    send, sendg, over_s,
    send_sem, recv_sem, sendg_sem, recvg_sem, sendo_sem, recvo_sem, own_sem, owng_sem,
):
    d, c, z, core = place()
    me = d * CTX + c
    mine = core == lax.div(c, 8)
    first = core * 8 + lax.rem(c, 8)
    all_here = greet_all()

    r = iota((16, TOK), 0)
    spread = (r == iota((16, TOK), 1)).astype(BF16)
    sizes = jnp.broadcast_to(lengths[...], (16, 16))
    high = dot((sizes // 8).astype(F32).astype(BF16), spread, 1, 0)
    low = dot((sizes % 8).astype(F32).astype(BF16), spread, 1, 0)
    ints = jnp.where(r < 8, unp[...].astype(F32), jnp.where(r < 12, high, low)).astype(BF16)
    for h in range(KVH):
        for p in range(2):
            sendg[p * 8 + h, 0:TOK, :] = g[:, h * 512 + p * 256 : h * 512 + (p + 1) * 256]
            sendg[p * 8 + h, TOK:GROWS, 0:TOK] = ints
            sendg[p * 8 + h, TOK:GROWS, TOK:256] = jnp.zeros((16, 128), BF16)

    all_here()

    def grads(j):
        target = (2 * z + lax.div(j, 8), core * 8 + lax.rem(j, 8))
        remote(sendg.at[j], dstg.at[c], sendg_sem, recvg_sem, target).start()

    owng = pltpu.make_async_copy(sendg.at[first], dstg.at[c], owng_sem)

    @pl.when(mine)
    def _():
        owng.start()

    @pl.when(jnp.logical_not(mine))
    def _():
        grads(first)

    def turn(n, carry):
        grads(lax.rem(first + lax.rem(n * 5, CTX), CTX))
        return carry

    lax.fori_loop(1, CTX, turn, 0)

    occupied = slots[...] >= 0
    count = jnp.where(occupied[0:1], 1.0, 0.0) + jnp.where(occupied[1:2], 1.0, 0.0)
    a, b = iota((DEV, DEV), 0), iota((DEV, DEV), 1)
    earlier = ((a < b) & (a // CTX == b // CTX)).astype(BF16)
    base = dot(jnp.broadcast_to(count, (16, DEV)).astype(BF16), earlier, 1, 0)[0:1].astype(jnp.int32)
    rows_of = jnp.concatenate([slots[...].astype(F32), jnp.zeros((126, DEV), F32)], axis=0).T
    value = jnp.zeros((8 * K, TOK), F32)
    over = jnp.zeros((1, 1), F32)
    for j in range(2):
        rank = base + j
        kept = occupied[j : j + 1]
        if K < FULL:
            lost = jnp.where(kept & (rank >= K - 1), 1.0, 0.0)
            over = jnp.maximum(over, jnp.max(lost, axis=1, keepdims=True))
            kept = kept & (rank < K - 1)
        slot = jnp.where(kept, iota((1, DEV), 1) // CTX * K + rank, -1)
        where = (iota((8 * K, DEV), 0) == slot).astype(BF16)
        holds = (rows_of[:, j : j + 1] == iota((DEV, TOK), 1).astype(F32)).astype(BF16)
        value = value + dot(where, holds, 1, 0)
    s = value.astype(BF16)
    sel[...] = s
    last = (iota((8 * K, TOK), 0) % K == K - 1) & (K < FULL)
    over_s[...] = jnp.where(last, over, 0.0)

    def build(h, carry):
        wide = pl.ds(pl.multiple_of(h * 512, 512), 512)
        narrow = pl.ds(pl.multiple_of(h * 128, 128), 128)
        yq = dot(sel[...], q[:, wide], 1, 0)
        yk = dot(sel[...], k[:, narrow], 1, 0) + over_s[...]
        yv = dot(sel[...], v[:, narrow], 1, 0) + over_s[...]
        for n in range(DP):
            rows = slice(n * K, (n + 1) * K)
            for p, ykv in ((0, yk), (1, yv)):
                t = ((n // 2 * 2 + p) * 2 + n % 2) * 8 + h
                send[t, :, 0:256] = yq[rows, p * 256 : (p + 1) * 256].astype(BF16)
                send[t, :, 256:384] = ykv[rows].astype(BF16)
        return carry

    lax.fori_loop(0, KVH, build, 0)

    own = pltpu.make_async_copy(send.at[me], dst.at[me], own_sem)
    own.start()
    to_all(send, dst, send_sem, recv_sem)
    own.wait()
    wait_all(send, dst, send_sem, recv_sem, DEV - 1)
    swap = remote(dst.at[:, :, pl.ds(256, 128)], other, sendo_sem, recvo_sem, (2 * z + 1 - core, c))
    swap.start()

    @pl.when(mine)
    def _():
        owng.wait()
        wait_all(sendg, dstg, sendg_sem, recvg_sem, CTX - 1)

    @pl.when(jnp.logical_not(mine))
    def _():
        wait_all(sendg, dstg, sendg_sem, recvg_sem, CTX)

    swap.wait()


def exchange_in(K, slots, unp, lengths, q, k, v, g):
    anywhere = pl.BlockSpec(memory_space=pl.ANY)
    vmem = pl.BlockSpec(memory_space=pltpu.VMEM)
    return pl.pallas_call(
        functools.partial(exchange_in_kernel, K),
        in_specs=[vmem] * 7,
        out_specs=[anywhere] * 3 + [vmem],
        out_shape=[
            jax.ShapeDtypeStruct((DEV, K, COLS), BF16),
            jax.ShapeDtypeStruct((DEV, K, 128), BF16),
            jax.ShapeDtypeStruct((CTX, GROWS, 256), BF16),
            jax.ShapeDtypeStruct((8 * K, TOK), BF16),
        ],
        scratch_shapes=[
            pltpu.VMEM((DEV, K, COLS), BF16),
            pltpu.VMEM((CTX, GROWS, 256), BF16),
            pltpu.VMEM((8 * K, TOK), F32),
        ]
        + [pltpu.SemaphoreType.DMA] * 8,
        compiler_params=pltpu.CompilerParams(
            has_side_effects=True, vmem_limit_bytes=VMEM_LIMIT, collective_id=K
        ),
        name="exchange_in",
    )(slots, unp, lengths, q, k, v, g)


def exchange_out_kernel(
    src, keep, give, srcg, dst, dstkv, dstg,
    other, total,
    send_sem, recv_sem, sendk_sem, recvk_sem, sendg_sem, recvg_sem, sendo_sem, recvo_sem,
    own_sem, ownk_sem, owng_sem,
):
    d, c, z, core = place()
    me = d * CTX + c
    e = lax.div(c, 8)
    mine = core == e
    slot = core * 8 + lax.rem(c, 8)

    def grads(j):
        remote(srcg.at[j], dstg.at[slot], sendg_sem, recvg_sem, (2 * z + e, j)).start()

    swap = remote(give, other, sendo_sem, recvo_sem, (2 * z + 1 - core, c))
    swap.start()
    own = pltpu.make_async_copy(src.at[me], dst.at[me], own_sem)
    own.start()
    owng = pltpu.make_async_copy(srcg.at[c], dstg.at[slot], owng_sem)

    @pl.when(mine)
    def _():
        owng.start()

    @pl.when(jnp.logical_not(mine))
    def _():
        grads(c)

    to_all(src, dst, send_sem, recv_sem, lambda n: grads(lax.rem(c + lax.rem(n * 5, CTX), CTX)))
    swap.wait()
    total[...] = (keep[...].astype(F32) + other[...].astype(F32)).astype(BF16)
    ownk = pltpu.make_async_copy(total.at[me], dstkv.at[me], ownk_sem)
    ownk.start()
    to_all(total, dstkv, sendk_sem, recvk_sem)
    own.wait()
    ownk.wait()

    @pl.when(mine)
    def _():
        owng.wait()
        wait_all(srcg, dstg, sendg_sem, recvg_sem, CTX - 1)

    @pl.when(jnp.logical_not(mine))
    def _():
        wait_all(srcg, dstg, sendg_sem, recvg_sem, CTX)

    wait_all(src, dst, send_sem, recv_sem, DEV - 1)
    wait_all(total, dstkv, sendk_sem, recvk_sem, DEV - 1)


def exchange_out(src, keep, give, srcg):
    anywhere = pl.BlockSpec(memory_space=pl.ANY)
    return pl.pallas_call(
        exchange_out_kernel,
        in_specs=[anywhere, pl.BlockSpec(memory_space=pltpu.VMEM), anywhere, anywhere],
        out_specs=[anywhere] * 3,
        out_shape=[
            jax.ShapeDtypeStruct(src.shape, BF16),
            jax.ShapeDtypeStruct(keep.shape, BF16),
            jax.ShapeDtypeStruct(srcg.shape, BF16),
        ],
        scratch_shapes=[pltpu.VMEM(keep.shape, BF16)] * 2 + [pltpu.SemaphoreType.DMA] * 11,
        compiler_params=pltpu.CompilerParams(has_side_effects=True, vmem_limit_bytes=VMEM_LIMIT),
        name="exchange_out",
    )(src, keep, give, srcg)


def attention_kernel(
    K, recv, other, recvg, att, back, keep, give, over, x, keyt, valuet, xo, mid, dk, dv, col, lengths
):
    scale = 1.0 / math.sqrt(DH)
    first_core = lax.rem(lax.axis_index("dp"), 2) == 0
    sizes = recvg[0, TOK:GROWS, 0:TOK].astype(F32)
    sizes = (sizes[8:9] * 8 + sizes[12:13]).astype(jnp.int32)
    for n in range(16):
        lengths[n] = jnp.sum(jnp.where(iota((1, TOK), 1) == n, sizes, 0))

    def slots_of(c):
        row = recvg[c, TOK : TOK + 8, 0:TOK].astype(F32)[0:1]
        return (iota((256, TOK), 0).astype(F32) == row).astype(BF16)

    occ = jnp.zeros((256, 128), F32)
    for c in range(CTX):
        occ = occ + dot(slots_of(c), (iota((TOK, 128), 1) == c).astype(BF16), 1, 0)
    pair = (iota((256, 256), 0) // 2 == iota((256, 256), 1) // 2).astype(BF16)
    count = dot(pair, occ.astype(BF16), 1, 0)
    before = (iota((128, 128), 0) < iota((128, 128), 1)).astype(BF16)
    base = dot(count.astype(BF16), before, 1, 0)
    u = iota((256, 128), 0)
    col[...] = base + (u % 2 + (u // 2) % 8 * K).astype(F32)

    most = jnp.zeros((8 * K, DH), F32)
    for grp in range(16):
        most = jnp.maximum(most, recv[grp, :, 256:384].astype(F32))
    flags = (iota((8 * K, DH), 0) % K == K - 1) & (K < FULL)
    over[0] = jnp.max(jnp.where(flags, most, 0.0))

    own_c = iota((256, 128), 0) // 16 == iota((256, 128), 1)

    def compact_slot(grp):
        tab = col[pl.ds(pl.multiple_of(grp * 16, 16), 16), :]
        return jnp.where(own_c, jnp.concatenate([tab] * CTX, axis=0), 0.0).astype(BF16)

    def sort_senders(grp, carry):
        r0 = pl.multiple_of(grp * 16, 16)
        slot = dot(compact_slot(grp), jnp.ones((128, 8 * K), BF16), 1, 0)
        t = (slot == iota((256, 8 * K), 1).astype(F32)).astype(BF16)
        rows = dot(t, recv[grp], 1, 0).astype(BF16)
        rows2 = dot(t, other[grp], 1, 0).astype(BF16)
        for c in range(CTX):
            mid[c, pl.ds(r0, 16), 0:384] = rows[c * 16 : (c + 1) * 16]
            mid[c, pl.ds(r0, 16), 384:512] = rows2[c * 16 : (c + 1) * 16]
        return carry

    lax.fori_loop(0, 16, sort_senders, 0, unroll=4)

    def sort_rows(c, carry):
        y = dot(slots_of(c), mid[c], 0, 0)
        r = pl.ds(pl.multiple_of(c * TOK, TOK), TOK)
        keys = jnp.where(first_core, y[:, 256:384], y[:, 384:512])
        values = jnp.where(first_core, y[:, 384:512], y[:, 256:384])
        x[r, 0:256] = y[:, 0:256].astype(BF16)
        x[r, 256:384] = keys.astype(BF16)
        x[r, 384:512] = values.astype(BF16)
        keyt[:, r] = keys.T.astype(BF16)
        valuet[:, r] = values.T.astype(BF16)
        return carry

    lax.fori_loop(0, CTX, sort_rows, 0, unroll=4)

    dk[...] = jnp.zeros_like(dk)
    dv[...] = jnp.zeros_like(dv)

    def doc_start(position):
        start, end = jnp.zeros_like(position), jnp.int32(0)
        for n in range(16):
            start = jnp.where(end <= position, end, start)
            end = end + lengths[n]
        return start

    def tile(i, carry):
        q0 = pl.multiple_of(i * BQ, BQ)
        lo = doc_start(q0) // BK
        width = i - lo + 1

        def attend(w):
            k0 = pl.multiple_of(lo * BK, BK)
            span = pl.ds(k0, w * BK)
            here = pl.ds(q0, BQ)
            chunks = [pl.ds(pl.multiple_of(k0 + t * BK, BK), BK) for t in range(w)]
            qpos = q0 + iota((1, BQ), 1)
            qstart = doc_start(qpos)

            def scores(h):
                queries = x[here, h * 128 : (h + 1) * 128]
                out = []
                for t in range(w):
                    kpos = k0 + t * BK + iota((BK, BQ), 0)
                    seen = kpos >= qstart
                    if t == w - 1:
                        seen = seen & (kpos <= qpos)
                    out.append(jnp.where(seen, dot(x[chunks[t], 256:384], queries, 1, 1), -1e30))
                return out

            def grads_of(h):
                return jnp.concatenate(
                    [recvg[2 * i + n, 0:TOK, h * 128 : (h + 1) * 128] for n in range(2)], axis=0
                )

            def probs(s):
                top = functools.reduce(jnp.maximum, [jnp.max(a, axis=0, keepdims=True) for a in s])
                e = [jnp.exp2((a - top) * (scale * math.log2(math.e))) for a in s]
                total = functools.reduce(jnp.add, [jnp.sum(a, axis=0, keepdims=True) for a in e])
                inverse = 1.0 / total
                return [a * inverse for a in e]

            def attend_values(h, p, grads):
                low = jnp.concatenate([a.astype(BF16) for a in p], axis=0)
                outt = dot(valuet[:, span], low, 1, 0).astype(BF16)
                out = outt.astype(F32).T.astype(BF16)
                for n in range(2):
                    att[2 * i + n, :, h * 128 : (h + 1) * 128] = out[n * TOK : (n + 1) * TOK]
                delta = jnp.sum(grads.astype(F32).T * outt.astype(F32), axis=0, keepdims=True)
                return low, delta

            def dprobs(grads):
                return [dot(x[r, 384:512], grads, 1, 1) for r in chunks]

            def dscores(p, dp, delta):
                return jnp.concatenate(
                    [(a * (b - delta) * scale).astype(BF16) for a, b in zip(p, dp)], axis=0
                )

            def query_grads(h, ds):
                xo[here, h * 128 : (h + 1) * 128] = dot(keyt[:, span], ds, 1, 0).T.astype(BF16)

            ga, gb = grads_of(0), grads_of(1)
            sa = scores(0)
            sb = scores(1)
            pa = probs(sa)
            dpa = dprobs(ga)
            pb = probs(sb)
            lowa, deltaa = attend_values(0, pa, ga)
            dpb = dprobs(gb)
            dsa = dscores(pa, dpa, deltaa)
            lowb, deltab = attend_values(1, pb, gb)
            query_grads(0, dsa)
            dsb = dscores(pb, dpb, deltab)
            query_grads(1, dsb)
            dv[span, :] += dot(lowa, ga, 1, 0) + dot(lowb, gb, 1, 0)
            dk[span, :] += dot(dsa, x[here, 0:128], 1, 0) + dot(dsb, x[here, 128:256], 1, 0)

        for w in range(1, WMAX + 1):
            pl.when(width == w)(functools.partial(attend, w))
        return carry

    lax.fori_loop(0, SEQ // BQ, tile, 0)
    xo[:, 256:384] = jnp.where(first_core, dk[...], dv[...]).astype(BF16)
    xo[:, 384:512] = jnp.where(first_core, dv[...], dk[...]).astype(BF16)

    def unsort_rows(c, carry):
        mid[c] = dot(
            slots_of(c), xo[pl.ds(pl.multiple_of(c * TOK, TOK), TOK), :], 1, 0
        ).astype(BF16)
        return carry

    lax.fori_loop(0, CTX, unsort_rows, 0, unroll=4)

    def unsort_senders(grp, carry):
        r0 = pl.multiple_of(grp * 16, 16)
        rows = jnp.concatenate([mid[c, pl.ds(r0, 16), :] for c in range(CTX)], axis=0)
        slot = dot(jnp.ones((8 * K, 128), BF16), compact_slot(grp), 1, 1)
        t = (slot == iota((8 * K, 256), 0).astype(F32)).astype(BF16)
        out = dot(t, rows, 1, 0).astype(BF16)
        back[grp] = out[:, 0:256]
        keep[grp] = out[:, 256:384]
        give[grp] = out[:, 384:512]
        return carry

    lax.fori_loop(0, 16, unsort_senders, 0, unroll=4)


def attention(K, recv, other, recvg):
    vmem = pl.BlockSpec(memory_space=pltpu.VMEM)
    return pl.pallas_call(
        functools.partial(attention_kernel, K),
        in_specs=[vmem] * 3,
        out_specs=[vmem] * 4 + [pl.BlockSpec(memory_space=pltpu.SMEM)],
        out_shape=[
            jax.ShapeDtypeStruct((CTX, TOK, 256), BF16),
            jax.ShapeDtypeStruct((16, 8 * K, 256), BF16),
            jax.ShapeDtypeStruct((16, 8 * K, 128), BF16),
            jax.ShapeDtypeStruct((16, 8 * K, 128), BF16),
            jax.ShapeDtypeStruct((1,), F32),
        ],
        scratch_shapes=[
            pltpu.VMEM((SEQ, 512), BF16),
            pltpu.VMEM((DH, SEQ), BF16),
            pltpu.VMEM((DH, SEQ), BF16),
            pltpu.VMEM((SEQ, 512), BF16),
            pltpu.VMEM((CTX, 256, 512), BF16),
            pltpu.VMEM((SEQ, DH), F32),
            pltpu.VMEM((SEQ, DH), F32),
            pltpu.VMEM((256, 128), F32),
            pltpu.SMEM((16,), jnp.int32),
        ],
        compiler_params=pltpu.CompilerParams(vmem_limit_bytes=VMEM_LIMIT),
        name="attention",
    )(recv, other, recvg)


def unpack_kernel(K, sel, back, backkv, att, attended, gq, gk, gv):
    s = sel[...]
    by_sequence = [(z, e) for z in range(4) for e in range(2)]
    for core, out in ((0, gk), (1, gv)):
        cols = slice(core * 256, (core + 1) * 256)
        attended[:, cols] = att[core, 0]
        rows = [back[z, core, e, 0].astype(F32) for z, e in by_sequence]
        gq[:, cols] = dot(s, jnp.concatenate(rows, axis=0).astype(BF16), 0, 0).astype(BF16)
        rows = [backkv[z, core, e, 0].astype(F32) for z, e in by_sequence]
        out[...] = dot(s, jnp.concatenate(rows, axis=0).astype(BF16), 0, 0).astype(BF16)


def unpack_rows(K, sel, back, backkv, att):
    return pl.pallas_call(
        functools.partial(unpack_kernel, K),
        grid=(KVH,),
        in_specs=[
            pl.BlockSpec((8 * K, TOK), lambda i: (0, 0)),
            pl.BlockSpec((4, 2, 2, 1, K, 256), lambda i: (0, 0, 0, i, 0, 0)),
            pl.BlockSpec((4, 2, 2, 1, K, 128), lambda i: (0, 0, 0, i, 0, 0)),
            pl.BlockSpec((2, 1, TOK, 256), lambda i: (0, i, 0, 0)),
        ],
        out_specs=[
            pl.BlockSpec((TOK, 512), lambda i: (0, i)),
            pl.BlockSpec((TOK, 512), lambda i: (0, i)),
            pl.BlockSpec((TOK, 128), lambda i: (0, i)),
            pl.BlockSpec((TOK, 128), lambda i: (0, i)),
        ],
        out_shape=[
            jax.ShapeDtypeStruct((TOK, H * DH), BF16),
            jax.ShapeDtypeStruct((TOK, H * DH), BF16),
            jax.ShapeDtypeStruct((TOK, KVH * DH), BF16),
            jax.ShapeDtypeStruct((TOK, KVH * DH), BF16),
        ],
        compiler_params=pltpu.CompilerParams(vmem_limit_bytes=VMEM_LIMIT),
        name="messages_to_rows",
    )(sel, back, backkv, att)


def middle(K, q_load, k_load, v_load, grad_out, pack_rows, unpack, doc_lengths):
    recv, other, recvg, sel = exchange_in(
        K, pack_rows[0].T, unpack, doc_lengths, q_load, k_load, v_load, grad_out
    )
    recv, other = (a.reshape(16, 8 * K, -1) for a in (recv, other))
    *parts, over = attention(K, recv, other, recvg)
    return over[0] > 0.5, (sel, *parts)


def finish(K, sel, att, back, keep, give):
    back, keep, give = (a.reshape(DEV, K, -1) for a in (back, keep, give))
    returned, returnedkv, turned = exchange_out(back, keep, give, att)
    returned, returnedkv = (a.reshape(4, 2, 2, KVH, K, -1) for a in (returned, returnedkv))
    return unpack_rows(K, sel, returned, returnedkv, turned.reshape(2, KVH, TOK, 256))


def local(*operands):
    over, parts = middle(SHORT, *operands)
    return lax.cond(
        over,
        lambda: finish(FULL, *middle(FULL, *operands)[1]),
        lambda: finish(SHORT, *parts),
    )


def solution(mesh):
    rows = P(("dp", "ctx"), None)
    return jax.shard_map(
        local,
        mesh=mesh,
        in_specs=(rows, rows, rows, rows, P(("dp", "ctx"), None, None), rows, P("dp", None)),
        out_specs=(rows, rows, rows, rows),
        check_vma=False,
    )
```

```python
import functools
import math

import jax
import jax.numpy as jnp
from jax import lax
from jax.experimental import pallas as pl
from jax.experimental.pallas import tpu as pltpu
from jax.sharding import PartitionSpec as P

H = 32
KVH = 8
DH = 128
TOK = 128
CTX = 16
DP = 8
DEV = 128
SEQ = 2048
MOST = 1024
COLS = 384
FULL = 32
SHORT = 24
GROWS = 144
BQ = 256
BK = 256
WMAX = MOST // BK + 1
VMEM_LIMIT = 56 * 2**20

F32 = jnp.float32
BF16 = jnp.bfloat16
MESH = pl.DeviceIdType.MESH


def dot(a, b, ca, cb):
    return lax.dot_general(a, b, (((ca,), (cb,)), ((), ())), preferred_element_type=F32)


def iota(shape, dim):
    return lax.broadcasted_iota(jnp.int32, shape, dim)


def remote(src, dst, send_sem, recv_sem, target):
    return pltpu.make_async_remote_copy(
        src_ref=src,
        dst_ref=dst,
        send_sem=send_sem,
        recv_sem=recv_sem,
        device_id=target,
        device_id_type=MESH,
    )


def row_slots(row):
    return (iota((256, TOK), 0).astype(F32) == row).astype(BF16)


def compact_slot(col, grp):
    tab = col[pl.ds(pl.multiple_of(grp * 16, 16), 16), :]
    own_c = iota((256, 128), 0) // 16 == iota((256, 128), 1)
    return jnp.where(own_c, jnp.concatenate([tab] * CTX, axis=0), 0.0).astype(BF16)


def place():
    d = lax.axis_index("dp")
    c = lax.axis_index("ctx")
    return d, c, lax.div(d, 2), lax.rem(d, 2)


def partner(n):
    d, c, z, core = place()
    x, y = lax.div(c, 4), lax.rem(c, 4)
    j = lax.rem(n * 37, DEV)
    dy = lax.rem(j, 2) + 2 * lax.rem(lax.div(j, 16), 2)
    dx = lax.rem(lax.div(j, 2), 2) + 2 * lax.rem(lax.div(j, 32), 2)
    dz = lax.rem(lax.div(j, 4), 2) + 2 * lax.div(j, 64)
    dcore = lax.rem(lax.div(j, 8), 2)
    return lax.rem(z + dz, 4) * 2 + lax.rem(core + dcore, 2), lax.rem(x + dx, 4) * 4 + lax.rem(y + dy, 4)


def to_all(src, dst, send_sem, recv_sem):
    d, c, _, _ = place()
    me = d * CTX + c

    def one(n):
        td, tc = partner(n)
        remote(src.at[td * CTX + tc], dst.at[me], send_sem, recv_sem, (td, tc)).start()

    def some(n, carry):
        for i in range(8):
            one(8 * n - 7 + i)
        return carry

    lax.fori_loop(1, CTX, some, 0)
    for n in range(121, DEV):
        one(n)


def greet_all():
    barrier = pltpu.get_barrier_semaphore()

    def greet(n, carry):
        pl.semaphore_signal(barrier, inc=1, device_id=partner(n), device_id_type=MESH)
        return carry

    lax.fori_loop(1, DEV, greet, 0)
    return lambda: pl.semaphore_wait(barrier, DEV - 1)


def wait_all(src, dst, send_sem, recv_sem, count):
    d, c, _, _ = place()
    remote(src.at[pl.ds(0, count)], dst.at[pl.ds(0, count)], send_sem, recv_sem, (d, c)).wait()


def exchange_in_kernel(
    K, slots, unp, lengths, q, k, v, g, dst, other, dstg, sel,
    send, sendg, over_s,
    send_sem, recv_sem, sendg_sem, recvg_sem, sendo_sem, recvo_sem, own_sem, owng_sem,
):
    d, c, z, core = place()
    me = d * CTX + c
    mine = core == lax.div(c, 8)
    first = core * 8 + lax.rem(c, 8)
    all_here = greet_all()

    r = iota((16, TOK), 0)
    spread = (r == iota((16, TOK), 1)).astype(BF16)
    sizes = jnp.broadcast_to(lengths[...], (16, 16))
    high = dot((sizes // 8).astype(F32).astype(BF16), spread, 1, 0)
    low = dot((sizes % 8).astype(F32).astype(BF16), spread, 1, 0)
    ints = jnp.where(r < 8, unp[...].astype(F32), jnp.where(r < 12, high, low)).astype(BF16)
    for h in range(KVH):
        for p in range(2):
            sendg[p * 8 + h, 0:TOK, :] = g[:, h * 512 + p * 256 : h * 512 + (p + 1) * 256]
            sendg[p * 8 + h, TOK:GROWS, 0:TOK] = ints
            sendg[p * 8 + h, TOK:GROWS, TOK:256] = jnp.zeros((16, 128), BF16)

    all_here()

    def grads(j):
        target = (2 * z + lax.div(j, 8), core * 8 + lax.rem(j, 8))
        remote(sendg.at[j], dstg.at[c], sendg_sem, recvg_sem, target).start()

    owng = pltpu.make_async_copy(sendg.at[first], dstg.at[c], owng_sem)

    @pl.when(mine)
    def _():
        owng.start()

    @pl.when(jnp.logical_not(mine))
    def _():
        grads(first)

    def turn(n, carry):
        grads(lax.rem(first + lax.rem(n * 5, CTX), CTX))
        return carry

    lax.fori_loop(1, CTX, turn, 0)

    occupied = slots[...] >= 0
    count = jnp.where(occupied[0:1], 1.0, 0.0) + jnp.where(occupied[1:2], 1.0, 0.0)
    a, b = iota((DEV, DEV), 0), iota((DEV, DEV), 1)
    earlier = ((a < b) & (a // CTX == b // CTX)).astype(BF16)
    base = dot(jnp.broadcast_to(count, (16, DEV)).astype(BF16), earlier, 1, 0)[0:1].astype(jnp.int32)
    rows_of = jnp.concatenate([slots[...].astype(F32), jnp.zeros((126, DEV), F32)], axis=0).T
    value = jnp.zeros((8 * K, TOK), F32)
    over = jnp.zeros((1, 1), F32)
    for j in range(2):
        rank = base + j
        kept = occupied[j : j + 1]
        if K < FULL:
            lost = jnp.where(kept & (rank >= K - 1), 1.0, 0.0)
            over = jnp.maximum(over, jnp.max(lost, axis=1, keepdims=True))
            kept = kept & (rank < K - 1)
        slot = jnp.where(kept, iota((1, DEV), 1) // CTX * K + rank, -1)
        where = (iota((8 * K, DEV), 0) == slot).astype(BF16)
        holds = (rows_of[:, j : j + 1] == iota((DEV, TOK), 1).astype(F32)).astype(BF16)
        value = value + dot(where, holds, 1, 0)
    s = value.astype(BF16)
    sel[...] = s
    last = (iota((8 * K, TOK), 0) % K == K - 1) & (K < FULL)
    over_s[...] = jnp.where(last, over, 0.0)

    def build(h, carry):
        wide = pl.ds(pl.multiple_of(h * 512, 512), 512)
        narrow = pl.ds(pl.multiple_of(h * 128, 128), 128)
        yq = dot(sel[...], q[:, wide], 1, 0)
        yk = dot(sel[...], k[:, narrow], 1, 0) + over_s[...]
        yv = dot(sel[...], v[:, narrow], 1, 0) + over_s[...]
        for n in range(DP):
            rows = slice(n * K, (n + 1) * K)
            for p, ykv in ((0, yk), (1, yv)):
                t = ((n // 2 * 2 + p) * 2 + n % 2) * 8 + h
                send[t, :, 0:256] = yq[rows, p * 256 : (p + 1) * 256].astype(BF16)
                send[t, :, 256:384] = ykv[rows].astype(BF16)
        return carry

    lax.fori_loop(0, KVH, build, 0)

    own = pltpu.make_async_copy(send.at[me], dst.at[me], own_sem)
    own.start()
    to_all(send, dst, send_sem, recv_sem)
    own.wait()
    wait_all(send, dst, send_sem, recv_sem, DEV - 1)
    swap = remote(dst.at[:, :, pl.ds(256, 128)], other, sendo_sem, recvo_sem, (2 * z + 1 - core, c))
    swap.start()

    @pl.when(mine)
    def _():
        owng.wait()
        wait_all(sendg, dstg, sendg_sem, recvg_sem, CTX - 1)

    @pl.when(jnp.logical_not(mine))
    def _():
        wait_all(sendg, dstg, sendg_sem, recvg_sem, CTX)

    swap.wait()


def exchange_in(K, slots, unp, lengths, q, k, v, g):
    anywhere = pl.BlockSpec(memory_space=pl.ANY)
    vmem = pl.BlockSpec(memory_space=pltpu.VMEM)
    return pl.pallas_call(
        functools.partial(exchange_in_kernel, K),
        in_specs=[vmem] * 7,
        out_specs=[anywhere] * 3 + [vmem],
        out_shape=[
            jax.ShapeDtypeStruct((DEV, K, COLS), BF16),
            jax.ShapeDtypeStruct((DEV, K, 128), BF16),
            jax.ShapeDtypeStruct((CTX, GROWS, 256), BF16),
            jax.ShapeDtypeStruct((8 * K, TOK), BF16),
        ],
        scratch_shapes=[
            pltpu.VMEM((DEV, K, COLS), BF16),
            pltpu.VMEM((CTX, GROWS, 256), BF16),
            pltpu.VMEM((8 * K, TOK), F32),
        ]
        + [pltpu.SemaphoreType.DMA] * 8,
        compiler_params=pltpu.CompilerParams(
            has_side_effects=True, vmem_limit_bytes=VMEM_LIMIT, collective_id=K
        ),
        name="exchange_in",
    )(slots, unp, lengths, q, k, v, g)


def exchange_out_kernel(
    K, rows_in, col, unp, srcg, dst, dstkv, dstg,
    mid, src, keep, give, other, total,
    send_sem, recv_sem, sendk_sem, recvk_sem, sendg_sem, recvg_sem, sendo_sem, recvo_sem,
    own_sem, ownk_sem, owng_sem,
):
    d, c, z, core = place()
    me = d * CTX + c
    e = lax.div(c, 8)
    mine = core == e
    slot = core * 8 + lax.rem(c, 8)

    def grads(j):
        remote(srcg.at[j], dstg.at[slot], sendg_sem, recvg_sem, (2 * z + e, j)).start()

    owng = pltpu.make_async_copy(srcg.at[c], dstg.at[slot], owng_sem)

    @pl.when(mine)
    def _():
        owng.start()

    @pl.when(jnp.logical_not(mine))
    def _():
        grads(c)

    def turn(n, carry):
        grads(lax.rem(c + lax.rem(n * 5, CTX), CTX))
        return carry

    lax.fori_loop(1, CTX, turn, 0)

    for n in range(CTX):
        slots = row_slots(unp[n : n + 1, :])
        mid[n] = dot(slots, rows_in[n * TOK : (n + 1) * TOK, :], 1, 0).astype(BF16)

    def unsort_senders(grp, carry):
        r0 = pl.multiple_of(grp * 16, 16)
        rows = jnp.concatenate([mid[n, pl.ds(r0, 16), :] for n in range(CTX)], axis=0)
        where = dot(jnp.ones((8 * K, 128), BF16), compact_slot(col, grp), 1, 1)
        t = (where == iota((8 * K, 256), 0).astype(F32)).astype(BF16)
        out = dot(t, rows, 1, 0)
        for n in range(8):
            part = out[n * K : (n + 1) * K]
            src[grp * 8 + n] = part[:, 0:256].astype(BF16)
            keep[grp * 8 + n] = part[:, 256:384].astype(BF16)
            give[grp * 8 + n] = part[:, 384:512].astype(BF16)
        return carry

    lax.fori_loop(0, 16, unsort_senders, 0, unroll=4)

    swap = remote(give, other, sendo_sem, recvo_sem, (2 * z + 1 - core, c))
    swap.start()
    own = pltpu.make_async_copy(src.at[me], dst.at[me], own_sem)
    own.start()
    to_all(src, dst, send_sem, recv_sem)
    swap.wait()
    total[...] = (keep[...].astype(F32) + other[...].astype(F32)).astype(BF16)
    ownk = pltpu.make_async_copy(total.at[me], dstkv.at[me], ownk_sem)
    ownk.start()
    to_all(total, dstkv, sendk_sem, recvk_sem)
    own.wait()
    ownk.wait()

    @pl.when(mine)
    def _():
        owng.wait()
        wait_all(srcg, dstg, sendg_sem, recvg_sem, CTX - 1)

    @pl.when(jnp.logical_not(mine))
    def _():
        wait_all(srcg, dstg, sendg_sem, recvg_sem, CTX)

    wait_all(src, dst, send_sem, recv_sem, DEV - 1)
    wait_all(total, dstkv, sendk_sem, recvk_sem, DEV - 1)


def exchange_out(K, rows, col, unp, srcg):
    anywhere = pl.BlockSpec(memory_space=pl.ANY)
    vmem = pl.BlockSpec(memory_space=pltpu.VMEM)
    wide = pltpu.VMEM((DEV, K, 256), BF16)
    narrow = pltpu.VMEM((DEV, K, 128), BF16)
    return pl.pallas_call(
        functools.partial(exchange_out_kernel, K),
        in_specs=[vmem, vmem, vmem, anywhere],
        out_specs=[anywhere] * 3,
        out_shape=[
            jax.ShapeDtypeStruct((DEV, K, 256), BF16),
            jax.ShapeDtypeStruct((DEV, K, 128), BF16),
            jax.ShapeDtypeStruct(srcg.shape, BF16),
        ],
        scratch_shapes=[pltpu.VMEM((CTX, 256, 512), BF16), wide, narrow, narrow, narrow, narrow]
        + [pltpu.SemaphoreType.DMA] * 11,
        compiler_params=pltpu.CompilerParams(has_side_effects=True, vmem_limit_bytes=VMEM_LIMIT),
        name="exchange_out",
    )(rows, col, unp, srcg)


def attention_kernel(
    K, recv, other, recvg, att, xo, col, unp, over, x, keyt, valuet, mid, dk, dv, lengths
):
    scale = 1.0 / math.sqrt(DH)
    first_core = lax.rem(lax.axis_index("dp"), 2) == 0
    sizes = recvg[0, TOK:GROWS, 0:TOK].astype(F32)
    sizes = (sizes[8:9] * 8 + sizes[12:13]).astype(jnp.int32)
    for n in range(16):
        lengths[n] = jnp.sum(jnp.where(iota((1, TOK), 1) == n, sizes, 0))

    def slots_of(c):
        return row_slots(recvg[c, TOK : TOK + 8, 0:TOK].astype(F32)[0:1])

    for c in range(CTX):
        unp[c : c + 1, :] = recvg[c, TOK : TOK + 8, 0:TOK].astype(F32)[0:1]

    occ = jnp.zeros((256, 128), F32)
    for c in range(CTX):
        occ = occ + dot(slots_of(c), (iota((TOK, 128), 1) == c).astype(BF16), 1, 0)
    pair = (iota((256, 256), 0) // 2 == iota((256, 256), 1) // 2).astype(BF16)
    count = dot(pair, occ.astype(BF16), 1, 0)
    before = (iota((128, 128), 0) < iota((128, 128), 1)).astype(BF16)
    base = dot(count.astype(BF16), before, 1, 0)
    u = iota((256, 128), 0)
    col[...] = base + (u % 2 + (u // 2) % 8 * K).astype(F32)

    most = jnp.zeros((8 * K, DH), F32)
    for grp in range(16):
        most = jnp.maximum(most, recv[grp, :, 256:384].astype(F32))
    flags = (iota((8 * K, DH), 0) % K == K - 1) & (K < FULL)
    over[0] = jnp.max(jnp.where(flags, most, 0.0))

    def sort_senders(grp, carry):
        r0 = pl.multiple_of(grp * 16, 16)
        slot = dot(compact_slot(col, grp), jnp.ones((128, 8 * K), BF16), 1, 0)
        t = (slot == iota((256, 8 * K), 1).astype(F32)).astype(BF16)
        rows = dot(t, recv[grp], 1, 0).astype(BF16)
        rows2 = dot(t, other[grp], 1, 0).astype(BF16)
        for c in range(CTX):
            mid[c, pl.ds(r0, 16), 0:384] = rows[c * 16 : (c + 1) * 16]
            mid[c, pl.ds(r0, 16), 384:512] = rows2[c * 16 : (c + 1) * 16]
        return carry

    lax.fori_loop(0, 16, sort_senders, 0, unroll=16)

    def sort_rows(c, carry):
        y = dot(slots_of(c), mid[c], 0, 0)
        r = pl.ds(pl.multiple_of(c * TOK, TOK), TOK)
        keys = jnp.where(first_core, y[:, 256:384], y[:, 384:512])
        values = jnp.where(first_core, y[:, 384:512], y[:, 256:384])
        x[r, 0:256] = y[:, 0:256].astype(BF16)
        x[r, 256:384] = keys.astype(BF16)
        x[r, 384:512] = values.astype(BF16)
        keyt[:, r] = keys.T.astype(BF16)
        valuet[:, r] = values.T.astype(BF16)
        return carry

    lax.fori_loop(0, CTX, sort_rows, 0, unroll=16)

    dk[...] = jnp.zeros_like(dk)
    dv[...] = jnp.zeros_like(dv)

    def doc_start(position):
        start, end = jnp.zeros_like(position), jnp.int32(0)
        for n in range(16):
            start = jnp.where(end <= position, end, start)
            end = end + lengths[n]
        return start

    def tile(i, carry):
        q0 = pl.multiple_of(i * BQ, BQ)
        lo = doc_start(q0) // BK
        width = i - lo + 1

        def attend(w):
            k0 = pl.multiple_of(lo * BK, BK)
            span = pl.ds(k0, w * BK)
            here = pl.ds(q0, BQ)
            chunks = [pl.ds(pl.multiple_of(k0 + t * BK, BK), BK) for t in range(w)]
            qpos = q0 + iota((1, BQ), 1)
            qstart = doc_start(qpos)

            def scores(h):
                queries = x[here, h * 128 : (h + 1) * 128]
                out = []
                for t in range(w):
                    kpos = k0 + t * BK + iota((BK, BQ), 0)
                    seen = kpos >= qstart
                    if t == w - 1:
                        seen = seen & (kpos <= qpos)
                    out.append(jnp.where(seen, dot(x[chunks[t], 256:384], queries, 1, 1), -1e30))
                return out

            def grads_of(h):
                return jnp.concatenate(
                    [recvg[2 * i + n, 0:TOK, h * 128 : (h + 1) * 128] for n in range(2)], axis=0
                )

            def probs(s):
                top = functools.reduce(jnp.maximum, [jnp.max(a, axis=0, keepdims=True) for a in s])
                e = [jnp.exp2((a - top) * (scale * math.log2(math.e))) for a in s]
                total = functools.reduce(jnp.add, [jnp.sum(a, axis=0, keepdims=True) for a in e])
                inverse = 1.0 / total
                return [a * inverse for a in e]

            def attend_values(h, p, grads):
                low = jnp.concatenate([a.astype(BF16) for a in p], axis=0)
                outt = dot(valuet[:, span], low, 1, 0).astype(BF16)
                out = outt.astype(F32).T.astype(BF16)
                for n in range(2):
                    att[2 * i + n, :, h * 128 : (h + 1) * 128] = out[n * TOK : (n + 1) * TOK]
                delta = jnp.sum(grads.astype(F32).T * outt.astype(F32), axis=0, keepdims=True)
                return low, delta

            def dprobs(grads):
                return [dot(x[r, 384:512], grads, 1, 1) for r in chunks]

            def dscores(p, dp, delta):
                return jnp.concatenate(
                    [(a * (b - delta) * scale).astype(BF16) for a, b in zip(p, dp)], axis=0
                )

            def query_grads(h, ds):
                xo[here, h * 128 : (h + 1) * 128] = dot(keyt[:, span], ds, 1, 0).T.astype(BF16)

            ga, gb = grads_of(0), grads_of(1)
            sa = scores(0)
            sb = scores(1)
            pa = probs(sa)
            dpa = dprobs(ga)
            pb = probs(sb)
            lowa, deltaa = attend_values(0, pa, ga)
            dpb = dprobs(gb)
            dsa = dscores(pa, dpa, deltaa)
            lowb, deltab = attend_values(1, pb, gb)
            query_grads(0, dsa)
            dsb = dscores(pb, dpb, deltab)
            query_grads(1, dsb)
            dv[span, :] += dot(lowa, ga, 1, 0) + dot(lowb, gb, 1, 0)
            dk[span, :] += dot(dsa, x[here, 0:128], 1, 0) + dot(dsb, x[here, 128:256], 1, 0)

        for w in range(1, WMAX + 1):
            pl.when(width == w)(functools.partial(attend, w))
        return carry

    lax.fori_loop(0, SEQ // BQ, tile, 0)
    xo[:, 256:384] = jnp.where(first_core, dk[...], dv[...]).astype(BF16)
    xo[:, 384:512] = jnp.where(first_core, dv[...], dk[...]).astype(BF16)


def attention(K, recv, other, recvg):
    vmem = pl.BlockSpec(memory_space=pltpu.VMEM)
    return pl.pallas_call(
        functools.partial(attention_kernel, K),
        in_specs=[vmem] * 3,
        out_specs=[vmem] * 4 + [pl.BlockSpec(memory_space=pltpu.SMEM)],
        out_shape=[
            jax.ShapeDtypeStruct((CTX, TOK, 256), BF16),
            jax.ShapeDtypeStruct((SEQ, 512), BF16),
            jax.ShapeDtypeStruct((256, 128), F32),
            jax.ShapeDtypeStruct((CTX, TOK), F32),
            jax.ShapeDtypeStruct((1,), F32),
        ],
        scratch_shapes=[
            pltpu.VMEM((SEQ, 512), BF16),
            pltpu.VMEM((DH, SEQ), BF16),
            pltpu.VMEM((DH, SEQ), BF16),
            pltpu.VMEM((CTX, 256, 512), BF16),
            pltpu.VMEM((SEQ, DH), F32),
            pltpu.VMEM((SEQ, DH), F32),
            pltpu.SMEM((16,), jnp.int32),
        ],
        compiler_params=pltpu.CompilerParams(vmem_limit_bytes=VMEM_LIMIT),
        name="attention",
    )(recv, other, recvg)


def unpack_kernel(K, sel, back, backkv, att, attended, gq, gk, gv):
    s = sel[...]
    by_sequence = [(z, e) for z in range(4) for e in range(2)]
    for core, out in ((0, gk), (1, gv)):
        cols = slice(core * 256, (core + 1) * 256)
        attended[:, cols] = att[core, 0]
        rows = [back[z, core, e, 0].astype(F32) for z, e in by_sequence]
        gq[:, cols] = dot(s, jnp.concatenate(rows, axis=0).astype(BF16), 0, 0).astype(BF16)
        rows = [backkv[z, core, e, 0].astype(F32) for z, e in by_sequence]
        out[...] = dot(s, jnp.concatenate(rows, axis=0).astype(BF16), 0, 0).astype(BF16)


def unpack_rows(K, sel, back, backkv, att):
    return pl.pallas_call(
        functools.partial(unpack_kernel, K),
        grid=(KVH,),
        in_specs=[
            pl.BlockSpec((8 * K, TOK), lambda i: (0, 0)),
            pl.BlockSpec((4, 2, 2, 1, K, 256), lambda i: (0, 0, 0, i, 0, 0)),
            pl.BlockSpec((4, 2, 2, 1, K, 128), lambda i: (0, 0, 0, i, 0, 0)),
            pl.BlockSpec((2, 1, TOK, 256), lambda i: (0, i, 0, 0)),
        ],
        out_specs=[
            pl.BlockSpec((TOK, 512), lambda i: (0, i)),
            pl.BlockSpec((TOK, 512), lambda i: (0, i)),
            pl.BlockSpec((TOK, 128), lambda i: (0, i)),
            pl.BlockSpec((TOK, 128), lambda i: (0, i)),
        ],
        out_shape=[
            jax.ShapeDtypeStruct((TOK, H * DH), BF16),
            jax.ShapeDtypeStruct((TOK, H * DH), BF16),
            jax.ShapeDtypeStruct((TOK, KVH * DH), BF16),
            jax.ShapeDtypeStruct((TOK, KVH * DH), BF16),
        ],
        compiler_params=pltpu.CompilerParams(vmem_limit_bytes=VMEM_LIMIT),
        name="messages_to_rows",
    )(sel, back, backkv, att)


def middle(K, q_load, k_load, v_load, grad_out, pack_rows, unpack, doc_lengths):
    recv, other, recvg, sel = exchange_in(
        K, pack_rows[0].T, unpack, doc_lengths, q_load, k_load, v_load, grad_out
    )
    recv, other = (a.reshape(16, 8 * K, -1) for a in (recv, other))
    *parts, over = attention(K, recv, other, recvg)
    return over[0] > 0.5, (sel, *parts)


def finish(K, sel, att, rows, col, unp):
    returned, returnedkv, turned = exchange_out(K, rows, col, unp, att)
    returned, returnedkv = (a.reshape(4, 2, 2, KVH, K, -1) for a in (returned, returnedkv))
    return unpack_rows(K, sel, returned, returnedkv, turned.reshape(2, KVH, TOK, 256))


def local(*operands):
    over, parts = middle(SHORT, *operands)
    return lax.cond(
        over,
        lambda: finish(FULL, *middle(FULL, *operands)[1]),
        lambda: finish(SHORT, *parts),
    )


def solution(mesh):
    rows = P(("dp", "ctx"), None)
    return jax.shard_map(
        local,
        mesh=mesh,
        in_specs=(rows, rows, rows, rows, P(("dp", "ctx"), None, None), rows, P("dp", None)),
        out_specs=(rows, rows, rows, rows),
        check_vma=False,
    )
```

```python
import functools
import math

import jax
import jax.numpy as jnp
from jax import lax
from jax.experimental import pallas as pl
from jax.experimental.pallas import tpu as pltpu
from jax.sharding import PartitionSpec as P

H = 32
KVH = 8
DH = 128
TOK = 128
CTX = 16
DP = 8
DEV = 128
SEQ = 2048
MOST = 1024
COLS = 384
FULL = 32
SHORT = 24
GROWS = 144
BQ = 256
BK = 256
WMAX = MOST // BK + 1
VMEM_LIMIT = 56 * 2**20

F32 = jnp.float32
BF16 = jnp.bfloat16
MESH = pl.DeviceIdType.MESH


def dot(a, b, ca, cb):
    return lax.dot_general(a, b, (((ca,), (cb,)), ((), ())), preferred_element_type=F32)


def iota(shape, dim):
    return lax.broadcasted_iota(jnp.int32, shape, dim)


def remote(src, dst, send_sem, recv_sem, target):
    return pltpu.make_async_remote_copy(
        src_ref=src,
        dst_ref=dst,
        send_sem=send_sem,
        recv_sem=recv_sem,
        device_id=target,
        device_id_type=MESH,
    )


def row_slots(row):
    return (iota((256, TOK), 0).astype(F32) == row).astype(BF16)


def compact_slot(col, grp):
    tab = col[pl.ds(pl.multiple_of(grp * 16, 16), 16), :]
    own_c = iota((256, 128), 0) // 16 == iota((256, 128), 1)
    return jnp.where(own_c, jnp.concatenate([tab] * CTX, axis=0), 0.0).astype(BF16)


def place():
    d = lax.axis_index("dp")
    c = lax.axis_index("ctx")
    return d, c, lax.div(d, 2), lax.rem(d, 2)


def partner(n):
    d, c, z, core = place()
    x, y = lax.div(c, 4), lax.rem(c, 4)
    j = lax.rem(n * 37, DEV)
    dy = lax.rem(j, 2) + 2 * lax.rem(lax.div(j, 16), 2)
    dx = lax.rem(lax.div(j, 2), 2) + 2 * lax.rem(lax.div(j, 32), 2)
    dz = lax.rem(lax.div(j, 4), 2) + 2 * lax.div(j, 64)
    dcore = lax.rem(lax.div(j, 8), 2)
    return lax.rem(z + dz, 4) * 2 + lax.rem(core + dcore, 2), lax.rem(x + dx, 4) * 4 + lax.rem(y + dy, 4)


def to_all(src, dst, send_sem, recv_sem):
    d, c, _, _ = place()
    me = d * CTX + c

    def one(n):
        td, tc = partner(n)
        remote(src.at[td * CTX + tc], dst.at[me], send_sem, recv_sem, (td, tc)).start()

    def some(n, carry):
        for i in range(8):
            one(8 * n - 7 + i)
        return carry

    lax.fori_loop(1, CTX, some, 0)
    for n in range(121, DEV):
        one(n)


def greet_all():
    barrier = pltpu.get_barrier_semaphore()

    def greet(n, carry):
        pl.semaphore_signal(barrier, inc=1, device_id=partner(n), device_id_type=MESH)
        return carry

    lax.fori_loop(1, DEV, greet, 0)
    return lambda: pl.semaphore_wait(barrier, DEV - 1)


def wait_all(src, dst, send_sem, recv_sem, count):
    d, c, _, _ = place()
    remote(src.at[pl.ds(0, count)], dst.at[pl.ds(0, count)], send_sem, recv_sem, (d, c)).wait()


def exchange_in_kernel(
    K, slots, unp, lengths, q, k, v, g, dst, other, dstg, sel,
    send, sendg, over_s,
    send_sem, recv_sem, sendg_sem, recvg_sem, sendo_sem, recvo_sem, own_sem, owng_sem,
):
    d, c, z, core = place()
    me = d * CTX + c
    mine = core == lax.div(c, 8)
    first = core * 8 + lax.rem(c, 8)
    all_here = greet_all()

    r = iota((16, TOK), 0)
    spread = (r == iota((16, TOK), 1)).astype(BF16)
    sizes = jnp.broadcast_to(lengths[...], (16, 16))
    high = dot((sizes // 8).astype(F32).astype(BF16), spread, 1, 0)
    low = dot((sizes % 8).astype(F32).astype(BF16), spread, 1, 0)
    ints = jnp.where(r < 8, unp[...].astype(F32), jnp.where(r < 12, high, low)).astype(BF16)
    for h in range(KVH):
        for p in range(2):
            sendg[p * 8 + h, 0:TOK, :] = g[:, h * 512 + p * 256 : h * 512 + (p + 1) * 256]
            sendg[p * 8 + h, TOK:GROWS, 0:TOK] = ints
            sendg[p * 8 + h, TOK:GROWS, TOK:256] = jnp.zeros((16, 128), BF16)

    all_here()

    def grads(j):
        target = (2 * z + lax.div(j, 8), core * 8 + lax.rem(j, 8))
        remote(sendg.at[j], dstg.at[c], sendg_sem, recvg_sem, target).start()

    owng = pltpu.make_async_copy(sendg.at[first], dstg.at[c], owng_sem)

    @pl.when(mine)
    def _():
        owng.start()

    @pl.when(jnp.logical_not(mine))
    def _():
        grads(first)

    def turn(n, carry):
        grads(lax.rem(first + lax.rem(n * 5, CTX), CTX))
        return carry

    lax.fori_loop(1, CTX, turn, 0)

    occupied = slots[...] >= 0
    count = jnp.where(occupied[0:1], 1.0, 0.0) + jnp.where(occupied[1:2], 1.0, 0.0)
    a, b = iota((DEV, DEV), 0), iota((DEV, DEV), 1)
    earlier = ((a < b) & (a // CTX == b // CTX)).astype(BF16)
    base = dot(jnp.broadcast_to(count, (16, DEV)).astype(BF16), earlier, 1, 0)[0:1].astype(jnp.int32)
    rows_of = jnp.concatenate([slots[...].astype(F32), jnp.zeros((126, DEV), F32)], axis=0).T
    value = jnp.zeros((8 * K, TOK), F32)
    over = jnp.zeros((1, 1), F32)
    for j in range(2):
        rank = base + j
        kept = occupied[j : j + 1]
        if K < FULL:
            lost = jnp.where(kept & (rank >= K - 1), 1.0, 0.0)
            over = jnp.maximum(over, jnp.max(lost, axis=1, keepdims=True))
            kept = kept & (rank < K - 1)
        slot = jnp.where(kept, iota((1, DEV), 1) // CTX * K + rank, -1)
        where = (iota((8 * K, DEV), 0) == slot).astype(BF16)
        holds = (rows_of[:, j : j + 1] == iota((DEV, TOK), 1).astype(F32)).astype(BF16)
        value = value + dot(where, holds, 1, 0)
    s = value.astype(BF16)
    sel[...] = s
    last = (iota((8 * K, TOK), 0) % K == K - 1) & (K < FULL)
    over_s[...] = jnp.where(last, over, 0.0)

    def build(h, carry):
        wide = pl.ds(pl.multiple_of(h * 512, 512), 512)
        narrow = pl.ds(pl.multiple_of(h * 128, 128), 128)
        yq = dot(sel[...], q[:, wide], 1, 0)
        yk = dot(sel[...], k[:, narrow], 1, 0) + over_s[...]
        yv = dot(sel[...], v[:, narrow], 1, 0) + over_s[...]
        for n in range(DP):
            rows = slice(n * K, (n + 1) * K)
            for p, ykv in ((0, yk), (1, yv)):
                t = ((n // 2 * 2 + p) * 2 + n % 2) * 8 + h
                send[t, :, 0:256] = yq[rows, p * 256 : (p + 1) * 256].astype(BF16)
                send[t, :, 256:384] = ykv[rows].astype(BF16)
        return carry

    lax.fori_loop(0, KVH, build, 0)

    own = pltpu.make_async_copy(send.at[me], dst.at[me], own_sem)
    own.start()
    to_all(send, dst, send_sem, recv_sem)
    own.wait()
    wait_all(send, dst, send_sem, recv_sem, DEV - 1)
    swap = remote(dst.at[:, :, pl.ds(256, 128)], other, sendo_sem, recvo_sem, (2 * z + 1 - core, c))
    swap.start()

    @pl.when(mine)
    def _():
        owng.wait()
        wait_all(sendg, dstg, sendg_sem, recvg_sem, CTX - 1)

    @pl.when(jnp.logical_not(mine))
    def _():
        wait_all(sendg, dstg, sendg_sem, recvg_sem, CTX)

    swap.wait()


def exchange_in(K, slots, unp, lengths, q, k, v, g):
    anywhere = pl.BlockSpec(memory_space=pl.ANY)
    vmem = pl.BlockSpec(memory_space=pltpu.VMEM)
    return pl.pallas_call(
        functools.partial(exchange_in_kernel, K),
        in_specs=[vmem] * 7,
        out_specs=[anywhere] * 3 + [vmem],
        out_shape=[
            jax.ShapeDtypeStruct((DEV, K, COLS), BF16),
            jax.ShapeDtypeStruct((DEV, K, 128), BF16),
            jax.ShapeDtypeStruct((CTX, GROWS, 256), BF16),
            jax.ShapeDtypeStruct((8 * K, TOK), BF16),
        ],
        scratch_shapes=[
            pltpu.VMEM((DEV, K, COLS), BF16),
            pltpu.VMEM((CTX, GROWS, 256), BF16),
            pltpu.VMEM((8 * K, TOK), F32),
        ]
        + [pltpu.SemaphoreType.DMA] * 8,
        compiler_params=pltpu.CompilerParams(
            has_side_effects=True, vmem_limit_bytes=VMEM_LIMIT, collective_id=K
        ),
        name="exchange_in",
    )(slots, unp, lengths, q, k, v, g)


def exchange_out_kernel(
    K, rows_in, col, unp, srcg, dst, dstkv, dstg,
    mid, src, keep, give, other, total,
    send_sem, recv_sem, sendk_sem, recvk_sem, sendg_sem, recvg_sem, sendo_sem, recvo_sem,
    own_sem, ownk_sem, owng_sem,
):
    d, c, z, core = place()
    me = d * CTX + c
    e = lax.div(c, 8)
    mine = core == e
    slot = core * 8 + lax.rem(c, 8)

    def grads(j):
        remote(srcg.at[j], dstg.at[slot], sendg_sem, recvg_sem, (2 * z + e, j)).start()

    owng = pltpu.make_async_copy(srcg.at[c], dstg.at[slot], owng_sem)

    @pl.when(mine)
    def _():
        owng.start()

    @pl.when(jnp.logical_not(mine))
    def _():
        grads(c)

    def turn(n, carry):
        grads(lax.rem(c + lax.rem(n * 5, CTX), CTX))
        return carry

    lax.fori_loop(1, CTX, turn, 0)

    for n in range(CTX):
        slots = row_slots(unp[n : n + 1, :])
        mid[n] = dot(slots, rows_in[n * TOK : (n + 1) * TOK, :], 1, 0).astype(BF16)

    def unsort_senders(grp, carry):
        r0 = pl.multiple_of(grp * 16, 16)
        rows = jnp.concatenate([mid[n, pl.ds(r0, 16), :] for n in range(CTX)], axis=0)
        where = dot(jnp.ones((8 * K, 128), BF16), compact_slot(col, grp), 1, 1)
        t = (where == iota((8 * K, 256), 0).astype(F32)).astype(BF16)
        out = dot(t, rows, 1, 0)
        for n in range(8):
            part = out[n * K : (n + 1) * K]
            src[grp * 8 + n] = part[:, 0:256].astype(BF16)
            keep[grp * 8 + n] = part[:, 256:384].astype(BF16)
            give[grp * 8 + n] = part[:, 384:512].astype(BF16)
        return carry

    lax.fori_loop(0, 16, unsort_senders, 0, unroll=4)

    swap = remote(give, other, sendo_sem, recvo_sem, (2 * z + 1 - core, c))
    swap.start()
    own = pltpu.make_async_copy(src.at[me], dst.at[me], own_sem)
    own.start()
    to_all(src, dst, send_sem, recv_sem)
    swap.wait()
    total[...] = (keep[...].astype(F32) + other[...].astype(F32)).astype(BF16)
    ownk = pltpu.make_async_copy(total.at[me], dstkv.at[me], ownk_sem)
    ownk.start()
    to_all(total, dstkv, sendk_sem, recvk_sem)
    own.wait()
    ownk.wait()

    @pl.when(mine)
    def _():
        owng.wait()
        wait_all(srcg, dstg, sendg_sem, recvg_sem, CTX - 1)

    @pl.when(jnp.logical_not(mine))
    def _():
        wait_all(srcg, dstg, sendg_sem, recvg_sem, CTX)

    wait_all(src, dst, send_sem, recv_sem, DEV - 1)
    wait_all(total, dstkv, sendk_sem, recvk_sem, DEV - 1)


def exchange_out(K, rows, col, unp, srcg):
    anywhere = pl.BlockSpec(memory_space=pl.ANY)
    vmem = pl.BlockSpec(memory_space=pltpu.VMEM)
    wide = pltpu.VMEM((DEV, K, 256), BF16)
    narrow = pltpu.VMEM((DEV, K, 128), BF16)
    return pl.pallas_call(
        functools.partial(exchange_out_kernel, K),
        in_specs=[vmem, vmem, vmem, anywhere],
        out_specs=[anywhere] * 3,
        out_shape=[
            jax.ShapeDtypeStruct((DEV, K, 256), BF16),
            jax.ShapeDtypeStruct((DEV, K, 128), BF16),
            jax.ShapeDtypeStruct(srcg.shape, BF16),
        ],
        scratch_shapes=[pltpu.VMEM((CTX, 256, 512), BF16), wide, narrow, narrow, narrow, narrow]
        + [pltpu.SemaphoreType.DMA] * 11,
        compiler_params=pltpu.CompilerParams(has_side_effects=True, vmem_limit_bytes=VMEM_LIMIT),
        name="exchange_out",
    )(rows, col, unp, srcg)


def attention_kernel(
    K, recv, other, recvg, att, xo, col, unp, over, x, keyt, valuet, mid, dk, dv, lengths
):
    scale = 1.0 / math.sqrt(DH)
    first_core = lax.rem(lax.axis_index("dp"), 2) == 0
    sizes = recvg[0, TOK:GROWS, 0:TOK].astype(F32)
    sizes = (sizes[8:9] * 8 + sizes[12:13]).astype(jnp.int32)
    for n in range(16):
        lengths[n] = jnp.sum(jnp.where(iota((1, TOK), 1) == n, sizes, 0))

    def slots_of(c):
        return row_slots(recvg[c, TOK : TOK + 8, 0:TOK].astype(F32)[0:1])

    for c in range(CTX):
        unp[c : c + 1, :] = recvg[c, TOK : TOK + 8, 0:TOK].astype(F32)[0:1]

    occ = jnp.zeros((256, 128), F32)
    for c in range(CTX):
        occ = occ + dot(slots_of(c), (iota((TOK, 128), 1) == c).astype(BF16), 1, 0)
    pair = (iota((256, 256), 0) // 2 == iota((256, 256), 1) // 2).astype(BF16)
    count = dot(pair, occ.astype(BF16), 1, 0)
    before = (iota((128, 128), 0) < iota((128, 128), 1)).astype(BF16)
    base = dot(count.astype(BF16), before, 1, 0)
    u = iota((256, 128), 0)
    col[...] = base + (u % 2 + (u // 2) % 8 * K).astype(F32)

    most = jnp.zeros((8 * K, DH), F32)
    for grp in range(16):
        most = jnp.maximum(most, recv[grp, :, 256:384].astype(F32))
    flags = (iota((8 * K, DH), 0) % K == K - 1) & (K < FULL)
    over[0] = jnp.max(jnp.where(flags, most, 0.0))

    def sort_senders(grp, carry):
        r0 = pl.multiple_of(grp * 16, 16)
        slot = dot(compact_slot(col, grp), jnp.ones((128, 8 * K), BF16), 1, 0)
        t = (slot == iota((256, 8 * K), 1).astype(F32)).astype(BF16)
        rows = dot(t, recv[grp], 1, 0).astype(BF16)
        rows2 = dot(t, other[grp], 1, 0).astype(BF16)
        for c in range(CTX):
            mid[c, pl.ds(r0, 16), 0:384] = rows[c * 16 : (c + 1) * 16]
            mid[c, pl.ds(r0, 16), 384:512] = rows2[c * 16 : (c + 1) * 16]
        return carry

    lax.fori_loop(0, 16, sort_senders, 0, unroll=16)

    def sort_rows(c, carry):
        y = dot(slots_of(c), mid[c], 0, 0)
        r = pl.ds(pl.multiple_of(c * TOK, TOK), TOK)
        keys = jnp.where(first_core, y[:, 256:384], y[:, 384:512])
        values = jnp.where(first_core, y[:, 384:512], y[:, 256:384])
        x[r, 0:256] = y[:, 0:256].astype(BF16)
        x[r, 256:384] = keys.astype(BF16)
        x[r, 384:512] = values.astype(BF16)
        keyt[:, r] = keys.T.astype(BF16)
        valuet[:, r] = values.T.astype(BF16)
        return carry

    lax.fori_loop(0, CTX, sort_rows, 0, unroll=16)

    dk[...] = jnp.zeros_like(dk)
    dv[...] = jnp.zeros_like(dv)

    def doc_start(position):
        start, end = jnp.zeros_like(position), jnp.int32(0)
        for n in range(16):
            start = jnp.where(end <= position, end, start)
            end = end + lengths[n]
        return start

    def tile(i, carry):
        q0 = pl.multiple_of(i * BQ, BQ)
        lo = doc_start(q0) // BK
        width = i - lo + 1

        def attend(w):
            k0 = pl.multiple_of(lo * BK, BK)
            span = pl.ds(k0, w * BK)
            here = pl.ds(q0, BQ)
            chunks = [pl.ds(pl.multiple_of(k0 + t * BK, BK), BK) for t in range(w)]
            qpos = q0 + iota((1, BQ), 1)
            qstart = doc_start(qpos)

            def scores(h):
                queries = x[here, h * 128 : (h + 1) * 128]
                out = []
                for t in range(w):
                    kpos = k0 + t * BK + iota((BK, BQ), 0)
                    seen = kpos >= qstart
                    if t == w - 1:
                        seen = seen & (kpos <= qpos)
                    out.append(jnp.where(seen, dot(x[chunks[t], 256:384], queries, 1, 1), -1e30))
                return out

            def grads_of(h):
                return jnp.concatenate(
                    [recvg[2 * i + n, 0:TOK, h * 128 : (h + 1) * 128] for n in range(2)], axis=0
                )

            def probs(s):
                top = functools.reduce(jnp.maximum, [jnp.max(a, axis=0, keepdims=True) for a in s])
                e = [jnp.exp2((a - top) * (scale * math.log2(math.e))) for a in s]
                total = functools.reduce(jnp.add, [jnp.sum(a, axis=0, keepdims=True) for a in e])
                inverse = 1.0 / total
                return [a * inverse for a in e]

            def attend_values(h, p, grads):
                low = jnp.concatenate([a.astype(BF16) for a in p], axis=0)
                outt = dot(valuet[:, span], low, 1, 0).astype(BF16)
                out = outt.astype(F32).T.astype(BF16)
                for n in range(2):
                    att[2 * i + n, :, h * 128 : (h + 1) * 128] = out[n * TOK : (n + 1) * TOK]
                delta = jnp.sum(grads.astype(F32).T * outt.astype(F32), axis=0, keepdims=True)
                return low, delta

            def dprobs(grads):
                return [dot(x[r, 384:512], grads, 1, 1) for r in chunks]

            def dscores(p, dp, delta):
                return jnp.concatenate(
                    [(a * (b - delta) * scale).astype(BF16) for a, b in zip(p, dp)], axis=0
                )

            def query_grads(h, ds):
                xo[here, h * 128 : (h + 1) * 128] = dot(keyt[:, span], ds, 1, 0).T.astype(BF16)

            ga, gb = grads_of(0), grads_of(1)
            sa = scores(0)
            sb = scores(1)
            pa = probs(sa)
            dpa = dprobs(ga)
            pb = probs(sb)
            lowa, deltaa = attend_values(0, pa, ga)
            dpb = dprobs(gb)
            dsa = dscores(pa, dpa, deltaa)
            lowb, deltab = attend_values(1, pb, gb)
            query_grads(0, dsa)
            dsb = dscores(pb, dpb, deltab)
            query_grads(1, dsb)
            dv[span, :] += dot(lowa, ga, 1, 0) + dot(lowb, gb, 1, 0)
            dk[span, :] += dot(dsa, x[here, 0:128], 1, 0) + dot(dsb, x[here, 128:256], 1, 0)

        for w in range(1, WMAX + 1):
            pl.when(width == w)(functools.partial(attend, w))
        return carry

    lax.fori_loop(0, SEQ // BQ, tile, 0)
    xo[:, 256:384] = jnp.where(first_core, dk[...], dv[...]).astype(BF16)
    xo[:, 384:512] = jnp.where(first_core, dv[...], dk[...]).astype(BF16)


def attention(K, recv, other, recvg):
    vmem = pl.BlockSpec(memory_space=pltpu.VMEM)
    return pl.pallas_call(
        functools.partial(attention_kernel, K),
        in_specs=[vmem] * 3,
        out_specs=[vmem] * 4 + [pl.BlockSpec(memory_space=pltpu.SMEM)],
        out_shape=[
            jax.ShapeDtypeStruct((CTX, TOK, 256), BF16),
            jax.ShapeDtypeStruct((SEQ, 512), BF16),
            jax.ShapeDtypeStruct((256, 128), F32),
            jax.ShapeDtypeStruct((CTX, TOK), F32),
            jax.ShapeDtypeStruct((1,), F32),
        ],
        scratch_shapes=[
            pltpu.VMEM((SEQ, 512), BF16),
            pltpu.VMEM((DH, SEQ), BF16),
            pltpu.VMEM((DH, SEQ), BF16),
            pltpu.VMEM((CTX, 256, 512), BF16),
            pltpu.VMEM((SEQ, DH), F32),
            pltpu.VMEM((SEQ, DH), F32),
            pltpu.SMEM((16,), jnp.int32),
        ],
        compiler_params=pltpu.CompilerParams(vmem_limit_bytes=VMEM_LIMIT),
        name="attention",
    )(recv, other, recvg)


STEP = 4


def unpack_kernel(sel, back, backkv, att, attended, gq, gk, gv):
    s = sel[...]
    by_sequence = [(z, e) for z in range(4) for e in range(2)]
    for h in range(STEP):
        for core, out in ((0, gk), (1, gv)):
            cols = slice(h * 512 + core * 256, h * 512 + (core + 1) * 256)
            attended[:, cols] = att[core, h]
            rows = [back[z, core, e, h].astype(F32) for z, e in by_sequence]
            gq[:, cols] = dot(s, jnp.concatenate(rows, axis=0).astype(BF16), 0, 0).astype(BF16)
            rows = [backkv[z, core, e, h].astype(F32) for z, e in by_sequence]
            out[:, h * 128 : (h + 1) * 128] = dot(
                s, jnp.concatenate(rows, axis=0).astype(BF16), 0, 0
            ).astype(BF16)


def unpack_rows(K, sel, back, backkv, att):
    return pl.pallas_call(
        unpack_kernel,
        grid=(KVH // STEP,),
        in_specs=[
            pl.BlockSpec((8 * K, TOK), lambda i: (0, 0)),
            pl.BlockSpec((4, 2, 2, STEP, K, 256), lambda i: (0, 0, 0, i, 0, 0)),
            pl.BlockSpec((4, 2, 2, STEP, K, 128), lambda i: (0, 0, 0, i, 0, 0)),
            pl.BlockSpec((2, STEP, TOK, 256), lambda i: (0, i, 0, 0)),
        ],
        out_specs=[
            pl.BlockSpec((TOK, STEP * 512), lambda i: (0, i)),
            pl.BlockSpec((TOK, STEP * 512), lambda i: (0, i)),
            pl.BlockSpec((TOK, STEP * 128), lambda i: (0, i)),
            pl.BlockSpec((TOK, STEP * 128), lambda i: (0, i)),
        ],
        out_shape=[
            jax.ShapeDtypeStruct((TOK, H * DH), BF16),
            jax.ShapeDtypeStruct((TOK, H * DH), BF16),
            jax.ShapeDtypeStruct((TOK, KVH * DH), BF16),
            jax.ShapeDtypeStruct((TOK, KVH * DH), BF16),
        ],
        compiler_params=pltpu.CompilerParams(vmem_limit_bytes=VMEM_LIMIT),
        name="messages_to_rows",
    )(sel, back, backkv, att)


def middle(K, q_load, k_load, v_load, grad_out, pack_rows, unpack, doc_lengths):
    recv, other, recvg, sel = exchange_in(
        K, pack_rows[0].T, unpack, doc_lengths, q_load, k_load, v_load, grad_out
    )
    recv, other = (a.reshape(16, 8 * K, -1) for a in (recv, other))
    *parts, over = attention(K, recv, other, recvg)
    return over[0] > 0.5, (sel, *parts)


def finish(K, sel, att, rows, col, unp):
    returned, returnedkv, turned = exchange_out(K, rows, col, unp, att)
    returned, returnedkv = (a.reshape(4, 2, 2, KVH, K, -1) for a in (returned, returnedkv))
    return unpack_rows(K, sel, returned, returnedkv, turned.reshape(2, KVH, TOK, 256))


def local(*operands):
    over, parts = middle(SHORT, *operands)
    return lax.cond(
        over,
        lambda: finish(FULL, *middle(FULL, *operands)[1]),
        lambda: finish(SHORT, *parts),
    )


def solution(mesh):
    rows = P(("dp", "ctx"), None)
    return jax.shard_map(
        local,
        mesh=mesh,
        in_specs=(rows, rows, rows, rows, P(("dp", "ctx"), None, None), rows, P("dp", None)),
        out_specs=(rows, rows, rows, rows),
        check_vma=False,
    )
```

```python
import functools
import math

import jax
import jax.numpy as jnp
from jax import lax
from jax.experimental import pallas as pl
from jax.experimental.pallas import tpu as pltpu
from jax.sharding import PartitionSpec as P

H = 32
KVH = 8
DH = 128
TOK = 128
CTX = 16
DP = 8
DEV = 128
SEQ = 2048
MOST = 1024
COLS = 384
FULL = 32
SHORT = 24
GROWS = 144
BQ = 256
BK = 256
WMAX = MOST // BK + 1
VMEM_LIMIT = 56 * 2**20

F32 = jnp.float32
BF16 = jnp.bfloat16
MESH = pl.DeviceIdType.MESH


def dot(a, b, ca, cb):
    return lax.dot_general(a, b, (((ca,), (cb,)), ((), ())), preferred_element_type=F32)


def iota(shape, dim):
    return lax.broadcasted_iota(jnp.int32, shape, dim)


def remote(src, dst, send_sem, recv_sem, target):
    return pltpu.make_async_remote_copy(
        src_ref=src,
        dst_ref=dst,
        send_sem=send_sem,
        recv_sem=recv_sem,
        device_id=target,
        device_id_type=MESH,
    )


def row_slots(row):
    return (iota((256, TOK), 0).astype(F32) == row).astype(BF16)


def compact_slot(col, grp):
    tab = col[pl.ds(pl.multiple_of(grp * 16, 16), 16), :]
    own_c = iota((256, 128), 0) // 16 == iota((256, 128), 1)
    return jnp.where(own_c, jnp.concatenate([tab] * CTX, axis=0), 0.0).astype(BF16)


def place():
    d = lax.axis_index("dp")
    c = lax.axis_index("ctx")
    return d, c, lax.div(d, 2), lax.rem(d, 2)


def partner(n):
    d, c, z, core = place()
    x, y = lax.div(c, 4), lax.rem(c, 4)
    j = lax.rem(n * 37, DEV)
    dy = lax.rem(j, 2) + 2 * lax.rem(lax.div(j, 16), 2)
    dx = lax.rem(lax.div(j, 2), 2) + 2 * lax.rem(lax.div(j, 32), 2)
    dz = lax.rem(lax.div(j, 4), 2) + 2 * lax.div(j, 64)
    dcore = lax.rem(lax.div(j, 8), 2)
    return lax.rem(z + dz, 4) * 2 + lax.rem(core + dcore, 2), lax.rem(x + dx, 4) * 4 + lax.rem(y + dy, 4)


def to_all(src, dst, send_sem, recv_sem):
    d, c, _, _ = place()
    me = d * CTX + c

    def one(n):
        td, tc = partner(n)
        remote(src.at[td * CTX + tc], dst.at[me], send_sem, recv_sem, (td, tc)).start()

    def some(n, carry):
        for i in range(8):
            one(8 * n - 7 + i)
        return carry

    lax.fori_loop(1, CTX, some, 0)
    for n in range(121, DEV):
        one(n)


def greet_all():
    barrier = pltpu.get_barrier_semaphore()

    def greet(n, carry):
        pl.semaphore_signal(barrier, inc=1, device_id=partner(n), device_id_type=MESH)
        return carry

    lax.fori_loop(1, DEV, greet, 0)
    return lambda: pl.semaphore_wait(barrier, DEV - 1)


def wait_all(src, dst, send_sem, recv_sem, count):
    d, c, _, _ = place()
    remote(src.at[pl.ds(0, count)], dst.at[pl.ds(0, count)], send_sem, recv_sem, (d, c)).wait()


def exchange_in_kernel(
    K, slots, unp, lengths, q_in, k_in, v_in, g, dst, other, dstg, sel,
    send, sendg, over_s, q, k, v,
    send_sem, recv_sem, sendg_sem, recvg_sem, sendo_sem, recvo_sem, own_sem, owng_sem,
    q_sem, k_sem, v_sem,
):
    d, c, z, core = place()
    me = d * CTX + c
    mine = core == lax.div(c, 8)
    first = core * 8 + lax.rem(c, 8)
    all_here = greet_all()
    loads = [
        pltpu.make_async_copy(a, b, sem)
        for a, b, sem in ((q_in, q, q_sem), (k_in, k, k_sem), (v_in, v, v_sem))
    ]
    for load in loads:
        load.start()

    r = iota((16, TOK), 0)
    spread = (r == iota((16, TOK), 1)).astype(BF16)
    sizes = jnp.broadcast_to(lengths[...], (16, 16))
    high = dot((sizes // 8).astype(F32).astype(BF16), spread, 1, 0)
    low = dot((sizes % 8).astype(F32).astype(BF16), spread, 1, 0)
    ints = jnp.where(r < 8, unp[...].astype(F32), jnp.where(r < 12, high, low)).astype(BF16)
    for h in range(KVH):
        for p in range(2):
            sendg[p * 8 + h, 0:TOK, :] = g[:, h * 512 + p * 256 : h * 512 + (p + 1) * 256]
            sendg[p * 8 + h, TOK:GROWS, 0:TOK] = ints
            sendg[p * 8 + h, TOK:GROWS, TOK:256] = jnp.zeros((16, 128), BF16)

    all_here()

    def grads(j):
        target = (2 * z + lax.div(j, 8), core * 8 + lax.rem(j, 8))
        remote(sendg.at[j], dstg.at[c], sendg_sem, recvg_sem, target).start()

    owng = pltpu.make_async_copy(sendg.at[first], dstg.at[c], owng_sem)

    @pl.when(mine)
    def _():
        owng.start()

    @pl.when(jnp.logical_not(mine))
    def _():
        grads(first)

    def turn(n, carry):
        grads(lax.rem(first + lax.rem(n * 5, CTX), CTX))
        return carry

    lax.fori_loop(1, CTX, turn, 0)

    occupied = slots[...] >= 0
    count = jnp.where(occupied[0:1], 1.0, 0.0) + jnp.where(occupied[1:2], 1.0, 0.0)
    a, b = iota((DEV, DEV), 0), iota((DEV, DEV), 1)
    earlier = ((a < b) & (a // CTX == b // CTX)).astype(BF16)
    base = dot(jnp.broadcast_to(count, (16, DEV)).astype(BF16), earlier, 1, 0)[0:1].astype(jnp.int32)
    rows_of = jnp.concatenate([slots[...].astype(F32), jnp.zeros((126, DEV), F32)], axis=0).T
    value = jnp.zeros((8 * K, TOK), F32)
    over = jnp.zeros((1, 1), F32)
    for j in range(2):
        rank = base + j
        kept = occupied[j : j + 1]
        if K < FULL:
            lost = jnp.where(kept & (rank >= K - 1), 1.0, 0.0)
            over = jnp.maximum(over, jnp.max(lost, axis=1, keepdims=True))
            kept = kept & (rank < K - 1)
        slot = jnp.where(kept, iota((1, DEV), 1) // CTX * K + rank, -1)
        where = (iota((8 * K, DEV), 0) == slot).astype(BF16)
        holds = (rows_of[:, j : j + 1] == iota((DEV, TOK), 1).astype(F32)).astype(BF16)
        value = value + dot(where, holds, 1, 0)
    s = value.astype(BF16)
    sel[...] = s
    last = (iota((8 * K, TOK), 0) % K == K - 1) & (K < FULL)
    over_s[...] = jnp.where(last, over, 0.0)

    for load in loads:
        load.wait()

    def build(h, carry):
        wide = pl.ds(pl.multiple_of(h * 512, 512), 512)
        narrow = pl.ds(pl.multiple_of(h * 128, 128), 128)
        yq = dot(sel[...], q[:, wide], 1, 0)
        yk = dot(sel[...], k[:, narrow], 1, 0) + over_s[...]
        yv = dot(sel[...], v[:, narrow], 1, 0) + over_s[...]
        for n in range(DP):
            rows = slice(n * K, (n + 1) * K)
            for p, ykv in ((0, yk), (1, yv)):
                t = ((n // 2 * 2 + p) * 2 + n % 2) * 8 + h
                send[t, :, 0:256] = yq[rows, p * 256 : (p + 1) * 256].astype(BF16)
                send[t, :, 256:384] = ykv[rows].astype(BF16)
        return carry

    lax.fori_loop(0, KVH, build, 0)

    own = pltpu.make_async_copy(send.at[me], dst.at[me], own_sem)
    own.start()
    to_all(send, dst, send_sem, recv_sem)
    own.wait()
    wait_all(send, dst, send_sem, recv_sem, DEV - 1)
    swap = remote(dst.at[:, :, pl.ds(256, 128)], other, sendo_sem, recvo_sem, (2 * z + 1 - core, c))
    swap.start()

    @pl.when(mine)
    def _():
        owng.wait()
        wait_all(sendg, dstg, sendg_sem, recvg_sem, CTX - 1)

    @pl.when(jnp.logical_not(mine))
    def _():
        wait_all(sendg, dstg, sendg_sem, recvg_sem, CTX)

    swap.wait()


def exchange_in(K, slots, unp, lengths, q, k, v, g):
    anywhere = pl.BlockSpec(memory_space=pl.ANY)
    vmem = pl.BlockSpec(memory_space=pltpu.VMEM)
    return pl.pallas_call(
        functools.partial(exchange_in_kernel, K),
        in_specs=[vmem] * 3 + [anywhere] * 3 + [vmem],
        out_specs=[anywhere] * 3 + [vmem],
        out_shape=[
            jax.ShapeDtypeStruct((DEV, K, COLS), BF16),
            jax.ShapeDtypeStruct((DEV, K, 128), BF16),
            jax.ShapeDtypeStruct((CTX, GROWS, 256), BF16),
            jax.ShapeDtypeStruct((8 * K, TOK), BF16),
        ],
        scratch_shapes=[
            pltpu.VMEM((DEV, K, COLS), BF16),
            pltpu.VMEM((CTX, GROWS, 256), BF16),
            pltpu.VMEM((8 * K, TOK), F32),
            pltpu.VMEM((TOK, H * DH), BF16),
            pltpu.VMEM((TOK, KVH * DH), BF16),
            pltpu.VMEM((TOK, KVH * DH), BF16),
        ]
        + [pltpu.SemaphoreType.DMA] * 11,
        compiler_params=pltpu.CompilerParams(
            has_side_effects=True, vmem_limit_bytes=VMEM_LIMIT, collective_id=K
        ),
        name="exchange_in",
    )(slots, unp, lengths, q, k, v, g)


def exchange_out_kernel(
    K, rows_hbm, col, unp, srcg, dst, dstkv, dstg,
    rows_in, mid, src, keep, give, other, total,
    send_sem, recv_sem, sendk_sem, recvk_sem, sendg_sem, recvg_sem, sendo_sem, recvo_sem,
    own_sem, ownk_sem, owng_sem, rows_sem,
):
    d, c, z, core = place()
    me = d * CTX + c
    e = lax.div(c, 8)
    mine = core == e
    slot = core * 8 + lax.rem(c, 8)

    def grads(j):
        remote(srcg.at[j], dstg.at[slot], sendg_sem, recvg_sem, (2 * z + e, j)).start()

    load = pltpu.make_async_copy(rows_hbm, rows_in, rows_sem)
    load.start()
    owng = pltpu.make_async_copy(srcg.at[c], dstg.at[slot], owng_sem)

    @pl.when(mine)
    def _():
        owng.start()

    @pl.when(jnp.logical_not(mine))
    def _():
        grads(c)

    def turn(n, carry):
        grads(lax.rem(c + lax.rem(n * 5, CTX), CTX))
        return carry

    lax.fori_loop(1, CTX, turn, 0)

    load.wait()
    for n in range(CTX):
        slots = row_slots(unp[n : n + 1, :])
        mid[n] = dot(slots, rows_in[n * TOK : (n + 1) * TOK, :], 1, 0).astype(BF16)

    def unsort_senders(grp, carry):
        r0 = pl.multiple_of(grp * 16, 16)
        rows = jnp.concatenate([mid[n, pl.ds(r0, 16), :] for n in range(CTX)], axis=0)
        where = dot(jnp.ones((8 * K, 128), BF16), compact_slot(col, grp), 1, 1)
        t = (where == iota((8 * K, 256), 0).astype(F32)).astype(BF16)
        out = dot(t, rows, 1, 0)
        for n in range(8):
            part = out[n * K : (n + 1) * K]
            src[grp * 8 + n] = part[:, 0:256].astype(BF16)
            keep[grp * 8 + n] = part[:, 256:384].astype(BF16)
            give[grp * 8 + n] = part[:, 384:512].astype(BF16)
        return carry

    lax.fori_loop(0, 16, unsort_senders, 0, unroll=4)

    swap = remote(give, other, sendo_sem, recvo_sem, (2 * z + 1 - core, c))
    swap.start()
    own = pltpu.make_async_copy(src.at[me], dst.at[me], own_sem)
    own.start()
    to_all(src, dst, send_sem, recv_sem)
    swap.wait()
    total[...] = (keep[...].astype(F32) + other[...].astype(F32)).astype(BF16)
    ownk = pltpu.make_async_copy(total.at[me], dstkv.at[me], ownk_sem)
    ownk.start()
    to_all(total, dstkv, sendk_sem, recvk_sem)
    own.wait()
    ownk.wait()

    @pl.when(mine)
    def _():
        owng.wait()
        wait_all(srcg, dstg, sendg_sem, recvg_sem, CTX - 1)

    @pl.when(jnp.logical_not(mine))
    def _():
        wait_all(srcg, dstg, sendg_sem, recvg_sem, CTX)

    wait_all(src, dst, send_sem, recv_sem, DEV - 1)
    wait_all(total, dstkv, sendk_sem, recvk_sem, DEV - 1)


def exchange_out(K, rows, col, unp, srcg):
    anywhere = pl.BlockSpec(memory_space=pl.ANY)
    vmem = pl.BlockSpec(memory_space=pltpu.VMEM)
    wide = pltpu.VMEM((DEV, K, 256), BF16)
    narrow = pltpu.VMEM((DEV, K, 128), BF16)
    return pl.pallas_call(
        functools.partial(exchange_out_kernel, K),
        in_specs=[anywhere, vmem, vmem, anywhere],
        out_specs=[anywhere] * 3,
        out_shape=[
            jax.ShapeDtypeStruct((DEV, K, 256), BF16),
            jax.ShapeDtypeStruct((DEV, K, 128), BF16),
            jax.ShapeDtypeStruct(srcg.shape, BF16),
        ],
        scratch_shapes=[pltpu.VMEM((SEQ, 512), BF16), pltpu.VMEM((CTX, 256, 512), BF16)]
        + [wide, narrow, narrow, narrow, narrow]
        + [pltpu.SemaphoreType.DMA] * 12,
        compiler_params=pltpu.CompilerParams(has_side_effects=True, vmem_limit_bytes=VMEM_LIMIT),
        name="exchange_out",
    )(rows, col, unp, srcg)


def attention_kernel(
    K, recv, other, recvg, att, xo, col, unp, over, x, keyt, valuet, mid, dk, dv, lengths
):
    scale = 1.0 / math.sqrt(DH)
    first_core = lax.rem(lax.axis_index("dp"), 2) == 0
    sizes = recvg[0, TOK:GROWS, 0:TOK].astype(F32)
    sizes = (sizes[8:9] * 8 + sizes[12:13]).astype(jnp.int32)
    for n in range(16):
        lengths[n] = jnp.sum(jnp.where(iota((1, TOK), 1) == n, sizes, 0))

    def slots_of(c):
        return row_slots(recvg[c, TOK : TOK + 8, 0:TOK].astype(F32)[0:1])

    for c in range(CTX):
        unp[c : c + 1, :] = recvg[c, TOK : TOK + 8, 0:TOK].astype(F32)[0:1]

    occ = jnp.zeros((256, 128), F32)
    for c in range(CTX):
        occ = occ + dot(slots_of(c), (iota((TOK, 128), 1) == c).astype(BF16), 1, 0)
    pair = (iota((256, 256), 0) // 2 == iota((256, 256), 1) // 2).astype(BF16)
    count = dot(pair, occ.astype(BF16), 1, 0)
    before = (iota((128, 128), 0) < iota((128, 128), 1)).astype(BF16)
    base = dot(count.astype(BF16), before, 1, 0)
    u = iota((256, 128), 0)
    col[...] = base + (u % 2 + (u // 2) % 8 * K).astype(F32)

    most = jnp.zeros((8 * K, DH), F32)
    for grp in range(16):
        most = jnp.maximum(most, recv[grp, :, 256:384].astype(F32))
    flags = (iota((8 * K, DH), 0) % K == K - 1) & (K < FULL)
    over[0] = jnp.max(jnp.where(flags, most, 0.0))

    def sort_senders(grp, carry):
        r0 = pl.multiple_of(grp * 16, 16)
        slot = dot(compact_slot(col, grp), jnp.ones((128, 8 * K), BF16), 1, 0)
        t = (slot == iota((256, 8 * K), 1).astype(F32)).astype(BF16)
        rows = dot(t, recv[grp], 1, 0).astype(BF16)
        rows2 = dot(t, other[grp], 1, 0).astype(BF16)
        for c in range(CTX):
            mid[c, pl.ds(r0, 16), 0:384] = rows[c * 16 : (c + 1) * 16]
            mid[c, pl.ds(r0, 16), 384:512] = rows2[c * 16 : (c + 1) * 16]
        return carry

    lax.fori_loop(0, 16, sort_senders, 0, unroll=16)

    def sort_rows(c, carry):
        y = dot(slots_of(c), mid[c], 0, 0)
        r = pl.ds(pl.multiple_of(c * TOK, TOK), TOK)
        keys = jnp.where(first_core, y[:, 256:384], y[:, 384:512])
        values = jnp.where(first_core, y[:, 384:512], y[:, 256:384])
        x[r, 0:256] = y[:, 0:256].astype(BF16)
        x[r, 256:384] = keys.astype(BF16)
        x[r, 384:512] = values.astype(BF16)
        keyt[:, r] = keys.T.astype(BF16)
        valuet[:, r] = values.T.astype(BF16)
        return carry

    lax.fori_loop(0, CTX, sort_rows, 0, unroll=16)

    dk[...] = jnp.zeros_like(dk)
    dv[...] = jnp.zeros_like(dv)

    def doc_start(position):
        start, end = jnp.zeros_like(position), jnp.int32(0)
        for n in range(16):
            start = jnp.where(end <= position, end, start)
            end = end + lengths[n]
        return start

    def tile(i, carry):
        q0 = pl.multiple_of(i * BQ, BQ)
        lo = doc_start(q0) // BK
        width = i - lo + 1

        def attend(w):
            k0 = pl.multiple_of(lo * BK, BK)
            span = pl.ds(k0, w * BK)
            here = pl.ds(q0, BQ)
            chunks = [pl.ds(pl.multiple_of(k0 + t * BK, BK), BK) for t in range(w)]
            qpos = q0 + iota((1, BQ), 1)
            qstart = doc_start(qpos)

            def scores(h):
                queries = x[here, h * 128 : (h + 1) * 128]
                out = []
                for t in range(w):
                    kpos = k0 + t * BK + iota((BK, BQ), 0)
                    seen = kpos >= qstart
                    if t == w - 1:
                        seen = seen & (kpos <= qpos)
                    out.append(jnp.where(seen, dot(x[chunks[t], 256:384], queries, 1, 1), -1e30))
                return out

            def grads_of(h):
                return jnp.concatenate(
                    [recvg[2 * i + n, 0:TOK, h * 128 : (h + 1) * 128] for n in range(2)], axis=0
                )

            def probs(s):
                top = functools.reduce(jnp.maximum, [jnp.max(a, axis=0, keepdims=True) for a in s])
                e = [jnp.exp2((a - top) * (scale * math.log2(math.e))) for a in s]
                total = functools.reduce(jnp.add, [jnp.sum(a, axis=0, keepdims=True) for a in e])
                inverse = 1.0 / total
                return [a * inverse for a in e]

            def attend_values(h, p, grads):
                low = jnp.concatenate([a.astype(BF16) for a in p], axis=0)
                outt = dot(valuet[:, span], low, 1, 0).astype(BF16)
                out = outt.astype(F32).T.astype(BF16)
                for n in range(2):
                    att[2 * i + n, :, h * 128 : (h + 1) * 128] = out[n * TOK : (n + 1) * TOK]
                delta = jnp.sum(grads.astype(F32).T * outt.astype(F32), axis=0, keepdims=True)
                return low, delta

            def dprobs(grads):
                return [dot(x[r, 384:512], grads, 1, 1) for r in chunks]

            def dscores(p, dp, delta):
                return jnp.concatenate(
                    [(a * (b - delta) * scale).astype(BF16) for a, b in zip(p, dp)], axis=0
                )

            def query_grads(h, ds):
                xo[here, h * 128 : (h + 1) * 128] = dot(keyt[:, span], ds, 1, 0).T.astype(BF16)

            ga, gb = grads_of(0), grads_of(1)
            sa = scores(0)
            sb = scores(1)
            pa = probs(sa)
            dpa = dprobs(ga)
            pb = probs(sb)
            lowa, deltaa = attend_values(0, pa, ga)
            dpb = dprobs(gb)
            dsa = dscores(pa, dpa, deltaa)
            lowb, deltab = attend_values(1, pb, gb)
            query_grads(0, dsa)
            dsb = dscores(pb, dpb, deltab)
            query_grads(1, dsb)
            dv[span, :] += dot(lowa, ga, 1, 0) + dot(lowb, gb, 1, 0)
            dk[span, :] += dot(dsa, x[here, 0:128], 1, 0) + dot(dsb, x[here, 128:256], 1, 0)

        for w in range(1, WMAX + 1):
            pl.when(width == w)(functools.partial(attend, w))
        return carry

    lax.fori_loop(0, SEQ // BQ, tile, 0)
    xo[:, 256:384] = jnp.where(first_core, dk[...], dv[...]).astype(BF16)
    xo[:, 384:512] = jnp.where(first_core, dv[...], dk[...]).astype(BF16)


def attention(K, recv, other, recvg):
    vmem = pl.BlockSpec(memory_space=pltpu.VMEM)
    return pl.pallas_call(
        functools.partial(attention_kernel, K),
        in_specs=[vmem] * 3,
        out_specs=[vmem] * 4 + [pl.BlockSpec(memory_space=pltpu.SMEM)],
        out_shape=[
            jax.ShapeDtypeStruct((CTX, TOK, 256), BF16),
            jax.ShapeDtypeStruct((SEQ, 512), BF16),
            jax.ShapeDtypeStruct((256, 128), F32),
            jax.ShapeDtypeStruct((CTX, TOK), F32),
            jax.ShapeDtypeStruct((1,), F32),
        ],
        scratch_shapes=[
            pltpu.VMEM((SEQ, 512), BF16),
            pltpu.VMEM((DH, SEQ), BF16),
            pltpu.VMEM((DH, SEQ), BF16),
            pltpu.VMEM((CTX, 256, 512), BF16),
            pltpu.VMEM((SEQ, DH), F32),
            pltpu.VMEM((SEQ, DH), F32),
            pltpu.SMEM((16,), jnp.int32),
        ],
        compiler_params=pltpu.CompilerParams(vmem_limit_bytes=VMEM_LIMIT),
        name="attention",
    )(recv, other, recvg)


STEP = 4


def unpack_kernel(sel, back, backkv, att, attended, gq, gk, gv):
    s = sel[...]
    by_sequence = [(z, e) for z in range(4) for e in range(2)]
    for h in range(STEP):
        for core, out in ((0, gk), (1, gv)):
            cols = slice(h * 512 + core * 256, h * 512 + (core + 1) * 256)
            attended[:, cols] = att[core, h]
            rows = [back[z, core, e, h].astype(F32) for z, e in by_sequence]
            gq[:, cols] = dot(s, jnp.concatenate(rows, axis=0).astype(BF16), 0, 0).astype(BF16)
            rows = [backkv[z, core, e, h].astype(F32) for z, e in by_sequence]
            out[:, h * 128 : (h + 1) * 128] = dot(
                s, jnp.concatenate(rows, axis=0).astype(BF16), 0, 0
            ).astype(BF16)


def unpack_rows(K, sel, back, backkv, att):
    return pl.pallas_call(
        unpack_kernel,
        grid=(KVH // STEP,),
        in_specs=[
            pl.BlockSpec((8 * K, TOK), lambda i: (0, 0)),
            pl.BlockSpec((4, 2, 2, STEP, K, 256), lambda i: (0, 0, 0, i, 0, 0)),
            pl.BlockSpec((4, 2, 2, STEP, K, 128), lambda i: (0, 0, 0, i, 0, 0)),
            pl.BlockSpec((2, STEP, TOK, 256), lambda i: (0, i, 0, 0)),
        ],
        out_specs=[
            pl.BlockSpec((TOK, STEP * 512), lambda i: (0, i)),
            pl.BlockSpec((TOK, STEP * 512), lambda i: (0, i)),
            pl.BlockSpec((TOK, STEP * 128), lambda i: (0, i)),
            pl.BlockSpec((TOK, STEP * 128), lambda i: (0, i)),
        ],
        out_shape=[
            jax.ShapeDtypeStruct((TOK, H * DH), BF16),
            jax.ShapeDtypeStruct((TOK, H * DH), BF16),
            jax.ShapeDtypeStruct((TOK, KVH * DH), BF16),
            jax.ShapeDtypeStruct((TOK, KVH * DH), BF16),
        ],
        compiler_params=pltpu.CompilerParams(vmem_limit_bytes=VMEM_LIMIT),
        name="messages_to_rows",
    )(sel, back, backkv, att)


def middle(K, q_load, k_load, v_load, grad_out, pack_rows, unpack, doc_lengths):
    recv, other, recvg, sel = exchange_in(
        K, pack_rows[0].T, unpack, doc_lengths, q_load, k_load, v_load, grad_out
    )
    recv, other = (a.reshape(16, 8 * K, -1) for a in (recv, other))
    *parts, over = attention(K, recv, other, recvg)
    return over[0] > 0.5, (sel, *parts)


def finish(K, sel, att, rows, col, unp):
    returned, returnedkv, turned = exchange_out(K, rows, col, unp, att)
    returned, returnedkv = (a.reshape(4, 2, 2, KVH, K, -1) for a in (returned, returnedkv))
    return unpack_rows(K, sel, returned, returnedkv, turned.reshape(2, KVH, TOK, 256))


def local(*operands):
    over, parts = middle(SHORT, *operands)
    return lax.cond(
        over,
        lambda: finish(FULL, *middle(FULL, *operands)[1]),
        lambda: finish(SHORT, *parts),
    )


def solution(mesh):
    rows = P(("dp", "ctx"), None)
    return jax.shard_map(
        local,
        mesh=mesh,
        in_specs=(rows, rows, rows, rows, P(("dp", "ctx"), None, None), rows, P("dp", None)),
        out_specs=(rows, rows, rows, rows),
        check_vma=False,
    )
```

```python
import functools
import math

import jax
import jax.numpy as jnp
from jax import lax
from jax.experimental import pallas as pl
from jax.experimental.pallas import tpu as pltpu
from jax.sharding import PartitionSpec as P

H = 32
KVH = 8
DH = 128
TOK = 128
CTX = 16
DP = 8
DEV = 128
SEQ = 2048
MOST = 1024
COLS = 384
FULL = 32
SHORT = 24
GROWS = 144
BQ = 256
BK = 256
WMAX = MOST // BK + 1
VMEM_LIMIT = 56 * 2**20

F32 = jnp.float32
BF16 = jnp.bfloat16
MESH = pl.DeviceIdType.MESH


def dot(a, b, ca, cb):
    return lax.dot_general(a, b, (((ca,), (cb,)), ((), ())), preferred_element_type=F32)


def iota(shape, dim):
    return lax.broadcasted_iota(jnp.int32, shape, dim)


def remote(src, dst, send_sem, recv_sem, target):
    return pltpu.make_async_remote_copy(
        src_ref=src,
        dst_ref=dst,
        send_sem=send_sem,
        recv_sem=recv_sem,
        device_id=target,
        device_id_type=MESH,
    )


def row_slots(row):
    return (iota((256, TOK), 0).astype(F32) == row).astype(BF16)


def compact_slot(col, grp):
    tab = col[pl.ds(pl.multiple_of(grp * 16, 16), 16), :]
    own_c = iota((256, 128), 0) // 16 == iota((256, 128), 1)
    return jnp.where(own_c, jnp.concatenate([tab] * CTX, axis=0), 0.0).astype(BF16)


def place():
    d = lax.axis_index("dp")
    c = lax.axis_index("ctx")
    return d, c, lax.div(d, 2), lax.rem(d, 2)


def partner(n):
    d, c, z, core = place()
    x, y = lax.div(c, 4), lax.rem(c, 4)
    j = lax.rem(n * 5, DEV)
    dy = lax.rem(j, 2) + 2 * lax.rem(lax.div(j, 16), 2)
    dx = lax.rem(lax.div(j, 2), 2) + 2 * lax.rem(lax.div(j, 32), 2)
    dz = lax.rem(lax.div(j, 4), 2) + 2 * lax.div(j, 64)
    dcore = lax.rem(lax.div(j, 8), 2)
    return lax.rem(z + dz, 4) * 2 + lax.rem(core + dcore, 2), lax.rem(x + dx, 4) * 4 + lax.rem(y + dy, 4)


def to_all(src, dst, send_sem, recv_sem):
    d, c, _, _ = place()
    me = d * CTX + c

    def one(n):
        td, tc = partner(n)
        remote(src.at[td * CTX + tc], dst.at[me], send_sem, recv_sem, (td, tc)).start()

    def some(n, carry):
        for i in range(8):
            one(8 * n - 7 + i)
        return carry

    lax.fori_loop(1, CTX, some, 0)
    for n in range(121, DEV):
        one(n)


def greet_all():
    barrier = pltpu.get_barrier_semaphore()

    def greet(n, carry):
        pl.semaphore_signal(barrier, inc=1, device_id=partner(n), device_id_type=MESH)
        return carry

    lax.fori_loop(1, DEV, greet, 0)
    return lambda: pl.semaphore_wait(barrier, DEV - 1)


def wait_all(src, dst, send_sem, recv_sem, count):
    d, c, _, _ = place()
    remote(src.at[pl.ds(0, count)], dst.at[pl.ds(0, count)], send_sem, recv_sem, (d, c)).wait()


def exchange_in_kernel(
    K, slots, unp, lengths, q_in, k_in, v_in, g, dst, other, dstg, sel,
    send, sendg, over_s, q, k, v,
    send_sem, recv_sem, sendg_sem, recvg_sem, sendo_sem, recvo_sem, own_sem, owng_sem,
    q_sem, k_sem, v_sem,
):
    d, c, z, core = place()
    me = d * CTX + c
    mine = core == lax.div(c, 8)
    first = core * 8 + lax.rem(c, 8)
    all_here = greet_all()
    loads = [
        pltpu.make_async_copy(a, b, sem)
        for a, b, sem in ((q_in, q, q_sem), (k_in, k, k_sem), (v_in, v, v_sem))
    ]
    for load in loads:
        load.start()

    r = iota((16, TOK), 0)
    spread = (r == iota((16, TOK), 1)).astype(BF16)
    sizes = jnp.broadcast_to(lengths[...], (16, 16))
    high = dot((sizes // 8).astype(F32).astype(BF16), spread, 1, 0)
    low = dot((sizes % 8).astype(F32).astype(BF16), spread, 1, 0)
    ints = jnp.where(r < 8, unp[...].astype(F32), jnp.where(r < 12, high, low)).astype(BF16)
    for h in range(KVH):
        for p in range(2):
            sendg[p * 8 + h, 0:TOK, :] = g[:, h * 512 + p * 256 : h * 512 + (p + 1) * 256]
            sendg[p * 8 + h, TOK:GROWS, 0:TOK] = ints
            sendg[p * 8 + h, TOK:GROWS, TOK:256] = jnp.zeros((16, 128), BF16)

    all_here()

    def grads(j):
        target = (2 * z + lax.div(j, 8), core * 8 + lax.rem(j, 8))
        remote(sendg.at[j], dstg.at[c], sendg_sem, recvg_sem, target).start()

    owng = pltpu.make_async_copy(sendg.at[first], dstg.at[c], owng_sem)

    @pl.when(mine)
    def _():
        owng.start()

    @pl.when(jnp.logical_not(mine))
    def _():
        grads(first)

    def turn(n, carry):
        grads(lax.rem(first + lax.rem(n * 5, CTX), CTX))
        return carry

    lax.fori_loop(1, CTX, turn, 0)

    occupied = slots[...] >= 0
    count = jnp.where(occupied[0:1], 1.0, 0.0) + jnp.where(occupied[1:2], 1.0, 0.0)
    a, b = iota((DEV, DEV), 0), iota((DEV, DEV), 1)
    earlier = ((a < b) & (a // CTX == b // CTX)).astype(BF16)
    base = dot(jnp.broadcast_to(count, (16, DEV)).astype(BF16), earlier, 1, 0)[0:1].astype(jnp.int32)
    rows_of = jnp.concatenate([slots[...].astype(F32), jnp.zeros((126, DEV), F32)], axis=0).T
    value = jnp.zeros((8 * K, TOK), F32)
    over = jnp.zeros((1, 1), F32)
    for j in range(2):
        rank = base + j
        kept = occupied[j : j + 1]
        if K < FULL:
            lost = jnp.where(kept & (rank >= K - 1), 1.0, 0.0)
            over = jnp.maximum(over, jnp.max(lost, axis=1, keepdims=True))
            kept = kept & (rank < K - 1)
        slot = jnp.where(kept, iota((1, DEV), 1) // CTX * K + rank, -1)
        where = (iota((8 * K, DEV), 0) == slot).astype(BF16)
        holds = (rows_of[:, j : j + 1] == iota((DEV, TOK), 1).astype(F32)).astype(BF16)
        value = value + dot(where, holds, 1, 0)
    s = value.astype(BF16)
    sel[...] = s
    last = (iota((8 * K, TOK), 0) % K == K - 1) & (K < FULL)
    over_s[...] = jnp.where(last, over, 0.0)

    for load in loads:
        load.wait()

    def build(h, carry):
        wide = pl.ds(pl.multiple_of(h * 512, 512), 512)
        narrow = pl.ds(pl.multiple_of(h * 128, 128), 128)
        yq = dot(sel[...], q[:, wide], 1, 0)
        yk = dot(sel[...], k[:, narrow], 1, 0) + over_s[...]
        yv = dot(sel[...], v[:, narrow], 1, 0) + over_s[...]
        for n in range(DP):
            rows = slice(n * K, (n + 1) * K)
            for p, ykv in ((0, yk), (1, yv)):
                t = ((n // 2 * 2 + p) * 2 + n % 2) * 8 + h
                send[t, :, 0:256] = yq[rows, p * 256 : (p + 1) * 256].astype(BF16)
                send[t, :, 256:384] = ykv[rows].astype(BF16)
        return carry

    lax.fori_loop(0, KVH, build, 0)

    own = pltpu.make_async_copy(send.at[me], dst.at[me], own_sem)
    own.start()
    to_all(send, dst, send_sem, recv_sem)
    own.wait()
    wait_all(send, dst, send_sem, recv_sem, DEV - 1)
    swap = remote(dst.at[:, :, pl.ds(256, 128)], other, sendo_sem, recvo_sem, (2 * z + 1 - core, c))
    swap.start()

    @pl.when(mine)
    def _():
        owng.wait()
        wait_all(sendg, dstg, sendg_sem, recvg_sem, CTX - 1)

    @pl.when(jnp.logical_not(mine))
    def _():
        wait_all(sendg, dstg, sendg_sem, recvg_sem, CTX)

    swap.wait()


def exchange_in(K, slots, unp, lengths, q, k, v, g):
    anywhere = pl.BlockSpec(memory_space=pl.ANY)
    vmem = pl.BlockSpec(memory_space=pltpu.VMEM)
    return pl.pallas_call(
        functools.partial(exchange_in_kernel, K),
        in_specs=[vmem] * 3 + [anywhere] * 3 + [vmem],
        out_specs=[anywhere] * 3 + [vmem],
        out_shape=[
            jax.ShapeDtypeStruct((DEV, K, COLS), BF16),
            jax.ShapeDtypeStruct((DEV, K, 128), BF16),
            jax.ShapeDtypeStruct((CTX, GROWS, 256), BF16),
            jax.ShapeDtypeStruct((8 * K, TOK), BF16),
        ],
        scratch_shapes=[
            pltpu.VMEM((DEV, K, COLS), BF16),
            pltpu.VMEM((CTX, GROWS, 256), BF16),
            pltpu.VMEM((8 * K, TOK), F32),
            pltpu.VMEM((TOK, H * DH), BF16),
            pltpu.VMEM((TOK, KVH * DH), BF16),
            pltpu.VMEM((TOK, KVH * DH), BF16),
        ]
        + [pltpu.SemaphoreType.DMA] * 11,
        compiler_params=pltpu.CompilerParams(
            has_side_effects=True, vmem_limit_bytes=VMEM_LIMIT, collective_id=K
        ),
        name="exchange_in",
    )(slots, unp, lengths, q, k, v, g)


def exchange_out_kernel(
    K, rows_hbm, col, unp, srcg, dst, dstkv, dstg,
    rows_in, mid, src, keep, give, other, total,
    send_sem, recv_sem, sendk_sem, recvk_sem, sendg_sem, recvg_sem, sendo_sem, recvo_sem,
    own_sem, ownk_sem, owng_sem, rows_sem,
):
    d, c, z, core = place()
    me = d * CTX + c
    e = lax.div(c, 8)
    mine = core == e
    slot = core * 8 + lax.rem(c, 8)

    def grads(j):
        remote(srcg.at[j], dstg.at[slot], sendg_sem, recvg_sem, (2 * z + e, j)).start()

    load = pltpu.make_async_copy(rows_hbm, rows_in, rows_sem)
    load.start()
    owng = pltpu.make_async_copy(srcg.at[c], dstg.at[slot], owng_sem)

    @pl.when(mine)
    def _():
        owng.start()

    @pl.when(jnp.logical_not(mine))
    def _():
        grads(c)

    def turn(n, carry):
        grads(lax.rem(c + lax.rem(n * 5, CTX), CTX))
        return carry

    lax.fori_loop(1, CTX, turn, 0)

    load.wait()
    for n in range(CTX):
        slots = row_slots(unp[n : n + 1, :])
        mid[n] = dot(slots, rows_in[n * TOK : (n + 1) * TOK, :], 1, 0).astype(BF16)

    def unsort_senders(grp, carry):
        r0 = pl.multiple_of(grp * 16, 16)
        rows = jnp.concatenate([mid[n, pl.ds(r0, 16), :] for n in range(CTX)], axis=0)
        where = dot(jnp.ones((8 * K, 128), BF16), compact_slot(col, grp), 1, 1)
        t = (where == iota((8 * K, 256), 0).astype(F32)).astype(BF16)
        out = dot(t, rows, 1, 0)
        for n in range(8):
            part = out[n * K : (n + 1) * K]
            src[grp * 8 + n] = part[:, 0:256].astype(BF16)
            keep[grp * 8 + n] = part[:, 256:384].astype(BF16)
            give[grp * 8 + n] = part[:, 384:512].astype(BF16)
        return carry

    lax.fori_loop(0, 16, unsort_senders, 0, unroll=4)

    swap = remote(give, other, sendo_sem, recvo_sem, (2 * z + 1 - core, c))
    swap.start()
    own = pltpu.make_async_copy(src.at[me], dst.at[me], own_sem)
    own.start()
    to_all(src, dst, send_sem, recv_sem)
    swap.wait()
    total[...] = (keep[...].astype(F32) + other[...].astype(F32)).astype(BF16)
    ownk = pltpu.make_async_copy(total.at[me], dstkv.at[me], ownk_sem)
    ownk.start()
    to_all(total, dstkv, sendk_sem, recvk_sem)
    own.wait()
    ownk.wait()

    @pl.when(mine)
    def _():
        owng.wait()
        wait_all(srcg, dstg, sendg_sem, recvg_sem, CTX - 1)

    @pl.when(jnp.logical_not(mine))
    def _():
        wait_all(srcg, dstg, sendg_sem, recvg_sem, CTX)

    wait_all(src, dst, send_sem, recv_sem, DEV - 1)
    wait_all(total, dstkv, sendk_sem, recvk_sem, DEV - 1)


def exchange_out(K, rows, col, unp, srcg):
    anywhere = pl.BlockSpec(memory_space=pl.ANY)
    vmem = pl.BlockSpec(memory_space=pltpu.VMEM)
    wide = pltpu.VMEM((DEV, K, 256), BF16)
    narrow = pltpu.VMEM((DEV, K, 128), BF16)
    return pl.pallas_call(
        functools.partial(exchange_out_kernel, K),
        in_specs=[anywhere, vmem, vmem, anywhere],
        out_specs=[anywhere] * 3,
        out_shape=[
            jax.ShapeDtypeStruct((DEV, K, 256), BF16),
            jax.ShapeDtypeStruct((DEV, K, 128), BF16),
            jax.ShapeDtypeStruct(srcg.shape, BF16),
        ],
        scratch_shapes=[pltpu.VMEM((SEQ, 512), BF16), pltpu.VMEM((CTX, 256, 512), BF16)]
        + [wide, narrow, narrow, narrow, narrow]
        + [pltpu.SemaphoreType.DMA] * 12,
        compiler_params=pltpu.CompilerParams(has_side_effects=True, vmem_limit_bytes=VMEM_LIMIT),
        name="exchange_out",
    )(rows, col, unp, srcg)


def attention_kernel(
    K, recv, other, recvg, att, xo, col, unp, over, x, keyt, valuet, mid, dk, dv, lengths
):
    scale = 1.0 / math.sqrt(DH)
    first_core = lax.rem(lax.axis_index("dp"), 2) == 0
    sizes = recvg[0, TOK:GROWS, 0:TOK].astype(F32)
    sizes = (sizes[8:9] * 8 + sizes[12:13]).astype(jnp.int32)
    for n in range(16):
        lengths[n] = jnp.sum(jnp.where(iota((1, TOK), 1) == n, sizes, 0))

    def slots_of(c):
        return row_slots(recvg[c, TOK : TOK + 8, 0:TOK].astype(F32)[0:1])

    for c in range(CTX):
        unp[c : c + 1, :] = recvg[c, TOK : TOK + 8, 0:TOK].astype(F32)[0:1]

    occ = jnp.zeros((256, 128), F32)
    for c in range(CTX):
        occ = occ + dot(slots_of(c), (iota((TOK, 128), 1) == c).astype(BF16), 1, 0)
    pair = (iota((256, 256), 0) // 2 == iota((256, 256), 1) // 2).astype(BF16)
    count = dot(pair, occ.astype(BF16), 1, 0)
    before = (iota((128, 128), 0) < iota((128, 128), 1)).astype(BF16)
    base = dot(count.astype(BF16), before, 1, 0)
    u = iota((256, 128), 0)
    col[...] = base + (u % 2 + (u // 2) % 8 * K).astype(F32)

    most = jnp.zeros((8 * K, DH), F32)
    for grp in range(16):
        most = jnp.maximum(most, recv[grp, :, 256:384].astype(F32))
    flags = (iota((8 * K, DH), 0) % K == K - 1) & (K < FULL)
    over[0] = jnp.max(jnp.where(flags, most, 0.0))

    def sort_senders(grp, carry):
        r0 = pl.multiple_of(grp * 16, 16)
        slot = dot(compact_slot(col, grp), jnp.ones((128, 8 * K), BF16), 1, 0)
        t = (slot == iota((256, 8 * K), 1).astype(F32)).astype(BF16)
        rows = dot(t, recv[grp], 1, 0).astype(BF16)
        rows2 = dot(t, other[grp], 1, 0).astype(BF16)
        for c in range(CTX):
            mid[c, pl.ds(r0, 16), 0:384] = rows[c * 16 : (c + 1) * 16]
            mid[c, pl.ds(r0, 16), 384:512] = rows2[c * 16 : (c + 1) * 16]
        return carry

    lax.fori_loop(0, 16, sort_senders, 0, unroll=16)

    def sort_rows(c, carry):
        y = dot(slots_of(c), mid[c], 0, 0)
        r = pl.ds(pl.multiple_of(c * TOK, TOK), TOK)
        keys = jnp.where(first_core, y[:, 256:384], y[:, 384:512])
        values = jnp.where(first_core, y[:, 384:512], y[:, 256:384])
        x[r, 0:256] = y[:, 0:256].astype(BF16)
        x[r, 256:384] = keys.astype(BF16)
        x[r, 384:512] = values.astype(BF16)
        keyt[:, r] = keys.T.astype(BF16)
        valuet[:, r] = values.T.astype(BF16)
        return carry

    lax.fori_loop(0, CTX, sort_rows, 0, unroll=16)

    dk[...] = jnp.zeros_like(dk)
    dv[...] = jnp.zeros_like(dv)

    def doc_start(position):
        start, end = jnp.zeros_like(position), jnp.int32(0)
        for n in range(16):
            start = jnp.where(end <= position, end, start)
            end = end + lengths[n]
        return start

    def tile(i, carry):
        q0 = pl.multiple_of(i * BQ, BQ)
        lo = doc_start(q0) // BK
        width = i - lo + 1

        def attend(w):
            k0 = pl.multiple_of(lo * BK, BK)
            span = pl.ds(k0, w * BK)
            here = pl.ds(q0, BQ)
            chunks = [pl.ds(pl.multiple_of(k0 + t * BK, BK), BK) for t in range(w)]
            qpos = q0 + iota((1, BQ), 1)
            qstart = doc_start(qpos)

            def scores(h):
                queries = x[here, h * 128 : (h + 1) * 128]
                out = []
                for t in range(w):
                    kpos = k0 + t * BK + iota((BK, BQ), 0)
                    seen = kpos >= qstart
                    if t == w - 1:
                        seen = seen & (kpos <= qpos)
                    out.append(jnp.where(seen, dot(x[chunks[t], 256:384], queries, 1, 1), -1e30))
                return out

            def grads_of(h):
                return jnp.concatenate(
                    [recvg[2 * i + n, 0:TOK, h * 128 : (h + 1) * 128] for n in range(2)], axis=0
                )

            def probs(s):
                top = functools.reduce(jnp.maximum, [jnp.max(a, axis=0, keepdims=True) for a in s])
                e = [jnp.exp2((a - top) * (scale * math.log2(math.e))) for a in s]
                total = functools.reduce(jnp.add, [jnp.sum(a, axis=0, keepdims=True) for a in e])
                inverse = 1.0 / total
                return [a * inverse for a in e]

            def attend_values(h, p, grads):
                low = jnp.concatenate([a.astype(BF16) for a in p], axis=0)
                outt = dot(valuet[:, span], low, 1, 0).astype(BF16)
                out = outt.astype(F32).T.astype(BF16)
                for n in range(2):
                    att[2 * i + n, :, h * 128 : (h + 1) * 128] = out[n * TOK : (n + 1) * TOK]
                delta = jnp.sum(grads.astype(F32).T * outt.astype(F32), axis=0, keepdims=True)
                return low, delta

            def dprobs(grads):
                return [dot(x[r, 384:512], grads, 1, 1) for r in chunks]

            def dscores(p, dp, delta):
                return jnp.concatenate(
                    [(a * (b - delta) * scale).astype(BF16) for a, b in zip(p, dp)], axis=0
                )

            def query_grads(h, ds):
                xo[here, h * 128 : (h + 1) * 128] = dot(keyt[:, span], ds, 1, 0).T.astype(BF16)

            ga, gb = grads_of(0), grads_of(1)
            sa = scores(0)
            sb = scores(1)
            pa = probs(sa)
            dpa = dprobs(ga)
            pb = probs(sb)
            lowa, deltaa = attend_values(0, pa, ga)
            dpb = dprobs(gb)
            dsa = dscores(pa, dpa, deltaa)
            lowb, deltab = attend_values(1, pb, gb)
            query_grads(0, dsa)
            dsb = dscores(pb, dpb, deltab)
            query_grads(1, dsb)
            dv[span, :] += dot(lowa, ga, 1, 0) + dot(lowb, gb, 1, 0)
            dk[span, :] += dot(dsa, x[here, 0:128], 1, 0) + dot(dsb, x[here, 128:256], 1, 0)

        for w in range(1, WMAX + 1):
            pl.when(width == w)(functools.partial(attend, w))
        return carry

    lax.fori_loop(0, SEQ // BQ, tile, 0)
    xo[:, 256:384] = jnp.where(first_core, dk[...], dv[...]).astype(BF16)
    xo[:, 384:512] = jnp.where(first_core, dv[...], dk[...]).astype(BF16)


def attention(K, recv, other, recvg):
    vmem = pl.BlockSpec(memory_space=pltpu.VMEM)
    return pl.pallas_call(
        functools.partial(attention_kernel, K),
        in_specs=[vmem] * 3,
        out_specs=[vmem] * 4 + [pl.BlockSpec(memory_space=pltpu.SMEM)],
        out_shape=[
            jax.ShapeDtypeStruct((CTX, TOK, 256), BF16),
            jax.ShapeDtypeStruct((SEQ, 512), BF16),
            jax.ShapeDtypeStruct((256, 128), F32),
            jax.ShapeDtypeStruct((CTX, TOK), F32),
            jax.ShapeDtypeStruct((1,), F32),
        ],
        scratch_shapes=[
            pltpu.VMEM((SEQ, 512), BF16),
            pltpu.VMEM((DH, SEQ), BF16),
            pltpu.VMEM((DH, SEQ), BF16),
            pltpu.VMEM((CTX, 256, 512), BF16),
            pltpu.VMEM((SEQ, DH), F32),
            pltpu.VMEM((SEQ, DH), F32),
            pltpu.SMEM((16,), jnp.int32),
        ],
        compiler_params=pltpu.CompilerParams(vmem_limit_bytes=VMEM_LIMIT),
        name="attention",
    )(recv, other, recvg)


STEP = 4


def unpack_kernel(sel, back, backkv, att, attended, gq, gk, gv):
    s = sel[...]
    by_sequence = [(z, e) for z in range(4) for e in range(2)]
    for h in range(STEP):
        for core, out in ((0, gk), (1, gv)):
            cols = slice(h * 512 + core * 256, h * 512 + (core + 1) * 256)
            attended[:, cols] = att[core, h]
            rows = [back[z, core, e, h].astype(F32) for z, e in by_sequence]
            gq[:, cols] = dot(s, jnp.concatenate(rows, axis=0).astype(BF16), 0, 0).astype(BF16)
            rows = [backkv[z, core, e, h].astype(F32) for z, e in by_sequence]
            out[:, h * 128 : (h + 1) * 128] = dot(
                s, jnp.concatenate(rows, axis=0).astype(BF16), 0, 0
            ).astype(BF16)


def unpack_rows(K, sel, back, backkv, att):
    return pl.pallas_call(
        unpack_kernel,
        grid=(KVH // STEP,),
        in_specs=[
            pl.BlockSpec((8 * K, TOK), lambda i: (0, 0)),
            pl.BlockSpec((4, 2, 2, STEP, K, 256), lambda i: (0, 0, 0, i, 0, 0)),
            pl.BlockSpec((4, 2, 2, STEP, K, 128), lambda i: (0, 0, 0, i, 0, 0)),
            pl.BlockSpec((2, STEP, TOK, 256), lambda i: (0, i, 0, 0)),
        ],
        out_specs=[
            pl.BlockSpec((TOK, STEP * 512), lambda i: (0, i)),
            pl.BlockSpec((TOK, STEP * 512), lambda i: (0, i)),
            pl.BlockSpec((TOK, STEP * 128), lambda i: (0, i)),
            pl.BlockSpec((TOK, STEP * 128), lambda i: (0, i)),
        ],
        out_shape=[
            jax.ShapeDtypeStruct((TOK, H * DH), BF16),
            jax.ShapeDtypeStruct((TOK, H * DH), BF16),
            jax.ShapeDtypeStruct((TOK, KVH * DH), BF16),
            jax.ShapeDtypeStruct((TOK, KVH * DH), BF16),
        ],
        compiler_params=pltpu.CompilerParams(vmem_limit_bytes=VMEM_LIMIT),
        name="messages_to_rows",
    )(sel, back, backkv, att)


def middle(K, q_load, k_load, v_load, grad_out, pack_rows, unpack, doc_lengths):
    recv, other, recvg, sel = exchange_in(
        K, pack_rows[0].T, unpack, doc_lengths, q_load, k_load, v_load, grad_out
    )
    recv, other = (a.reshape(16, 8 * K, -1) for a in (recv, other))
    *parts, over = attention(K, recv, other, recvg)
    return over[0] > 0.5, (sel, *parts)


def finish(K, sel, att, rows, col, unp):
    returned, returnedkv, turned = exchange_out(K, rows, col, unp, att)
    returned, returnedkv = (a.reshape(4, 2, 2, KVH, K, -1) for a in (returned, returnedkv))
    return unpack_rows(K, sel, returned, returnedkv, turned.reshape(2, KVH, TOK, 256))


def local(*operands):
    over, parts = middle(SHORT, *operands)
    return lax.cond(
        over,
        lambda: finish(FULL, *middle(FULL, *operands)[1]),
        lambda: finish(SHORT, *parts),
    )


def solution(mesh):
    rows = P(("dp", "ctx"), None)
    return jax.shard_map(
        local,
        mesh=mesh,
        in_specs=(rows, rows, rows, rows, P(("dp", "ctx"), None, None), rows, P("dp", None)),
        out_specs=(rows, rows, rows, rows),
        check_vma=False,
    )
```

```python
import functools
import math

import jax
import jax.numpy as jnp
from jax import lax
from jax.experimental import pallas as pl
from jax.experimental.pallas import tpu as pltpu
from jax.sharding import PartitionSpec as P

H = 32
KVH = 8
DH = 128
TOK = 128
CTX = 16
DP = 8
DEV = 128
SEQ = 2048
MOST = 1024
COLS = 384
FULL = 32
SHORT = 24
GROWS = 144
BQ = 256
BK = 256
WMAX = MOST // BK + 1
VMEM_LIMIT = 56 * 2**20

F32 = jnp.float32
BF16 = jnp.bfloat16
MESH = pl.DeviceIdType.MESH


def dot(a, b, ca, cb):
    return lax.dot_general(a, b, (((ca,), (cb,)), ((), ())), preferred_element_type=F32)


def iota(shape, dim):
    return lax.broadcasted_iota(jnp.int32, shape, dim)


def remote(src, dst, send_sem, recv_sem, target):
    return pltpu.make_async_remote_copy(
        src_ref=src,
        dst_ref=dst,
        send_sem=send_sem,
        recv_sem=recv_sem,
        device_id=target,
        device_id_type=MESH,
    )


def row_slots(row):
    return (iota((256, TOK), 0).astype(F32) == row).astype(BF16)


def compact_slot(col, grp):
    tab = col[pl.ds(pl.multiple_of(grp * 16, 16), 16), :]
    own_c = iota((256, 128), 0) // 16 == iota((256, 128), 1)
    return jnp.where(own_c, jnp.concatenate([tab] * CTX, axis=0), 0.0).astype(BF16)


def place():
    d = lax.axis_index("dp")
    c = lax.axis_index("ctx")
    return d, c, lax.div(d, 2), lax.rem(d, 2)


def partner(n):
    d, c, z, core = place()
    x, y = lax.div(c, 4), lax.rem(c, 4)
    j = lax.rem(n * 45, DEV)
    dy = lax.rem(j, 2) + 2 * lax.rem(lax.div(j, 16), 2)
    dx = lax.rem(lax.div(j, 2), 2) + 2 * lax.rem(lax.div(j, 32), 2)
    dz = lax.rem(lax.div(j, 4), 2) + 2 * lax.div(j, 64)
    dcore = lax.rem(lax.div(j, 8), 2)
    return lax.rem(z + dz, 4) * 2 + lax.rem(core + dcore, 2), lax.rem(x + dx, 4) * 4 + lax.rem(y + dy, 4)


def to_all(src, dst, send_sem, recv_sem):
    d, c, _, _ = place()
    me = d * CTX + c

    def one(n):
        td, tc = partner(n)
        remote(src.at[td * CTX + tc], dst.at[me], send_sem, recv_sem, (td, tc)).start()

    def some(n, carry):
        for i in range(8):
            one(8 * n - 7 + i)
        return carry

    lax.fori_loop(1, CTX, some, 0)
    for n in range(121, DEV):
        one(n)


def greet_all():
    barrier = pltpu.get_barrier_semaphore()

    def greet(n, carry):
        pl.semaphore_signal(barrier, inc=1, device_id=partner(n), device_id_type=MESH)
        return carry

    lax.fori_loop(1, DEV, greet, 0)
    return lambda: pl.semaphore_wait(barrier, DEV - 1)


def wait_all(src, dst, send_sem, recv_sem, count):
    d, c, _, _ = place()
    remote(src.at[pl.ds(0, count)], dst.at[pl.ds(0, count)], send_sem, recv_sem, (d, c)).wait()


def exchange_in_kernel(
    K, slots, unp, lengths, q_in, k_in, v_in, g, dst, other, dstg, sel,
    send, sendg, over_s, q, k, v,
    send_sem, recv_sem, sendg_sem, recvg_sem, sendo_sem, recvo_sem, own_sem, owng_sem,
    q_sem, k_sem, v_sem,
):
    d, c, z, core = place()
    me = d * CTX + c
    mine = core == lax.div(c, 8)
    first = core * 8 + lax.rem(c, 8)
    all_here = greet_all()
    loads = [
        pltpu.make_async_copy(a, b, sem)
        for a, b, sem in ((q_in, q, q_sem), (k_in, k, k_sem), (v_in, v, v_sem))
    ]
    for load in loads:
        load.start()

    r = iota((16, TOK), 0)
    spread = (r == iota((16, TOK), 1)).astype(BF16)
    sizes = jnp.broadcast_to(lengths[...], (16, 16))
    high = dot((sizes // 8).astype(F32).astype(BF16), spread, 1, 0)
    low = dot((sizes % 8).astype(F32).astype(BF16), spread, 1, 0)
    ints = jnp.where(r < 8, unp[...].astype(F32), jnp.where(r < 12, high, low)).astype(BF16)
    for h in range(KVH):
        for p in range(2):
            sendg[p * 8 + h, 0:TOK, :] = g[:, h * 512 + p * 256 : h * 512 + (p + 1) * 256]
            sendg[p * 8 + h, TOK:GROWS, 0:TOK] = ints
            sendg[p * 8 + h, TOK:GROWS, TOK:256] = jnp.zeros((16, 128), BF16)

    all_here()

    def grads(j):
        target = (2 * z + lax.div(j, 8), core * 8 + lax.rem(j, 8))
        remote(sendg.at[j], dstg.at[c], sendg_sem, recvg_sem, target).start()

    owng = pltpu.make_async_copy(sendg.at[first], dstg.at[c], owng_sem)

    @pl.when(mine)
    def _():
        owng.start()

    @pl.when(jnp.logical_not(mine))
    def _():
        grads(first)

    def turn(n, carry):
        grads(lax.rem(first + lax.rem(n * 5, CTX), CTX))
        return carry

    lax.fori_loop(1, CTX, turn, 0)

    occupied = slots[...] >= 0
    count = jnp.where(occupied[0:1], 1.0, 0.0) + jnp.where(occupied[1:2], 1.0, 0.0)
    a, b = iota((DEV, DEV), 0), iota((DEV, DEV), 1)
    earlier = ((a < b) & (a // CTX == b // CTX)).astype(BF16)
    base = dot(jnp.broadcast_to(count, (16, DEV)).astype(BF16), earlier, 1, 0)[0:1].astype(jnp.int32)
    rows_of = jnp.concatenate([slots[...].astype(F32), jnp.zeros((126, DEV), F32)], axis=0).T
    value = jnp.zeros((8 * K, TOK), F32)
    over = jnp.zeros((1, 1), F32)
    for j in range(2):
        rank = base + j
        kept = occupied[j : j + 1]
        if K < FULL:
            lost = jnp.where(kept & (rank >= K - 1), 1.0, 0.0)
            over = jnp.maximum(over, jnp.max(lost, axis=1, keepdims=True))
            kept = kept & (rank < K - 1)
        slot = jnp.where(kept, iota((1, DEV), 1) // CTX * K + rank, -1)
        where = (iota((8 * K, DEV), 0) == slot).astype(BF16)
        holds = (rows_of[:, j : j + 1] == iota((DEV, TOK), 1).astype(F32)).astype(BF16)
        value = value + dot(where, holds, 1, 0)
    s = value.astype(BF16)
    sel[...] = s
    last = (iota((8 * K, TOK), 0) % K == K - 1) & (K < FULL)
    over_s[...] = jnp.where(last, over, 0.0)

    for load in loads:
        load.wait()

    def build(h, carry):
        wide = pl.ds(pl.multiple_of(h * 512, 512), 512)
        narrow = pl.ds(pl.multiple_of(h * 128, 128), 128)
        yq = dot(sel[...], q[:, wide], 1, 0)
        yk = dot(sel[...], k[:, narrow], 1, 0) + over_s[...]
        yv = dot(sel[...], v[:, narrow], 1, 0) + over_s[...]
        for n in range(DP):
            rows = slice(n * K, (n + 1) * K)
            for p, ykv in ((0, yk), (1, yv)):
                t = ((n // 2 * 2 + p) * 2 + n % 2) * 8 + h
                send[t, :, 0:256] = yq[rows, p * 256 : (p + 1) * 256].astype(BF16)
                send[t, :, 256:384] = ykv[rows].astype(BF16)
        return carry

    lax.fori_loop(0, KVH, build, 0)

    own = pltpu.make_async_copy(send.at[me], dst.at[me], own_sem)
    own.start()
    to_all(send, dst, send_sem, recv_sem)
    own.wait()
    wait_all(send, dst, send_sem, recv_sem, DEV - 1)
    swap = remote(dst.at[:, :, pl.ds(256, 128)], other, sendo_sem, recvo_sem, (2 * z + 1 - core, c))
    swap.start()

    @pl.when(mine)
    def _():
        owng.wait()
        wait_all(sendg, dstg, sendg_sem, recvg_sem, CTX - 1)

    @pl.when(jnp.logical_not(mine))
    def _():
        wait_all(sendg, dstg, sendg_sem, recvg_sem, CTX)

    swap.wait()


def exchange_in(K, slots, unp, lengths, q, k, v, g):
    anywhere = pl.BlockSpec(memory_space=pl.ANY)
    vmem = pl.BlockSpec(memory_space=pltpu.VMEM)
    return pl.pallas_call(
        functools.partial(exchange_in_kernel, K),
        in_specs=[vmem] * 3 + [anywhere] * 3 + [vmem],
        out_specs=[anywhere] * 3 + [vmem],
        out_shape=[
            jax.ShapeDtypeStruct((DEV, K, COLS), BF16),
            jax.ShapeDtypeStruct((DEV, K, 128), BF16),
            jax.ShapeDtypeStruct((CTX, GROWS, 256), BF16),
            jax.ShapeDtypeStruct((8 * K, TOK), BF16),
        ],
        scratch_shapes=[
            pltpu.VMEM((DEV, K, COLS), BF16),
            pltpu.VMEM((CTX, GROWS, 256), BF16),
            pltpu.VMEM((8 * K, TOK), F32),
            pltpu.VMEM((TOK, H * DH), BF16),
            pltpu.VMEM((TOK, KVH * DH), BF16),
            pltpu.VMEM((TOK, KVH * DH), BF16),
        ]
        + [pltpu.SemaphoreType.DMA] * 11,
        compiler_params=pltpu.CompilerParams(
            has_side_effects=True, vmem_limit_bytes=VMEM_LIMIT, collective_id=K
        ),
        name="exchange_in",
    )(slots, unp, lengths, q, k, v, g)


def exchange_out_kernel(
    K, rows_hbm, col, unp, srcg, dst, dstkv, dstg,
    rows_in, mid, src, keep, give, other, total,
    send_sem, recv_sem, sendk_sem, recvk_sem, sendg_sem, recvg_sem, sendo_sem, recvo_sem,
    own_sem, ownk_sem, owng_sem, rows_sem,
):
    d, c, z, core = place()
    me = d * CTX + c
    e = lax.div(c, 8)
    mine = core == e
    slot = core * 8 + lax.rem(c, 8)

    def grads(j):
        remote(srcg.at[j], dstg.at[slot], sendg_sem, recvg_sem, (2 * z + e, j)).start()

    load = pltpu.make_async_copy(rows_hbm, rows_in, rows_sem)
    load.start()
    owng = pltpu.make_async_copy(srcg.at[c], dstg.at[slot], owng_sem)

    @pl.when(mine)
    def _():
        owng.start()

    @pl.when(jnp.logical_not(mine))
    def _():
        grads(c)

    def turn(n, carry):
        grads(lax.rem(c + lax.rem(n * 5, CTX), CTX))
        return carry

    lax.fori_loop(1, CTX, turn, 0)

    load.wait()
    for n in range(CTX):
        slots = row_slots(unp[n : n + 1, :])
        mid[n] = dot(slots, rows_in[n * TOK : (n + 1) * TOK, :], 1, 0).astype(BF16)

    def unsort_senders(grp, carry):
        r0 = pl.multiple_of(grp * 16, 16)
        rows = jnp.concatenate([mid[n, pl.ds(r0, 16), :] for n in range(CTX)], axis=0)
        where = dot(jnp.ones((8 * K, 128), BF16), compact_slot(col, grp), 1, 1)
        t = (where == iota((8 * K, 256), 0).astype(F32)).astype(BF16)
        out = dot(t, rows, 1, 0)
        for n in range(8):
            part = out[n * K : (n + 1) * K]
            src[grp * 8 + n] = part[:, 0:256].astype(BF16)
            keep[grp * 8 + n] = part[:, 256:384].astype(BF16)
            give[grp * 8 + n] = part[:, 384:512].astype(BF16)
        return carry

    lax.fori_loop(0, 16, unsort_senders, 0, unroll=4)

    swap = remote(give, other, sendo_sem, recvo_sem, (2 * z + 1 - core, c))
    swap.start()
    own = pltpu.make_async_copy(src.at[me], dst.at[me], own_sem)
    own.start()
    to_all(src, dst, send_sem, recv_sem)
    swap.wait()
    total[...] = (keep[...].astype(F32) + other[...].astype(F32)).astype(BF16)
    ownk = pltpu.make_async_copy(total.at[me], dstkv.at[me], ownk_sem)
    ownk.start()
    to_all(total, dstkv, sendk_sem, recvk_sem)
    own.wait()
    ownk.wait()

    @pl.when(mine)
    def _():
        owng.wait()
        wait_all(srcg, dstg, sendg_sem, recvg_sem, CTX - 1)

    @pl.when(jnp.logical_not(mine))
    def _():
        wait_all(srcg, dstg, sendg_sem, recvg_sem, CTX)

    wait_all(src, dst, send_sem, recv_sem, DEV - 1)
    wait_all(total, dstkv, sendk_sem, recvk_sem, DEV - 1)


def exchange_out(K, rows, col, unp, srcg):
    anywhere = pl.BlockSpec(memory_space=pl.ANY)
    vmem = pl.BlockSpec(memory_space=pltpu.VMEM)
    wide = pltpu.VMEM((DEV, K, 256), BF16)
    narrow = pltpu.VMEM((DEV, K, 128), BF16)
    return pl.pallas_call(
        functools.partial(exchange_out_kernel, K),
        in_specs=[anywhere, vmem, vmem, anywhere],
        out_specs=[anywhere] * 3,
        out_shape=[
            jax.ShapeDtypeStruct((DEV, K, 256), BF16),
            jax.ShapeDtypeStruct((DEV, K, 128), BF16),
            jax.ShapeDtypeStruct(srcg.shape, BF16),
        ],
        scratch_shapes=[pltpu.VMEM((SEQ, 512), BF16), pltpu.VMEM((CTX, 256, 512), BF16)]
        + [wide, narrow, narrow, narrow, narrow]
        + [pltpu.SemaphoreType.DMA] * 12,
        compiler_params=pltpu.CompilerParams(has_side_effects=True, vmem_limit_bytes=VMEM_LIMIT),
        name="exchange_out",
    )(rows, col, unp, srcg)


def attention_kernel(
    K, recv, other, recvg, att, xo, col, unp, over, x, keyt, valuet, mid, dk, dv, lengths
):
    scale = 1.0 / math.sqrt(DH)
    first_core = lax.rem(lax.axis_index("dp"), 2) == 0
    sizes = recvg[0, TOK:GROWS, 0:TOK].astype(F32)
    sizes = (sizes[8:9] * 8 + sizes[12:13]).astype(jnp.int32)
    for n in range(16):
        lengths[n] = jnp.sum(jnp.where(iota((1, TOK), 1) == n, sizes, 0))

    def slots_of(c):
        return row_slots(recvg[c, TOK : TOK + 8, 0:TOK].astype(F32)[0:1])

    for c in range(CTX):
        unp[c : c + 1, :] = recvg[c, TOK : TOK + 8, 0:TOK].astype(F32)[0:1]

    occ = jnp.zeros((256, 128), F32)
    for c in range(CTX):
        occ = occ + dot(slots_of(c), (iota((TOK, 128), 1) == c).astype(BF16), 1, 0)
    pair = (iota((256, 256), 0) // 2 == iota((256, 256), 1) // 2).astype(BF16)
    count = dot(pair, occ.astype(BF16), 1, 0)
    before = (iota((128, 128), 0) < iota((128, 128), 1)).astype(BF16)
    base = dot(count.astype(BF16), before, 1, 0)
    u = iota((256, 128), 0)
    col[...] = base + (u % 2 + (u // 2) % 8 * K).astype(F32)

    most = jnp.zeros((8 * K, DH), F32)
    for grp in range(16):
        most = jnp.maximum(most, recv[grp, :, 256:384].astype(F32))
    flags = (iota((8 * K, DH), 0) % K == K - 1) & (K < FULL)
    over[0] = jnp.max(jnp.where(flags, most, 0.0))

    def sort_senders(grp, carry):
        r0 = pl.multiple_of(grp * 16, 16)
        slot = dot(compact_slot(col, grp), jnp.ones((128, 8 * K), BF16), 1, 0)
        t = (slot == iota((256, 8 * K), 1).astype(F32)).astype(BF16)
        rows = dot(t, recv[grp], 1, 0).astype(BF16)
        rows2 = dot(t, other[grp], 1, 0).astype(BF16)
        for c in range(CTX):
            mid[c, pl.ds(r0, 16), 0:384] = rows[c * 16 : (c + 1) * 16]
            mid[c, pl.ds(r0, 16), 384:512] = rows2[c * 16 : (c + 1) * 16]
        return carry

    lax.fori_loop(0, 16, sort_senders, 0, unroll=16)

    def sort_rows(c, carry):
        y = dot(slots_of(c), mid[c], 0, 0)
        r = pl.ds(pl.multiple_of(c * TOK, TOK), TOK)
        keys = jnp.where(first_core, y[:, 256:384], y[:, 384:512])
        values = jnp.where(first_core, y[:, 384:512], y[:, 256:384])
        x[r, 0:256] = y[:, 0:256].astype(BF16)
        x[r, 256:384] = keys.astype(BF16)
        x[r, 384:512] = values.astype(BF16)
        keyt[:, r] = keys.T.astype(BF16)
        valuet[:, r] = values.T.astype(BF16)
        return carry

    lax.fori_loop(0, CTX, sort_rows, 0, unroll=16)

    dk[...] = jnp.zeros_like(dk)
    dv[...] = jnp.zeros_like(dv)

    def doc_start(position):
        start, end = jnp.zeros_like(position), jnp.int32(0)
        for n in range(16):
            start = jnp.where(end <= position, end, start)
            end = end + lengths[n]
        return start

    def tile(i, carry):
        q0 = pl.multiple_of(i * BQ, BQ)
        lo = doc_start(q0) // BK
        width = i - lo + 1

        def attend(w):
            k0 = pl.multiple_of(lo * BK, BK)
            span = pl.ds(k0, w * BK)
            here = pl.ds(q0, BQ)
            chunks = [pl.ds(pl.multiple_of(k0 + t * BK, BK), BK) for t in range(w)]
            qpos = q0 + iota((1, BQ), 1)
            qstart = doc_start(qpos)

            def scores(h):
                queries = x[here, h * 128 : (h + 1) * 128]
                out = []
                for t in range(w):
                    kpos = k0 + t * BK + iota((BK, BQ), 0)
                    seen = kpos >= qstart
                    if t == w - 1:
                        seen = seen & (kpos <= qpos)
                    out.append(jnp.where(seen, dot(x[chunks[t], 256:384], queries, 1, 1), -1e30))
                return out

            def grads_of(h):
                return jnp.concatenate(
                    [recvg[2 * i + n, 0:TOK, h * 128 : (h + 1) * 128] for n in range(2)], axis=0
                )

            def probs(s):
                top = functools.reduce(jnp.maximum, [jnp.max(a, axis=0, keepdims=True) for a in s])
                e = [jnp.exp2((a - top) * (scale * math.log2(math.e))) for a in s]
                total = functools.reduce(jnp.add, [jnp.sum(a, axis=0, keepdims=True) for a in e])
                inverse = 1.0 / total
                return [a * inverse for a in e]

            def attend_values(h, p, grads):
                low = jnp.concatenate([a.astype(BF16) for a in p], axis=0)
                outt = dot(valuet[:, span], low, 1, 0).astype(BF16)
                out = outt.astype(F32).T.astype(BF16)
                for n in range(2):
                    att[2 * i + n, :, h * 128 : (h + 1) * 128] = out[n * TOK : (n + 1) * TOK]
                delta = jnp.sum(grads.astype(F32).T * outt.astype(F32), axis=0, keepdims=True)
                return low, delta

            def dprobs(grads):
                return [dot(x[r, 384:512], grads, 1, 1) for r in chunks]

            def dscores(p, dp, delta):
                return jnp.concatenate(
                    [(a * (b - delta) * scale).astype(BF16) for a, b in zip(p, dp)], axis=0
                )

            def query_grads(h, ds):
                xo[here, h * 128 : (h + 1) * 128] = dot(keyt[:, span], ds, 1, 0).T.astype(BF16)

            ga, gb = grads_of(0), grads_of(1)
            sa = scores(0)
            sb = scores(1)
            pa = probs(sa)
            dpa = dprobs(ga)
            pb = probs(sb)
            lowa, deltaa = attend_values(0, pa, ga)
            dpb = dprobs(gb)
            dsa = dscores(pa, dpa, deltaa)
            lowb, deltab = attend_values(1, pb, gb)
            query_grads(0, dsa)
            dsb = dscores(pb, dpb, deltab)
            query_grads(1, dsb)
            dv[span, :] += dot(lowa, ga, 1, 0) + dot(lowb, gb, 1, 0)
            dk[span, :] += dot(dsa, x[here, 0:128], 1, 0) + dot(dsb, x[here, 128:256], 1, 0)

        for w in range(1, WMAX + 1):
            pl.when(width == w)(functools.partial(attend, w))
        return carry

    lax.fori_loop(0, SEQ // BQ, tile, 0)
    xo[:, 256:384] = jnp.where(first_core, dk[...], dv[...]).astype(BF16)
    xo[:, 384:512] = jnp.where(first_core, dv[...], dk[...]).astype(BF16)


def attention(K, recv, other, recvg):
    vmem = pl.BlockSpec(memory_space=pltpu.VMEM)
    return pl.pallas_call(
        functools.partial(attention_kernel, K),
        in_specs=[vmem] * 3,
        out_specs=[vmem] * 4 + [pl.BlockSpec(memory_space=pltpu.SMEM)],
        out_shape=[
            jax.ShapeDtypeStruct((CTX, TOK, 256), BF16),
            jax.ShapeDtypeStruct((SEQ, 512), BF16),
            jax.ShapeDtypeStruct((256, 128), F32),
            jax.ShapeDtypeStruct((CTX, TOK), F32),
            jax.ShapeDtypeStruct((1,), F32),
        ],
        scratch_shapes=[
            pltpu.VMEM((SEQ, 512), BF16),
            pltpu.VMEM((DH, SEQ), BF16),
            pltpu.VMEM((DH, SEQ), BF16),
            pltpu.VMEM((CTX, 256, 512), BF16),
            pltpu.VMEM((SEQ, DH), F32),
            pltpu.VMEM((SEQ, DH), F32),
            pltpu.SMEM((16,), jnp.int32),
        ],
        compiler_params=pltpu.CompilerParams(vmem_limit_bytes=VMEM_LIMIT),
        name="attention",
    )(recv, other, recvg)


STEP = 4


def unpack_kernel(sel, back, backkv, att, attended, gq, gk, gv):
    s = sel[...]
    by_sequence = [(z, e) for z in range(4) for e in range(2)]
    for h in range(STEP):
        for core, out in ((0, gk), (1, gv)):
            cols = slice(h * 512 + core * 256, h * 512 + (core + 1) * 256)
            attended[:, cols] = att[core, h]
            rows = [back[z, core, e, h].astype(F32) for z, e in by_sequence]
            gq[:, cols] = dot(s, jnp.concatenate(rows, axis=0).astype(BF16), 0, 0).astype(BF16)
            rows = [backkv[z, core, e, h].astype(F32) for z, e in by_sequence]
            out[:, h * 128 : (h + 1) * 128] = dot(
                s, jnp.concatenate(rows, axis=0).astype(BF16), 0, 0
            ).astype(BF16)


def unpack_rows(K, sel, back, backkv, att):
    return pl.pallas_call(
        unpack_kernel,
        grid=(KVH // STEP,),
        in_specs=[
            pl.BlockSpec((8 * K, TOK), lambda i: (0, 0)),
            pl.BlockSpec((4, 2, 2, STEP, K, 256), lambda i: (0, 0, 0, i, 0, 0)),
            pl.BlockSpec((4, 2, 2, STEP, K, 128), lambda i: (0, 0, 0, i, 0, 0)),
            pl.BlockSpec((2, STEP, TOK, 256), lambda i: (0, i, 0, 0)),
        ],
        out_specs=[
            pl.BlockSpec((TOK, STEP * 512), lambda i: (0, i)),
            pl.BlockSpec((TOK, STEP * 512), lambda i: (0, i)),
            pl.BlockSpec((TOK, STEP * 128), lambda i: (0, i)),
            pl.BlockSpec((TOK, STEP * 128), lambda i: (0, i)),
        ],
        out_shape=[
            jax.ShapeDtypeStruct((TOK, H * DH), BF16),
            jax.ShapeDtypeStruct((TOK, H * DH), BF16),
            jax.ShapeDtypeStruct((TOK, KVH * DH), BF16),
            jax.ShapeDtypeStruct((TOK, KVH * DH), BF16),
        ],
        compiler_params=pltpu.CompilerParams(vmem_limit_bytes=VMEM_LIMIT),
        name="messages_to_rows",
    )(sel, back, backkv, att)


def middle(K, q_load, k_load, v_load, grad_out, pack_rows, unpack, doc_lengths):
    recv, other, recvg, sel = exchange_in(
        K, pack_rows[0].T, unpack, doc_lengths, q_load, k_load, v_load, grad_out
    )
    recv, other = (a.reshape(16, 8 * K, -1) for a in (recv, other))
    *parts, over = attention(K, recv, other, recvg)
    return over[0] > 0.5, (sel, *parts)


def finish(K, sel, att, rows, col, unp):
    returned, returnedkv, turned = exchange_out(K, rows, col, unp, att)
    returned, returnedkv = (a.reshape(4, 2, 2, KVH, K, -1) for a in (returned, returnedkv))
    return unpack_rows(K, sel, returned, returnedkv, turned.reshape(2, KVH, TOK, 256))


def local(*operands):
    over, parts = middle(SHORT, *operands)
    return lax.cond(
        over,
        lambda: finish(FULL, *middle(FULL, *operands)[1]),
        lambda: finish(SHORT, *parts),
    )


def solution(mesh):
    rows = P(("dp", "ctx"), None)
    return jax.shard_map(
        local,
        mesh=mesh,
        in_specs=(rows, rows, rows, rows, P(("dp", "ctx"), None, None), rows, P("dp", None)),
        out_specs=(rows, rows, rows, rows),
        check_vma=False,
    )
```
